32 devices in a mesh: groups: 2 (over y), phi: 4 (over z), gz: 2 (over x), row: 2 (over core).
Axes of the slice: x: 2, y: 2, z: 4, core: 2. Of those that a mesh axis runs over, the one named last changes fastest.
Arguments:
- field: float32 [6, 16, 32, 256], P('groups', 'row', 'phi', 'gz'), parts along dimension 0, may hold values from -900 to 900
- velocity: float32 [6, 16, 32, 256], P('groups', 'row', 'phi', 'gz'), parts along dimension 0, may hold values from -4 to 4
- basis: float32 [16, 3, 16, 32, 256], P('groups', None, 'row', 'phi', 'gz'), parts along dimension 0, may hold values from -200 to 200
- wall_region: int32 [64, 256], P(('groups', 'phi'), 'gz'), parts along dimension 0, may hold values from 0 to 7
- wall_conductance: float32 [16], P('groups'), parts along dimension 0, may hold values from 0.1 to 10
Outputs:
- next_vector: float32 [6, 16, 32, 256], P('groups', 'row', 'phi', 'gz'), parts along dimension 0
- hessenberg: float32 [18], P('groups'), parts along dimension 0
The draws below stay inside these ranges and needn't reach their ends.
There are 2 independent parts, one for each index of `groups`. The reference program is written for one: setup_inputs(seed, part) draws one part's arguments, and reference() takes and returns one part's arrays. A program takes and returns all parts, laid end to end along the dimension named above; each array names one. Nothing has to cross between parts.
All inputs are finite; a program needn't handle non-finite values.
Results may differ from the reference program's by a relative error of at most 0.00015.
Values sent between devices are 32-bit elements; how exact they have to be, the bound alone decides.
No kernel may reach another device: no remote copies, remote signals or barrier semaphores. Data moves between devices by JAX's collectives and lax.ppermute only.
A program may use at most 64 MiB of HBM per device.

```python
import math
import jax
import jax.numpy as jnp

KRYLOV = 8
NREG = 8
NR = 16
NP = 32
NZ = 256


def common_noise(key):
    folded = jax.random.fold_in(key, 7)
    key_base, key_rough, key_weights = jax.random.split(folded, 3)
    shape = (KRYLOV + 1, 3, NR, NP, NZ)
    base = jax.random.truncated_normal(key_base, -4.0, 4.0, shape, jnp.float32)
    mixing = 0.3
    rough = jnp.exp(jax.random.uniform(key_rough, (1, 1, NR, NP, NZ), jnp.float32, 0.0, math.log(10.0)))
    ramp = 1.0 + 2.0 * jnp.arange(NZ, dtype=jnp.float32) / NZ
    weights = jax.random.uniform(key_weights, (KRYLOV,), jnp.float32, 0.3, 0.8)
    return (base * rough * ramp, weights, mixing)


def draw_field(key, part):
    noise, weights, mixing = common_noise(key)
    total = noise[KRYLOV]
    for position in range(KRYLOV):
        total = total + weights[position] * noise[position]
    return total


def draw_basis(key, part):
    noise, weights, mixing = common_noise(key)
    return noise[:KRYLOV] + mixing * noise[KRYLOV][None]


def plant(result, rng, smallest, high):
    longest = result.shape.index(max(result.shape))
    spots = []
    for shift in (0, 1):
        where = [jax.random.randint(jax.random.fold_in(rng, axis), (), 0, length) for axis, length in enumerate(result.shape)]
        where[longest] = (where[longest] + shift) % result.shape[longest]
        spots.append(tuple(where))
    return result.at[spots[0]].set(smallest).at[spots[1]].set(high)


def level_of(stream_key, extent, shards, smallest, high):
    loudness = 1.0
    for dim, shards_of in shards:
        steps = jax.random.uniform(jax.random.fold_in(jax.random.fold_in(stream_key, 6), dim), (shards_of,), jnp.float32, smallest / len(shards), high / len(shards))
        loudness = loudness * jnp.repeat(jnp.exp(steps), extent[dim] // shards_of).reshape((-1,) + (1,) * (len(extent) - 1 - dim))
    return loudness


def scatter_about(rng, extent, scale, bound, pieces=(), kind=jnp.bfloat16):
    drawn = jax.random.normal(rng, extent, jnp.float32) * scale
    if len(pieces) > 0:
        drawn = level_of(rng, extent, pieces, -0.22, 0.18) * drawn
    return jnp.clip(drawn, min=-bound, max=bound).astype(kind)


def setup_inputs(seed: int = 0, part: int = 0) -> dict:
    key_list = jax.random.split(jax.random.key(seed), 6)
    part_splits = jax.random.split(jax.random.fold_in(key_list[5], part), 6)
    return {
        "field": draw_field(jax.random.fold_in(jax.random.fold_in(key_list[5], part), 71), part),
        "velocity": scatter_about(part_splits[1], (3, NR, NP, NZ), 0.7, 4.0, ((1, 2), (2, 4), (3, 2)), jnp.float32),
        "basis": draw_basis(jax.random.fold_in(jax.random.fold_in(key_list[5], part), 71), part),
        "wall_region": plant(jax.random.randint(part_splits[3], (NP, NZ), 0, NREG), jax.random.fold_in(part_splits[3], 1), 0, NREG - 1).astype(jnp.int32),
        "wall_conductance": jnp.clip(jnp.exp(jax.random.uniform(part_splits[4], (NREG,), jnp.float32, math.log(0.1), math.log(10.0))), 0.1, 10.0),
    }


advect_step = 0.2
diffuse_step = 0.1
epsilon = 1e-06

def cell_part(padded, radial_step, azimuth_step, axial_step):
    radial_count = padded.shape[1] - 2
    azimuth_count = padded.shape[2] - 2
    axial_count = padded.shape[3] - 2
    return padded[:, 1 + radial_step:1 + radial_step + radial_count, 1 + azimuth_step:1 + azimuth_step + azimuth_count, 1 + axial_step:1 + axial_step + axial_count]

def velocity_terms(padded_velocity):
    center = cell_part(padded_velocity, 0, 0, 0)
    radial_grad = 0.5 * (cell_part(padded_velocity, 1, 0, 0) - cell_part(padded_velocity, -1, 0, 0))
    azimuth_grad = 0.5 * (cell_part(padded_velocity, 0, 1, 0) - cell_part(padded_velocity, 0, -1, 0))
    axial_grad = 0.5 * (cell_part(padded_velocity, 0, 0, 1) - cell_part(padded_velocity, 0, 0, -1))
    return (center, radial_grad, azimuth_grad, axial_grad)

def tendency(padded, motion, radius):
    center_speed, radial_grad, azimuth_grad, axial_grad = motion
    center = cell_part(padded, 0, 0, 0)
    outward = cell_part(padded, 1, 0, 0)
    inward = cell_part(padded, -1, 0, 0)
    forward = cell_part(padded, 0, 1, 0)
    behind = cell_part(padded, 0, -1, 0)
    above_cell = cell_part(padded, 0, 0, 1)
    below_cell = cell_part(padded, 0, 0, -1)
    radial_speed = center_speed[0]
    azimuth_speed = center_speed[1]
    axial_speed = center_speed[2]
    upwind = jnp.maximum(radial_speed, 0.0) * (center - inward) + jnp.minimum(radial_speed, 0.0) * (outward - center) + jnp.maximum(azimuth_speed, 0.0) * (center - behind) + jnp.minimum(azimuth_speed, 0.0) * (forward - center) + jnp.maximum(axial_speed, 0.0) * (center - below_cell) + jnp.minimum(axial_speed, 0.0) * (above_cell - center)
    stretch = center[0] * radial_grad + center[1] * azimuth_grad + center[2] * axial_grad
    induction = stretch - upwind
    bending = (center[1] * radial_speed - azimuth_speed * center[0]) / radius
    laplace = ((radius + 0.5) * (outward - center) - (radius - 0.5) * (center - inward)) / radius + (forward + behind - 2.0 * center) + (above_cell + below_cell - 2.0 * center)
    turning = 0.5 * (forward - behind)
    inverse_square = 1.0 / (radius * radius)
    diffuse_radial = laplace[0] - center[0] * inverse_square - 2.0 * turning[1] / radius
    diffuse_azimuth = laplace[1] - center[1] * inverse_square + 2.0 * turning[0] / radius
    diffuse_axial = laplace[2]
    radial_rate = advect_step * induction[0] + diffuse_step * diffuse_radial
    azimuth_rate = advect_step * (induction[1] + bending) + diffuse_step * diffuse_azimuth
    axial_rate = advect_step * induction[2] + diffuse_step * diffuse_axial
    return jnp.stack([radial_rate, azimuth_rate, axial_rate])

def extend_global(fields, flip_signs, wall_factors):
    half_turn = NP // 2
    axis_layer = jnp.roll(fields[:, 0], -half_turn, axis=1) * flip_signs[:, None, None]
    wall_layer = fields[:, -1] * wall_factors
    radial = jnp.concatenate([axis_layer[:, None], fields, wall_layer[:, None]], axis=1)
    looped = jnp.concatenate([radial[:, :, -1:], radial, radial[:, :, :1]], axis=2)
    return jnp.pad(looped, ((0, 0), (0, 0), (0, 0), (1, 1)))

def reference(field, velocity, basis, wall_region, wall_conductance):
    conductance = wall_conductance[wall_region]
    reflect = 1.0 - 2.0 * conductance / (1.0 + conductance)
    field_wall = jnp.broadcast_to(reflect[None], (3,) + reflect.shape)
    unity = jnp.ones_like(reflect)
    velocity_wall = jnp.stack([-unity, unity, unity])
    flip_signs = jnp.array([-1.0, -1.0, 1.0], dtype=jnp.float32)
    radius = (jnp.arange(NR, dtype=jnp.float32) + 0.5)[:, None, None]
    motion = velocity_terms(extend_global(velocity, flip_signs, velocity_wall))
    section_one = field + tendency(extend_global(field, flip_signs, field_wall), motion, radius)
    second = 0.75 * field + 0.25 * (section_one + tendency(extend_global(section_one, flip_signs, field_wall), motion, radius))
    advanced = field / 3.0 + 2.0 / 3.0 * (second + tendency(extend_global(second, flip_signs, field_wall), motion, radius))
    remaining = advanced
    weights = []
    for position in range(KRYLOV):
        vector = basis[position]
        weight = jnp.sum(vector * remaining) / jnp.sum(vector * vector)
        weights.append(weight)
        remaining = remaining - weight * vector
    spread = jnp.sqrt(jnp.mean(remaining * remaining) + epsilon)
    return (remaining / spread, jnp.concatenate([jnp.stack(weights), spread[None]]))
```

```python
import jax
import jax.numpy as jnp
from jax import lax
from jax.sharding import PartitionSpec as P

advect_step = 0.2
diffuse_step = 0.1
epsilon = 1e-06


def with_halo(block, sides, width, periodic):
    for axis, dim in sides:
        count = lax.axis_size(axis)
        forward = [(i, i + 1) for i in range(count - 1)]
        if periodic:
            forward.append((count - 1, 0))
        backward = [(target, source) for source, target in forward]
        low = lax.ppermute(
            lax.slice_in_dim(block, block.shape[dim] - width, None, axis=dim), axis, forward
        )
        high = lax.ppermute(lax.slice_in_dim(block, 0, width, axis=dim), axis, backward)
        block = jnp.concatenate([low, block, high], axis=dim)
    return block


def from_behind(value, axis, steps):
    count = lax.axis_size(axis)
    pairs = [(source, (source + steps) % count) for source in range(count)]
    return lax.ppermute(value, axis, pairs)


def cell_part(padded, radial_step, azimuth_step, axial_step):
    radial_count = padded.shape[1] - 2
    azimuth_count = padded.shape[2] - 2
    axial_count = padded.shape[3] - 2
    return padded[
        :,
        1 + radial_step : 1 + radial_step + radial_count,
        1 + azimuth_step : 1 + azimuth_step + azimuth_count,
        1 + axial_step : 1 + axial_step + axial_count,
    ]


def velocity_terms(padded_velocity):
    center = cell_part(padded_velocity, 0, 0, 0)
    radial_grad = 0.5 * (cell_part(padded_velocity, 1, 0, 0) - cell_part(padded_velocity, -1, 0, 0))
    azimuth_grad = 0.5 * (
        cell_part(padded_velocity, 0, 1, 0) - cell_part(padded_velocity, 0, -1, 0)
    )
    axial_grad = 0.5 * (cell_part(padded_velocity, 0, 0, 1) - cell_part(padded_velocity, 0, 0, -1))
    return (center, radial_grad, azimuth_grad, axial_grad)


def tendency(padded, motion, radius):
    center_speed, radial_grad, azimuth_grad, axial_grad = motion
    center = cell_part(padded, 0, 0, 0)
    outward = cell_part(padded, 1, 0, 0)
    inward = cell_part(padded, -1, 0, 0)
    forward = cell_part(padded, 0, 1, 0)
    behind = cell_part(padded, 0, -1, 0)
    above_cell = cell_part(padded, 0, 0, 1)
    below_cell = cell_part(padded, 0, 0, -1)
    radial_speed = center_speed[0]
    azimuth_speed = center_speed[1]
    axial_speed = center_speed[2]
    upwind = (
        jnp.maximum(radial_speed, 0.0) * (center - inward)
        + jnp.minimum(radial_speed, 0.0) * (outward - center)
        + jnp.maximum(azimuth_speed, 0.0) * (center - behind)
        + jnp.minimum(azimuth_speed, 0.0) * (forward - center)
        + jnp.maximum(axial_speed, 0.0) * (center - below_cell)
        + jnp.minimum(axial_speed, 0.0) * (above_cell - center)
    )
    stretch = center[0] * radial_grad + center[1] * azimuth_grad + center[2] * axial_grad
    induction = stretch - upwind
    bending = (center[1] * radial_speed - azimuth_speed * center[0]) / radius
    laplace = (
        ((radius + 0.5) * (outward - center) - (radius - 0.5) * (center - inward)) / radius
        + (forward + behind - 2.0 * center)
        + (above_cell + below_cell - 2.0 * center)
    )
    turning = 0.5 * (forward - behind)
    inverse_square = 1.0 / (radius * radius)
    diffuse_radial = laplace[0] - center[0] * inverse_square - 2.0 * turning[1] / radius
    diffuse_azimuth = laplace[1] - center[1] * inverse_square + 2.0 * turning[0] / radius
    diffuse_axial = laplace[2]
    radial_rate = advect_step * induction[0] + diffuse_step * diffuse_radial
    azimuth_rate = advect_step * (induction[1] + bending) + diffuse_step * diffuse_azimuth
    axial_rate = advect_step * induction[2] + diffuse_step * diffuse_axial
    return jnp.stack([radial_rate, azimuth_rate, axial_rate])


def extend_local(fields, flip_signs, wall_factors):
    half_turn = lax.axis_size("phi") // 2
    beside_all = with_halo(fields, (("phi", 2),), 1, True)
    padded = with_halo(beside_all, (("row", 1), ("gz", 3)), 1, False)
    opposite = from_behind(beside_all[:, 0], "phi", half_turn)
    axis_layer = jnp.pad(opposite * flip_signs[:, None, None], ((0, 0), (0, 0), (1, 1)))
    middle = padded[:, 1:-1]
    inner_side = padded[:, 0]
    outer_side = padded[:, -1]
    wall_layer = jnp.pad(fields[:, -1] * wall_factors, ((0, 0), (1, 1), (1, 1)))
    row_position = lax.axis_index("row")
    inner_layer = jnp.where(row_position == 0, axis_layer, inner_side)
    outer_layer = jnp.where(row_position == lax.axis_size("row") - 1, wall_layer, outer_side)
    return jnp.concatenate([inner_layer[:, None], middle, outer_layer[:, None]], axis=1)


def summed_over_part(values):
    axes = ("phi", "gz", "row")
    count = lax.axis_size(axes)
    copies = jnp.broadcast_to(values[None], (count,) + values.shape)
    return jnp.sum(lax.all_to_all(copies, axes, 0, 0, tiled=True), axis=0)


def local(field, velocity, basis, wall_region, wall_conductance):
    regions = wall_conductance.shape[0]
    one_hot = (
        wall_region[None, :, :] == jnp.arange(regions, dtype=jnp.int32)[:, None, None]
    ).astype(jnp.float32)
    conductance = jnp.sum(one_hot * wall_conductance[:, None, None], axis=0)
    reflect = 1.0 - 2.0 * conductance / (1.0 + conductance)
    field_wall = jnp.broadcast_to(reflect[None], (3,) + reflect.shape)
    unity = jnp.ones_like(reflect)
    velocity_wall = jnp.stack([-unity, unity, unity])
    flip_signs = jnp.array([-1.0, -1.0, 1.0], dtype=jnp.float32)
    radial_cells = field.shape[1]
    radius = (
        (lax.axis_index("row") * radial_cells + jnp.arange(radial_cells, dtype=jnp.int32)).astype(
            jnp.float32
        )
        + 0.5
    )[:, None, None]
    joined = extend_local(
        jnp.concatenate([field, velocity], axis=0),
        jnp.concatenate([flip_signs, flip_signs]),
        jnp.concatenate([field_wall, velocity_wall], axis=0),
    )
    motion = velocity_terms(joined[3:])
    section_one = field + tendency(joined[:3], motion, radius)
    second = 0.75 * field + 0.25 * (
        section_one + tendency(extend_local(section_one, flip_signs, field_wall), motion, radius)
    )
    advanced = field / 3.0 + 2.0 / 3.0 * (
        second + tendency(extend_local(second, flip_signs, field_wall), motion, radius)
    )
    cell_count = float(
        field.size * lax.axis_size("phi") * lax.axis_size("gz") * lax.axis_size("row")
    )
    vectors = basis.shape[0]
    everything = jnp.concatenate([basis, advanced[None]], axis=0)
    flat = everything.reshape(vectors + 1, -1)
    partial = lax.dot_general(
        flat, flat, (((1,), (1,)), ((), ())), precision=lax.Precision.HIGHEST
    )
    gram = summed_over_part(partial)
    weights = []
    pending = gram[vectors, :vectors]
    for position in range(vectors):
        weight = pending[position] / gram[position, position]
        weights.append(weight)
        pending = pending - weight * gram[:vectors, position]
    factors = jnp.stack(weights)
    remaining = advanced - jnp.sum(factors[:, None, None, None, None] * basis, axis=0)
    signed = jnp.concatenate([-factors, jnp.ones((1,), jnp.float32)])
    energy = jnp.maximum(jnp.sum(signed[:, None] * signed[None, :] * gram), 0.0)
    spread = jnp.sqrt(energy / cell_count + epsilon)
    return (remaining / spread, jnp.concatenate([factors, spread[None]]))


def solution(mesh):
    return jax.shard_map(
        local,
        mesh=mesh,
        in_specs=(
            P("groups", "row", "phi", "gz"),
            P("groups", "row", "phi", "gz"),
            P("groups", None, "row", "phi", "gz"),
            P(("groups", "phi"), "gz"),
            P("groups"),
        ),
        out_specs=(P("groups", "row", "phi", "gz"), P("groups")),
        check_vma=False,
    )
```

```python
import functools

import jax
import jax.numpy as jnp
import numpy as np
from jax import lax
from jax.experimental import pallas as pl
from jax.experimental.pallas import tpu as pltpu
from jax.sharding import PartitionSpec as P

advect = 0.2
diffuse = 0.1
epsilon = 1e-06
signs = (-1.0, -1.0, 1.0)
wall_signs = (-1.0, 1.0, 1.0)

tiles = 15
wall_row = 8 * tiles
corner_row = wall_row + 8
side_rows = corner_row + 24
low_corner = 8 * tiles
high_corner = low_corner + 24
radial_rows = high_corner + 24
window = 14
sub = 16


def row_of(component, w):
    return (component * window + w) * sub


def vmem(count):
    return [pl.BlockSpec(memory_space=pltpu.VMEM)] * count


def shape(*dims):
    return jax.ShapeDtypeStruct(dims, jnp.float32)


def lanes(rows):
    return lax.broadcasted_iota(jnp.int32, (rows, 128), 1)


def pack_kernel(fold, conductance, region, field, velocity, up, down, inner, outer, reflect, *corners):
    top = lax.axis_index("row").astype(jnp.float32)
    kinds = region[...]
    value = jnp.zeros(kinds.shape, jnp.float32)
    for kind in range(conductance.shape[0]):
        value = jnp.where(kinds == kind, conductance[kind], value)
    reflect[...] = 1.0 - 2.0 * value / (1.0 + value)

    def column(source, c, q):
        return source[pl.ds(c * 64 + q, 8, stride=8), :]

    def layer(source, c, r):
        return source[pl.ds(c * 64 + r * 8, 8), :]

    radius = lax.broadcasted_iota(jnp.int32, (8, 128), 0).astype(jnp.float32) + (top * 8.0 + 0.5)
    turn = diffuse / radius
    for out, (one, two, three), direction in ((up, (7, 6, 5), -1.0), (down, (0, 1, 2), 1.0)):
        for c in range(3):
            out[pl.ds(8 * c, 8), :] = column(field, c, one)
            out[pl.ds(8 * (3 + c), 8), :] = column(velocity, c, one)
            out[pl.ds(8 * (6 + c), 8), :] = column(field, c, two)
            out[pl.ds(8 * (9 + c), 8), :] = column(velocity, c, two)
        speed = column(velocity, 1, two)
        carry = diffuse + advect * jnp.maximum(-direction * speed, 0.0)
        stretch = (0.5 * advect * direction) * column(field, 1, two)
        far = [column(field, c, three) for c in range(3)]
        term = [carry * far[c] + stretch * column(velocity, c, three) for c in range(3)]
        term[0] = term[0] - (direction * turn) * far[1]
        term[1] = term[1] + (direction * turn) * far[0]
        for c in range(3):
            out[pl.ds(8 * (12 + c), 8), :] = term[c]
        out[pl.ds(wall_row, 1), :] = reflect[pl.ds(one, 1), :]
        out[pl.ds(wall_row + 1, 1), :] = reflect[pl.ds(two, 1), :]
    for side, (one, two) in ((0, (7, 6)), (1, (0, 1))):
        if fold:
            out, base = (down, up)[side], corner_row
        else:
            out, base = corners[side], 0
        for place, (r, q) in enumerate(((0, one), (0, two), (1, one))):
            out[pl.ds(base + 8 * place, 3), :] = field[pl.ds(r * 8 + q, 3, stride=64), :]
            out[pl.ds(base + 8 * place + 3, 3), :] = velocity[pl.ds(r * 8 + q, 3, stride=64), :]
    for out, (one, two, three), direction in ((inner, (0, 1, 2), 1.0), (outer, (7, 6, 5), -1.0)):
        middle = top * 8.0 + (two + 0.5)
        pull = diffuse * (middle + 0.5 * direction) / jnp.full((8, 128), middle)
        speed = layer(velocity, 0, two)
        carry = pull + advect * jnp.maximum(-direction * speed, 0.0)
        stretch = (0.5 * advect * direction) * layer(field, 0, two)
        for c in range(3):
            out[pl.ds(8 * c, 8), :] = layer(field, c, one)
            out[pl.ds(8 * (3 + c), 8), :] = layer(velocity, c, one)
            out[pl.ds(8 * (6 + c), 8), :] = layer(field, c, two)
            out[pl.ds(8 * (9 + c), 8), :] = layer(velocity, c, two)
            out[pl.ds(8 * (12 + c), 8), :] = carry * layer(field, c, three) + stretch * layer(
                velocity, c, three
            )


def radial_kernel(below, above, inner, outer, out):
    low_half = lax.axis_index("row") == 0
    for tile in range(tiles):
        rows = pl.ds(8 * tile, 8)
        out[rows, :] = jnp.where(low_half, outer[rows, :], inner[rows, :])
    for source, base in ((below, low_corner), (above, high_corner)):
        for place, (one, two, first) in enumerate(((7, 0, 0), (7, 0, 48), (6, 1, 0))):
            out[pl.ds(base + 8 * place, 6), :] = jnp.where(
                low_half,
                source[pl.ds(first + one, 6, stride=8), :],
                source[pl.ds(first + two, 6, stride=8), :],
            )


def window_kernel(
    fold, field, velocity, below, above, behind, across, reflect, *rest
):
    if fold:
        corner_low, corner_high, corner_base = above, below, corner_row
        walls, strip, cells = rest[0], rest[1], rest[2]
    else:
        corner_low, corner_high, corner_base = rest[0], rest[1], 0
        walls, strip, cells = rest[2], rest[3], rest[4]
    low_half = lax.axis_index("row") == 0
    nothing = jnp.zeros((8, 128), jnp.float32)
    empty = jnp.zeros((sub, 128), jnp.float32)
    for c in range(6):
        source = field if c < 3 else velocity
        sign = signs[c % 3]
        base = 64 * (c % 3)
        cells[pl.ds(row_of(c, 0), sub), :] = empty
        cells[pl.ds(row_of(c, window - 1), sub), :] = empty
        for r in range(8):
            cells[pl.ds(row_of(c, r + 3), 8), :] = source[pl.ds(base + 8 * r, 8), :]
        for w in range(1, window - 1):
            cells[pl.ds(row_of(c, w) + 8, 8), :] = nothing
        for w, first in ((2, 0), (1, 48)):
            place = pl.ds(first + 8 * c, 8)
            cells[pl.ds(row_of(c, w), 8), :] = jnp.where(
                low_half, sign * behind[place, :], across[place, :]
            )
            cells[pl.ds(row_of(c, 13 - w), 8), :] = jnp.where(low_half, across[place, :], 0.0)
        for depth in range(2):
            place = pl.ds(48 * depth + 8 * c, 8)
            cells[pl.ds(row_of(c, 3) + 15 - depth, 8, stride=sub), :] = below[place, :]
            cells[pl.ds(row_of(c, 3) + 8 + depth, 8, stride=sub), :] = above[place, :]
    flip = lax.broadcasted_iota(jnp.int32, (6, 128), 0)
    flip = jnp.where((flip == 2) | (flip == 5), 1.0, -1.0)
    for place, (w, step) in enumerate(((2, 0), (2, 1), (1, 0))):
        for axis_source, base, q in (
            (corner_low, low_corner, 15 - step),
            (corner_high, high_corner, 8 + step),
        ):
            ghost = flip * axis_source[pl.ds(corner_base + 8 * place, 6), :]
            other = across[pl.ds(base + 8 * place, 6), :]
            low = jnp.where(low_half, ghost, other)
            high = jnp.where(low_half, other, 0.0)
            for c in range(6):
                cells[pl.ds(row_of(c, w) + q, 1), :] = low[c : c + 1]
                cells[pl.ds(row_of(c, 13 - w) + q, 1), :] = high[c : c + 1]
    walls[pl.ds(0, 8), :] = reflect[...]
    walls[pl.ds(8, 8), :] = nothing
    walls[pl.ds(8, 2), :] = above[pl.ds(wall_row, 2), :]
    walls[pl.ds(15, 1), :] = below[pl.ds(wall_row, 1), :]
    walls[pl.ds(14, 1), :] = below[pl.ds(wall_row + 1, 1), :]
    slot = lanes(sub) // 8
    for c in range(6):
        packed = jnp.where(slot == 12, pltpu.roll(walls[...], 100, 1), 0.0)
        for w in range(1, window - 1):
            row = cells[pl.ds(row_of(c, w), sub), :]
            packed = jnp.where(slot == w - 1, pltpu.roll(row, (8 * (w - 1) + 4) % 128, 1), packed)
        strip[pl.ds(sub * c, sub), :] = packed


def back(value, axis, step=1):
    return pltpu.roll(value, step, axis)


def ahead(value, axis, step=1):
    return pltpu.roll(value, value.shape[axis] - step, axis)


def rate(center, sides, coefficients):
    inward, outward, before, after, under, over = sides
    pull_in, pull_out, pull_before, pull_after, pull_under, pull_over, keep, mix, turn = coefficients
    result = []
    for c in range(3):
        value = (
            (pull_in * inward[c] + pull_out * outward[c])
            + (pull_before * before[c] + pull_after * after[c])
            + (pull_under * under[c] + pull_over * over[c])
            + keep * center[c]
        )
        for d in range(3):
            value = value + mix[c][d] * center[d]
        result.append(value)
    result[0] = result[0] - turn * (after[1] - before[1])
    result[1] = result[1] + turn * (after[0] - before[0])
    return result


def coefficients_of(speed, sides, sense, inner_pull, outer_pull, bend, inverse_square, turn):
    inward, outward, before, after, under, over = sides
    radial, around, axial = speed
    around_here = sense * around
    pulls = (
        inner_pull + advect * jnp.maximum(radial, 0.0),
        outer_pull - advect * jnp.minimum(radial, 0.0),
        diffuse + advect * jnp.maximum(around_here, 0.0),
        diffuse - advect * jnp.minimum(around_here, 0.0),
        diffuse + advect * jnp.maximum(axial, 0.0),
        diffuse - advect * jnp.minimum(axial, 0.0),
    )
    keep = -6.0 * diffuse - advect * (jnp.abs(radial) + jnp.abs(around) + jnp.abs(axial))
    half = 0.5 * advect
    mix = []
    for c in range(3):
        mix.append(
            [
                half * (outward[c] - inward[c]),
                (half * sense) * (after[c] - before[c]),
                half * (over[c] - under[c]),
            ]
        )
    mix[0][0] = mix[0][0] - diffuse * inverse_square
    mix[1][1] = mix[1][1] - diffuse * inverse_square + bend * radial
    mix[1][0] = mix[1][0] - bend * around
    return pulls + (keep, mix, turn)


def stage_kernel(
    many, below, above, behind, across, walls, strip, *rest
):
    others = rest[: 2 if many else 1]
    (cells, basis, gram, message, advanced, first, second, edge_low, edge_high) = rest[len(others) :]
    top = lax.axis_index("row")
    low_half = top == 0
    place = lax.axis_index("gz")
    has_low = place > 0
    has_high = place < lax.axis_size("gz") - 1
    lane = lanes(sub)
    slot, inside = lane // 8, lane % 8
    mine = [strip[pl.ds(sub * c, sub), :] for c in range(6)]
    if many:
        from_low = [others[0][pl.ds(sub * c, sub), :] for c in range(6)]
        from_high = [others[1][pl.ds(sub * c, sub), :] for c in range(6)]
        strips = [
            [jnp.where(inside < 4, b, a) for a, b in zip(mine, from_low)],
            [jnp.where(inside < 4, a, b) for a, b in zip(mine, from_high)],
        ]
    else:
        other = [others[0][pl.ds(sub * c, sub), :] for c in range(6)]
        strips = [[jnp.where((inside < 4) == has_high, a, b) for a, b in zip(mine, other)]]

    number = (slot - 2).astype(jnp.float32) + top.astype(jnp.float32) * 8.0 + 0.5
    inverse = 1.0 / number
    strip_scalars = (
        jnp.where(number < 0.0, -1.0, 1.0),
        diffuse * (number - 0.5) * inverse,
        diffuse * (number + 0.5) * inverse,
        advect * inverse,
        inverse * inverse,
        diffuse * jnp.abs(inverse),
    )
    strip_wall = jnp.logical_and(slot == 10, top == 1)

    def strip_sides(values):
        return (
            [back(v, 1, 8) for v in values],
            [ahead(v, 1, 8) for v in values],
            [back(v, 0) for v in values],
            [ahead(v, 0) for v in values],
            [back(v, 1) for v in values],
            [ahead(v, 1) for v in values],
        )

    def walled(values, factors):
        return [jnp.where(strip_wall, f * back(v, 1, 8), v) for v, f in zip(values, factors)]

    levels = []
    flows = []
    for line in strips:
        factor = ahead(line[0], 1, 16)
        flow = walled(line[3:], wall_signs)
        flows.append(flow)
        table = coefficients_of(flow, strip_sides(flow), *strip_scalars)
        start = walled(line[:3], [factor] * 3)
        one = rate(start, strip_sides(start), table)
        one = walled([a + b for a, b in zip(start, one)], [factor] * 3)
        two = rate(one, strip_sides(one), table)
        two = [0.75 * s + 0.25 * (a + b) for s, a, b in zip(start, one, two)]
        levels.append((start, one, two))

    def store_edges(low_values, high_values):
        for c in range(3):
            edge_low[pl.ds(sub * c, sub), :] = jnp.where(has_low, low_values[c], 0.0)
            edge_high[pl.ds(sub * c, sub), :] = jnp.where(has_high, high_values[c], 0.0)

    def axial(value, c, w, size):
        low = pltpu.roll(edge_low[pl.ds(sub * c, size), :], (128 - (8 * (w - 1) + 3)) % 128, 1)
        high = pltpu.roll(edge_high[pl.ds(sub * c, size), :], (127 - (8 * (w - 1) + 4)) % 128, 1)
        at = lane[:size]
        return jnp.where(at == 0, low, back(value, 1)), jnp.where(at == 127, high, ahead(value, 1))

    def pick(low, high):
        return jnp.where(low_half, np.float32(low), np.float32(high))

    def scalars(w):
        options = []
        for half in range(2):
            r = half * 8 + (w - 3) + 0.5
            options.append(
                (
                    -1.0 if r < 0 else 1.0,
                    diffuse * (r - 0.5) / r,
                    diffuse * (r + 0.5) / r,
                    advect / r,
                    1.0 / (r * r),
                    diffuse / abs(r),
                )
            )
        return [pick(a, b) for a, b in zip(*options)]

    def read(source, c, w, size=sub):
        return source[pl.ds(row_of(c, w), size), :]

    for c in range(6):
        last = read(cells, c, 10)
        factor = walls[...] if c < 3 else wall_signs[c - 3]
        cells[pl.ds(row_of(c, 11), sub), :] = jnp.where(low_half, read(cells, c, 11), factor * last)

    flow_low, flow_high = flows[0], flows[-1]

    def flow_table(w, size):
        speed, sides = [], [[], [], [], [], [], []]
        for c in range(3):
            value = read(cells, 3 + c, w)
            low = pltpu.roll(jnp.where(has_low, flow_low[c], 0.0), (128 - (8 * (w - 1) + 3)) % 128, 1)
            high = pltpu.roll(jnp.where(has_high, flow_high[c], 0.0), (127 - (8 * (w - 1) + 4)) % 128, 1)
            under = jnp.where(lane == 0, low, back(value, 1))
            over = jnp.where(lane == 127, high, ahead(value, 1))
            for side, part in zip(
                sides,
                (
                    read(cells, 3 + c, w - 1),
                    read(cells, 3 + c, w + 1),
                    back(value, 0),
                    ahead(value, 0),
                    under,
                    over,
                ),
            ):
                side.append(part[:size])
            speed.append(value[:size])
        return coefficients_of(speed, sides, *scalars(w))

    def field_rate(source, w, size):
        center, sides = [], [[], [], [], [], [], []]
        for c in range(3):
            value = read(source, c, w)
            under, over = axial(value[:size], c, w, size)
            for side, part in zip(
                sides,
                (
                    read(source, c, w - 1, size),
                    read(source, c, w + 1, size),
                    back(value, 0)[:size],
                    ahead(value, 0)[:size],
                    under,
                    over,
                ),
            ):
                side.append(part)
            center.append(value[:size])
        return center, rate(center, sides, flow_table(w, size))

    store_edges(levels[0][0], levels[-1][0])
    for w in range(1, 13):
        center, change = field_rate(cells, w, sub)
        for c in range(3):
            first[pl.ds(row_of(c, w), sub), :] = center[c] + change[c]
    for c in range(3):
        rows = pl.ds(8 * (12 + c), 8)
        low, high = pl.ds(row_of(c, 1), 8), pl.ds(row_of(c, 12), 8)
        first[low, :] += jnp.where(low_half, signs[c] * behind[rows, :], across[rows, :])
        first[high, :] += jnp.where(low_half, across[rows, :], 0.0)
        before = pl.ds(row_of(c, 3) + 14, 8, stride=sub)
        after = pl.ds(row_of(c, 3) + 9, 8, stride=sub)
        first[before, :] = first[before, :] + below[rows, :]
        first[after, :] = first[after, :] + above[rows, :]

    def close_wall(source):
        for c in range(3):
            source[pl.ds(row_of(c, 11), sub), :] = jnp.where(
                low_half, read(source, c, 11), walls[...] * read(source, c, 10)
            )

    close_wall(first)
    store_edges(levels[0][1], levels[-1][1])
    for w in range(2, 12):
        center, change = field_rate(first, w, sub)
        for c in range(3):
            second[pl.ds(row_of(c, w), sub), :] = 0.75 * read(cells, c, w) + 0.25 * (
                center[c] + change[c]
            )
    close_wall(second)
    store_edges(levels[0][2], levels[-1][2])
    count = basis.shape[0] // 192
    sums = [jnp.zeros((8, 128), jnp.float32) for _ in range(count + 1)]
    for w in range(3, 11):
        center, change = field_rate(second, w, 8)
        for c in range(3):
            rows = pl.ds(64 * c + 8 * (w - 3), 8)
            value = read(cells, c, w, 8) / 3.0 + (2.0 / 3.0) * (center[c] + change[c])
            advanced[rows, :] = value
            for m in range(count):
                sums[m] += basis[pl.ds(192 * m + 64 * c + 8 * (w - 3), 8), :] * value
            sums[count] += value * value
    spot = lanes(1)
    line = gram[...]
    for m in range(count + 1):
        total = jnp.sum(jnp.sum(sums[m], axis=0, keepdims=True), axis=1, keepdims=True)
        line = jnp.where(spot == m, total, line)
    for device in range(message.shape[0]):
        message[device] = line


def gram_place(m, n):
    return 16 + m * (m + 1) // 2 + n


def gram_kernel(basis, out):
    count = basis.shape[0] // 192
    spot = lanes(1)
    line = jnp.zeros((1, 128), jnp.float32)
    for m in range(count):
        sums = [jnp.zeros((8, 128), jnp.float32) for _ in range(m + 1)]
        for tile in range(24):
            value = basis[pl.ds(192 * m + 8 * tile, 8), :]
            for n in range(m + 1):
                sums[n] += value * basis[pl.ds(192 * n + 8 * tile, 8), :]
        for n in range(m + 1):
            total = jnp.sum(jnp.sum(sums[n], axis=0, keepdims=True), axis=1, keepdims=True)
            line = jnp.where(spot == gram_place(m, n), total, line)
    out[...] = line


def finish_kernel(cell_count, messages, advanced, basis, out, hessenberg):
    count = basis.shape[0] // 192
    total = messages[0]
    for device in range(1, messages.shape[0]):
        total = total + messages[device]

    def entry(index):
        return jnp.broadcast_to(total[:, index : index + 1], (8, 128))

    pending = [entry(m) for m in range(count)]
    energy = entry(count)
    weights = []
    for m in range(count):
        diagonal = entry(gram_place(m, m))
        weight = pending[m] / diagonal
        weights.append(weight)
        energy = energy - weight * (2.0 * pending[m] - weight * diagonal)
        for n in range(m + 1, count):
            pending[n] = pending[n] - weight * entry(gram_place(n, m))
    spread = jnp.sqrt(jnp.maximum(energy, 0.0) / cell_count + epsilon)
    scale = 1.0 / spread
    for tile in range(24):
        rows = pl.ds(8 * tile, 8)
        value = advanced[rows, :]
        for m in range(count):
            value = value - weights[m] * basis[pl.ds(192 * m + 8 * tile, 8), :]
        out[rows, :] = value * scale
    for m in range(count):
        hessenberg[m] = weights[m][0, 0]
    hessenberg[count] = spread[0, 0]


def shift(value, axis, step):
    count = lax.axis_size(axis)
    return lax.ppermute(value, axis, [(i, (i + step) % count) for i in range(count)])


def local(field, velocity, basis, wall_region, wall_conductance):
    loop = lax.axis_size("phi")
    ends = lax.axis_size("gz")
    halves = lax.axis_size("row")
    fold = loop == 4
    many = ends > 2
    vectors = basis.shape[0]
    field_rows = field.reshape(192, 128)
    flow_rows = velocity.reshape(192, 128)
    basis_rows = basis.reshape(vectors * 192, 128)
    side = corner_row if not fold else side_rows
    packed = pl.pallas_call(
        functools.partial(pack_kernel, fold),
        in_specs=[pl.BlockSpec(memory_space=pltpu.SMEM)] + vmem(3),
        out_specs=vmem(5 if fold else 7),
        out_shape=[
            shape(side, 128),
            shape(side, 128),
            shape(8 * tiles, 128),
            shape(8 * tiles, 128),
            shape(8, 128),
        ]
        + ([] if fold else [shape(24, 128)] * 2),
    )(wall_conductance, wall_region, field_rows, flow_rows)
    up, down, inner, outer, reflect = packed[:5]
    below = shift(up, "phi", 1)
    above = shift(down, "phi", -1)
    half = loop // 2
    turned = []
    for p in range(loop):
        for r in range(halves):
            turned.append((p * halves + r, ((p + half) % loop if r == 0 else p) * halves + r))
    behind = lax.ppermute(inner, ("phi", "row"), turned)
    corners = []
    if not fold:
        corners = [shift(packed[5], "phi", half + 1), shift(packed[6], "phi", half - 1)]
    gram = pl.pallas_call(
        gram_kernel, in_specs=vmem(1), out_specs=vmem(1)[0], out_shape=shape(1, 128)
    )(basis_rows)
    radial = pl.pallas_call(
        radial_kernel, in_specs=vmem(4), out_specs=vmem(1)[0], out_shape=shape(radial_rows, 128)
    )(below, above, inner, outer)
    across = lax.ppermute(radial, "row", [(0, 1), (1, 0)])
    walls, strip, cells = pl.pallas_call(
        functools.partial(window_kernel, fold),
        in_specs=vmem(7 + len(corners)),
        out_specs=vmem(3),
        out_shape=[shape(sub, 128), shape(6 * sub, 128), shape(6 * window * sub, 128)],
    )(field_rows, flow_rows, below, above, behind, across, reflect, *corners)
    if many:
        up_pairs = [(i, i + 1) for i in range(ends - 1)]
        others = [
            lax.ppermute(strip, "gz", up_pairs),
            lax.ppermute(strip, "gz", [(b, a) for a, b in up_pairs]),
        ]
    else:
        others = [lax.ppermute(strip, "gz", [(0, 1), (1, 0)])]
    axes = ("phi", "gz", "row")
    devices = lax.axis_size(axes)
    message, advanced = pl.pallas_call(
        functools.partial(stage_kernel, many),
        in_specs=vmem(9 + len(others)),
        out_specs=vmem(2),
        out_shape=[shape(devices, 1, 128), shape(192, 128)],
        scratch_shapes=[
            pltpu.VMEM((3 * window * sub, 128), jnp.float32),
            pltpu.VMEM((3 * window * sub, 128), jnp.float32),
            pltpu.VMEM((3 * sub, 128), jnp.float32),
            pltpu.VMEM((3 * sub, 128), jnp.float32),
        ],
    )(below, above, behind, across, walls, strip, *others, cells, basis_rows, gram)
    messages = lax.all_to_all(message, axes, 0, 0, tiled=True)
    out, hessenberg = pl.pallas_call(
        functools.partial(finish_kernel, float(field.size * devices)),
        in_specs=vmem(3),
        out_specs=vmem(1) + [pl.BlockSpec(memory_space=pltpu.SMEM)],
        out_shape=[shape(192, 128), shape(vectors + 1)],
    )(messages, advanced, basis_rows)
    return out.reshape(field.shape), hessenberg


def solution(mesh):
    return jax.shard_map(
        local,
        mesh=mesh,
        in_specs=(
            P("groups", "row", "phi", "gz"),
            P("groups", "row", "phi", "gz"),
            P("groups", None, "row", "phi", "gz"),
            P(("groups", "phi"), "gz"),
            P("groups"),
        ),
        out_specs=(P("groups", "row", "phi", "gz"), P("groups")),
        check_vma=False,
    )
```

```python
import functools

import jax
import jax.numpy as jnp
import numpy as np
from jax import lax
from jax.experimental import pallas as pl
from jax.experimental.pallas import tpu as pltpu
from jax.sharding import PartitionSpec as P

advect = 0.2
diffuse = 0.1
epsilon = 1e-06
signs = (-1.0, -1.0, 1.0)
wall_signs = (-1.0, 1.0, 1.0)

tiles = 15
wall_row = 8 * tiles
corner_row = wall_row + 8
axis_row = corner_row + 24
side_rows = axis_row + 24
window = 14
sub = 16


def row_of(component, w):
    return (component * window + w) * sub


def vmem(count):
    return [pl.BlockSpec(memory_space=pltpu.VMEM)] * count


def shape(*dims):
    return pltpu.VMEM(dims, jnp.float32)


def near(*values):
    return [pltpu.with_memory_space_constraint(value, pltpu.VMEM) for value in values]


def lanes(rows):
    return lax.broadcasted_iota(jnp.int32, (rows, 128), 1)


def layer(source, c, r):
    return source[pl.ds(c * 64 + r * 8, 8), :]


def inner_kernel(field, velocity, inner):
    middle = lax.axis_index("row").astype(jnp.float32) * 8.0 + 1.5
    pull = diffuse * (middle + 0.5) / jnp.full((8, 128), middle)
    carry = pull - advect * jnp.minimum(layer(velocity, 0, 1), 0.0)
    stretch = (0.5 * advect) * layer(field, 0, 1)
    for c in range(3):
        inner[pl.ds(8 * c, 8), :] = layer(field, c, 0)
        inner[pl.ds(8 * (3 + c), 8), :] = layer(velocity, c, 0)
        inner[pl.ds(8 * (6 + c), 8), :] = layer(field, c, 1)
        inner[pl.ds(8 * (9 + c), 8), :] = layer(velocity, c, 1)
        inner[pl.ds(8 * (12 + c), 8), :] = carry * layer(field, c, 2) + stretch * layer(
            velocity, c, 2
        )


def sides_kernel(
    fold, conductance, region, field, velocity, far_field, far_flow, up, down, reflect, *corners
):
    top = lax.axis_index("row")
    kinds = region[...]
    value = jnp.zeros(kinds.shape, jnp.float32)
    for kind in range(conductance.shape[0]):
        value = jnp.where(kinds == kind, conductance[kind], value)
    reflect[...] = 1.0 - 2.0 * value / (1.0 + value)

    def column(source, c, q):
        return source[pl.ds(c * 64 + q, 8, stride=8), :]

    def cell(source, r, q):
        return source[pl.ds(r * 8 + q, 3, stride=64), :]

    radius = lax.broadcasted_iota(jnp.int32, (8, 128), 0).astype(jnp.float32)
    turn = diffuse / (radius + (top.astype(jnp.float32) * 8.0 + 0.5))
    for out, (one, two, three), direction in ((up, (7, 6, 5), -1.0), (down, (0, 1, 2), 1.0)):
        for c in range(3):
            out[pl.ds(8 * c, 8), :] = column(field, c, one)
            out[pl.ds(8 * (3 + c), 8), :] = column(velocity, c, one)
            out[pl.ds(8 * (6 + c), 8), :] = column(field, c, two)
            out[pl.ds(8 * (9 + c), 8), :] = column(velocity, c, two)
        speed = column(velocity, 1, two)
        carry = diffuse + advect * jnp.maximum(-direction * speed, 0.0)
        stretch = (0.5 * advect * direction) * column(field, 1, two)
        far = [column(field, c, three) for c in range(3)]
        term = [carry * far[c] + stretch * column(velocity, c, three) for c in range(3)]
        term[0] = term[0] - (direction * turn) * far[1]
        term[1] = term[1] + (direction * turn) * far[0]
        for c in range(3):
            out[pl.ds(8 * (12 + c), 8), :] = term[c]
        out[pl.ds(wall_row, 1), :] = reflect[pl.ds(one, 1), :]
        out[pl.ds(wall_row + 1, 1), :] = reflect[pl.ds(two, 1), :]
        for place, (r, q) in enumerate(((0, one), (0, two), (1, one))):
            for part, source in enumerate((far_field, far_flow)):
                out[pl.ds(corner_row + 8 * place + 3 * part, 3), :] = jnp.where(
                    top == 0, cell(source, r, q), cell(source, 7 - r, q)
                )
    for side, (one, two) in ((0, (7, 6)), (1, (0, 1))):
        if fold:
            out, base = (down, up)[side], axis_row
        else:
            out, base = corners[side], 0
        for place, (r, q) in enumerate(((0, one), (0, two), (1, one))):
            out[pl.ds(base + 8 * place, 3), :] = cell(field, r, q)
            out[pl.ds(base + 8 * place + 3, 3), :] = cell(velocity, r, q)


def window_kernel(
    fold, field, velocity, far_field, far_flow, below, above, behind, reflect, *rest
):
    if fold:
        axis_low, axis_high, axis_base = above, below, axis_row
    else:
        axis_low, axis_high, axis_base = rest[0], rest[1], 0
    walls, strip, cells = rest[-3:]
    low_half = lax.axis_index("row") == 0
    nothing = jnp.zeros((8, 128), jnp.float32)
    for c in range(6):
        source, far = (field, far_field) if c < 3 else (velocity, far_flow)
        sign = signs[c % 3]
        for r in range(8):
            cells[pl.ds(row_of(c, r + 3), 8), :] = layer(source, c % 3, r)
        for w in range(window):
            cells[pl.ds(row_of(c, w) + 8, 8), :] = nothing
        for w in range(3):
            ghost = sign * behind[pl.ds(48 * (2 - w) + 8 * c, 8), :] if w > 0 else 0.0
            cells[pl.ds(row_of(c, w), 8), :] = jnp.where(low_half, ghost, layer(far, c % 3, 5 + w))
            cells[pl.ds(row_of(c, 11 + w), 8), :] = jnp.where(low_half, layer(far, c % 3, w), 0.0)
        for depth in range(2):
            place = pl.ds(48 * depth + 8 * c, 8)
            cells[pl.ds(row_of(c, 3) + 15 - depth, 8, stride=sub), :] = below[place, :]
            cells[pl.ds(row_of(c, 3) + 8 + depth, 8, stride=sub), :] = above[place, :]
    flip = lax.broadcasted_iota(jnp.int32, (6, 128), 0)
    flip = jnp.where((flip == 2) | (flip == 5), 1.0, -1.0)
    for place, (w, step) in enumerate(((2, 0), (2, 1), (1, 0))):
        for axis_source, source, q in ((axis_low, below, 15 - step), (axis_high, above, 8 + step)):
            ghost = flip * axis_source[pl.ds(axis_base + 8 * place, 6), :]
            other = source[pl.ds(corner_row + 8 * place, 6), :]
            low = jnp.where(low_half, ghost, other)
            high = jnp.where(low_half, other, 0.0)
            for c in range(6):
                cells[pl.ds(row_of(c, w) + q, 1), :] = low[c : c + 1]
                cells[pl.ds(row_of(c, 13 - w) + q, 1), :] = high[c : c + 1]
    walls[pl.ds(0, 8), :] = reflect[...]
    walls[pl.ds(8, 8), :] = nothing
    walls[pl.ds(8, 2), :] = above[pl.ds(wall_row, 2), :]
    walls[pl.ds(15, 1), :] = below[pl.ds(wall_row, 1), :]
    walls[pl.ds(14, 1), :] = below[pl.ds(wall_row + 1, 1), :]
    slot = lanes(sub) // 8
    for c in range(6):
        packed = jnp.where(slot == 12, pltpu.roll(walls[...], 100, 1), 0.0)
        for w in range(1, window - 1):
            row = cells[pl.ds(row_of(c, w), sub), :]
            packed = jnp.where(slot == w - 1, pltpu.roll(row, (8 * (w - 1) + 4) % 128, 1), packed)
        strip[pl.ds(sub * c, sub), :] = packed


def back(value, axis, step=1):
    return pltpu.roll(value, step, axis)


def ahead(value, axis, step=1):
    return pltpu.roll(value, value.shape[axis] - step, axis)


def rate(center, sides, coefficients):
    inward, outward, before, after, under, over = sides
    pull_in, pull_out, pull_before, pull_after, pull_under, pull_over, keep, mix, turn = coefficients
    result = []
    for c in range(3):
        value = (
            (pull_in * inward[c] + pull_out * outward[c])
            + (pull_before * before[c] + pull_after * after[c])
            + (pull_under * under[c] + pull_over * over[c])
            + keep * center[c]
        )
        for d in range(3):
            value = value + mix[c][d] * center[d]
        result.append(value)
    result[0] = result[0] - turn * (after[1] - before[1])
    result[1] = result[1] + turn * (after[0] - before[0])
    return result


def coefficients_of(speed, sides, sense, inner_pull, outer_pull, bend, inverse_square, turn):
    inward, outward, before, after, under, over = sides
    radial, around, axial = speed
    around_here = sense * around
    pulls = (
        inner_pull + advect * jnp.maximum(radial, 0.0),
        outer_pull - advect * jnp.minimum(radial, 0.0),
        diffuse + advect * jnp.maximum(around_here, 0.0),
        diffuse - advect * jnp.minimum(around_here, 0.0),
        diffuse + advect * jnp.maximum(axial, 0.0),
        diffuse - advect * jnp.minimum(axial, 0.0),
    )
    keep = -6.0 * diffuse - advect * (jnp.abs(radial) + jnp.abs(around) + jnp.abs(axial))
    half = 0.5 * advect
    mix = []
    for c in range(3):
        mix.append(
            [
                half * (outward[c] - inward[c]),
                (half * sense) * (after[c] - before[c]),
                half * (over[c] - under[c]),
            ]
        )
    mix[0][0] = mix[0][0] - diffuse * inverse_square
    mix[1][1] = mix[1][1] - diffuse * inverse_square + bend * radial
    mix[1][0] = mix[1][0] - bend * around
    return pulls + (keep, mix, turn)


def stage_kernel(
    many, below, above, behind, walls, strip, *rest
):
    others = rest[: 2 if many else 1]
    (cells, basis, gram, message, advanced, first, second, edge_low, edge_high) = rest[len(others) :]
    top = lax.axis_index("row")
    low_half = top == 0
    place = lax.axis_index("gz")
    has_low = place > 0
    has_high = place < lax.axis_size("gz") - 1
    lane = lanes(sub)
    slot, inside = lane // 8, lane % 8
    mine = [strip[pl.ds(sub * c, sub), :] for c in range(6)]
    if many:
        from_low = [others[0][pl.ds(sub * c, sub), :] for c in range(6)]
        from_high = [others[1][pl.ds(sub * c, sub), :] for c in range(6)]
        strips = [
            [jnp.where(inside < 4, b, a) for a, b in zip(mine, from_low)],
            [jnp.where(inside < 4, a, b) for a, b in zip(mine, from_high)],
        ]
    else:
        other = [others[0][pl.ds(sub * c, sub), :] for c in range(6)]
        strips = [[jnp.where((inside < 4) == has_high, a, b) for a, b in zip(mine, other)]]

    number = (slot - 2).astype(jnp.float32) + top.astype(jnp.float32) * 8.0 + 0.5
    inverse = 1.0 / number
    strip_scalars = (
        jnp.where(number < 0.0, -1.0, 1.0),
        diffuse * (number - 0.5) * inverse,
        diffuse * (number + 0.5) * inverse,
        advect * inverse,
        inverse * inverse,
        diffuse * jnp.abs(inverse),
    )
    strip_wall = jnp.logical_and(slot == 10, top == 1)

    def strip_sides(values):
        return (
            [back(v, 1, 8) for v in values],
            [ahead(v, 1, 8) for v in values],
            [back(v, 0) for v in values],
            [ahead(v, 0) for v in values],
            [back(v, 1) for v in values],
            [ahead(v, 1) for v in values],
        )

    def walled(values, factors):
        return [jnp.where(strip_wall, f * back(v, 1, 8), v) for v, f in zip(values, factors)]

    levels = []
    flows = []
    for line in strips:
        factor = ahead(line[0], 1, 16)
        flow = walled(line[3:], wall_signs)
        flows.append(flow)
        table = coefficients_of(flow, strip_sides(flow), *strip_scalars)
        start = walled(line[:3], [factor] * 3)
        one = rate(start, strip_sides(start), table)
        one = walled([a + b for a, b in zip(start, one)], [factor] * 3)
        two = rate(one, strip_sides(one), table)
        two = [0.75 * s + 0.25 * (a + b) for s, a, b in zip(start, one, two)]
        levels.append((start, one, two))

    def store_edges(low_values, high_values):
        for c in range(3):
            edge_low[pl.ds(sub * c, sub), :] = jnp.where(has_low, low_values[c], 0.0)
            edge_high[pl.ds(sub * c, sub), :] = jnp.where(has_high, high_values[c], 0.0)

    def axial(value, c, w, size):
        low = pltpu.roll(edge_low[pl.ds(sub * c, size), :], (128 - (8 * (w - 1) + 3)) % 128, 1)
        high = pltpu.roll(edge_high[pl.ds(sub * c, size), :], (127 - (8 * (w - 1) + 4)) % 128, 1)
        at = lane[:size]
        return jnp.where(at == 0, low, back(value, 1)), jnp.where(at == 127, high, ahead(value, 1))

    def pick(low, high):
        return jnp.where(low_half, np.float32(low), np.float32(high))

    def scalars(w):
        options = []
        for half in range(2):
            r = half * 8 + (w - 3) + 0.5
            options.append(
                (
                    -1.0 if r < 0 else 1.0,
                    diffuse * (r - 0.5) / r,
                    diffuse * (r + 0.5) / r,
                    advect / r,
                    1.0 / (r * r),
                    diffuse / abs(r),
                )
            )
        return [pick(a, b) for a, b in zip(*options)]

    def read(source, c, w, size=sub):
        return source[pl.ds(row_of(c, w), size), :]

    for c in range(6):
        last = read(cells, c, 10)
        factor = walls[...] if c < 3 else wall_signs[c - 3]
        cells[pl.ds(row_of(c, 11), sub), :] = jnp.where(low_half, read(cells, c, 11), factor * last)

    flow_low, flow_high = flows[0], flows[-1]

    def flow_table(w, size):
        speed, sides = [], [[], [], [], [], [], []]
        for c in range(3):
            value = read(cells, 3 + c, w)
            low = pltpu.roll(jnp.where(has_low, flow_low[c], 0.0), (128 - (8 * (w - 1) + 3)) % 128, 1)
            high = pltpu.roll(jnp.where(has_high, flow_high[c], 0.0), (127 - (8 * (w - 1) + 4)) % 128, 1)
            under = jnp.where(lane == 0, low, back(value, 1))
            over = jnp.where(lane == 127, high, ahead(value, 1))
            for side, part in zip(
                sides,
                (
                    read(cells, 3 + c, w - 1),
                    read(cells, 3 + c, w + 1),
                    back(value, 0),
                    ahead(value, 0),
                    under,
                    over,
                ),
            ):
                side.append(part[:size])
            speed.append(value[:size])
        return coefficients_of(speed, sides, *scalars(w))

    def field_rate(source, w, size):
        center, sides = [], [[], [], [], [], [], []]
        for c in range(3):
            value = read(source, c, w)
            under, over = axial(value[:size], c, w, size)
            for side, part in zip(
                sides,
                (
                    read(source, c, w - 1, size),
                    read(source, c, w + 1, size),
                    back(value, 0)[:size],
                    ahead(value, 0)[:size],
                    under,
                    over,
                ),
            ):
                side.append(part)
            center.append(value[:size])
        return center, rate(center, sides, flow_table(w, size))

    store_edges(levels[0][0], levels[-1][0])
    for w in range(1, 13):
        center, change = field_rate(cells, w, sub)
        for c in range(3):
            first[pl.ds(row_of(c, w), sub), :] = center[c] + change[c]
    for c in range(3):
        rows = pl.ds(8 * (12 + c), 8)
        low = pl.ds(row_of(c, 1), 8)
        first[low, :] = first[low, :] + jnp.where(low_half, signs[c] * behind[rows, :], 0.0)
        before = pl.ds(row_of(c, 3) + 14, 8, stride=sub)
        after = pl.ds(row_of(c, 3) + 9, 8, stride=sub)
        first[before, :] = first[before, :] + below[rows, :]
        first[after, :] = first[after, :] + above[rows, :]

    def close_wall(source):
        for c in range(3):
            source[pl.ds(row_of(c, 11), sub), :] = jnp.where(
                low_half, read(source, c, 11), walls[...] * read(source, c, 10)
            )

    close_wall(first)
    store_edges(levels[0][1], levels[-1][1])
    for w in range(2, 12):
        center, change = field_rate(first, w, sub)
        for c in range(3):
            second[pl.ds(row_of(c, w), sub), :] = 0.75 * read(cells, c, w) + 0.25 * (
                center[c] + change[c]
            )
    close_wall(second)
    store_edges(levels[0][2], levels[-1][2])
    count = basis.shape[0] // 192
    sums = [jnp.zeros((8, 128), jnp.float32) for _ in range(count + 1)]
    for w in range(3, 11):
        center, change = field_rate(second, w, 8)
        for c in range(3):
            rows = pl.ds(64 * c + 8 * (w - 3), 8)
            value = read(cells, c, w, 8) / 3.0 + (2.0 / 3.0) * (center[c] + change[c])
            advanced[rows, :] = value
            for m in range(count):
                sums[m] += basis[pl.ds(192 * m + 64 * c + 8 * (w - 3), 8), :] * value
            sums[count] += value * value
    spot = lanes(1)
    line = gram[...]
    for m in range(count + 1):
        total = jnp.sum(jnp.sum(sums[m], axis=0, keepdims=True), axis=1, keepdims=True)
        line = jnp.where(spot == m, total, line)
    for device in range(message.shape[0]):
        message[device] = line


def gram_place(m, n):
    return 16 + m * (m + 1) // 2 + n


def gram_kernel(basis, out):
    count = basis.shape[0] // 192
    spot = lanes(1)
    line = jnp.zeros((1, 128), jnp.float32)
    for m in range(count):
        sums = [jnp.zeros((8, 128), jnp.float32) for _ in range(m + 1)]
        for tile in range(24):
            value = basis[pl.ds(192 * m + 8 * tile, 8), :]
            for n in range(m + 1):
                sums[n] += value * basis[pl.ds(192 * n + 8 * tile, 8), :]
        for n in range(m + 1):
            total = jnp.sum(jnp.sum(sums[n], axis=0, keepdims=True), axis=1, keepdims=True)
            line = jnp.where(spot == gram_place(m, n), total, line)
    out[...] = line


def finish_kernel(cell_count, messages, advanced, basis, out, hessenberg):
    count = basis.shape[0] // 192
    total = messages[0]
    for device in range(1, messages.shape[0]):
        total = total + messages[device]

    def entry(index):
        return jnp.broadcast_to(total[:, index : index + 1], (8, 128))

    pending = [entry(m) for m in range(count)]
    energy = entry(count)
    weights = []
    for m in range(count):
        diagonal = entry(gram_place(m, m))
        weight = pending[m] / diagonal
        weights.append(weight)
        energy = energy - weight * (2.0 * pending[m] - weight * diagonal)
        for n in range(m + 1, count):
            pending[n] = pending[n] - weight * entry(gram_place(n, m))
    spread = jnp.sqrt(jnp.maximum(energy, 0.0) / cell_count + epsilon)
    scale = 1.0 / spread
    for tile in range(24):
        rows = pl.ds(8 * tile, 8)
        value = advanced[rows, :]
        for m in range(count):
            value = value - weights[m] * basis[pl.ds(192 * m + 8 * tile, 8), :]
        out[rows, :] = value * scale
    for m in range(count):
        hessenberg[m] = weights[m][0, 0]
    hessenberg[count] = spread[0, 0]


def shift(value, axis, step):
    count = lax.axis_size(axis)
    return lax.ppermute(value, axis, [(i, (i + step) % count) for i in range(count)])


def local(field, velocity, basis, wall_region, wall_conductance):
    loop = lax.axis_size("phi")
    ends = lax.axis_size("gz")
    halves = lax.axis_size("row")
    fold = loop == 4
    many = ends > 2
    vectors = basis.shape[0]
    field_rows = field.reshape(192, 128)
    flow_rows = velocity.reshape(192, 128)
    swap = [(0, 1), (1, 0)]
    far_field = lax.ppermute(field_rows, "row", swap)
    far_flow = lax.ppermute(flow_rows, "row", swap)
    field_rows, flow_rows, basis_rows = near(
        field_rows, flow_rows, basis.reshape(vectors * 192, 128)
    )
    inner = pl.pallas_call(
        inner_kernel, in_specs=vmem(2), out_specs=vmem(1)[0], out_shape=shape(8 * tiles, 128)
    )(field_rows, flow_rows)
    half = loop // 2
    turned = []
    for p in range(loop):
        for r in range(halves):
            turned.append((p * halves + r, ((p + half) % loop if r == 0 else p) * halves + r))
    behind = lax.ppermute(inner, ("phi", "row"), turned)
    far_field, far_flow = near(far_field, far_flow)
    side = side_rows if fold else axis_row
    packed = pl.pallas_call(
        functools.partial(sides_kernel, fold),
        in_specs=[pl.BlockSpec(memory_space=pltpu.SMEM)] + vmem(5),
        out_specs=vmem(3 if fold else 5),
        out_shape=[shape(side, 128), shape(side, 128), shape(8, 128)]
        + ([] if fold else [shape(24, 128)] * 2),
    )(wall_conductance, wall_region, field_rows, flow_rows, far_field, far_flow)
    up, down, reflect = packed[:3]
    below = shift(up, "phi", 1)
    above = shift(down, "phi", -1)
    corners = []
    if not fold:
        corners = [shift(packed[3], "phi", half + 1), shift(packed[4], "phi", half - 1)]
    gram = pl.pallas_call(
        gram_kernel, in_specs=vmem(1), out_specs=vmem(1)[0], out_shape=shape(1, 128)
    )(basis_rows)
    below, above, behind, gram, *corners = lax.optimization_barrier(
        (below, above, behind, gram, *corners)
    )
    below, above, behind, gram, *corners = near(below, above, behind, gram, *corners)
    walls, strip, cells = pl.pallas_call(
        functools.partial(window_kernel, fold),
        in_specs=vmem(8 + len(corners)),
        out_specs=vmem(3),
        out_shape=[shape(sub, 128), shape(6 * sub, 128), shape(6 * window * sub, 128)],
    )(field_rows, flow_rows, far_field, far_flow, below, above, behind, reflect, *corners)
    if many:
        up_pairs = [(i, i + 1) for i in range(ends - 1)]
        others = [
            lax.ppermute(strip, "gz", up_pairs),
            lax.ppermute(strip, "gz", [(b, a) for a, b in up_pairs]),
        ]
    else:
        others = [lax.ppermute(strip, "gz", swap)]
    walls, strip, cells, *others = near(walls, strip, cells, *others)
    axes = ("phi", "gz", "row")
    devices = lax.axis_size(axes)
    message, advanced = pl.pallas_call(
        functools.partial(stage_kernel, many),
        in_specs=vmem(8 + len(others)),
        out_specs=vmem(2),
        out_shape=[shape(devices, 1, 128), shape(192, 128)],
        scratch_shapes=[
            pltpu.VMEM((3 * window * sub, 128), jnp.float32),
            pltpu.VMEM((3 * window * sub, 128), jnp.float32),
            pltpu.VMEM((3 * sub, 128), jnp.float32),
            pltpu.VMEM((3 * sub, 128), jnp.float32),
        ],
    )(below, above, behind, walls, strip, *others, cells, basis_rows, gram)
    messages = lax.all_to_all(message, axes, 0, 0, tiled=True)
    messages, advanced = near(messages, advanced)
    out, hessenberg = pl.pallas_call(
        functools.partial(finish_kernel, float(field.size * devices)),
        in_specs=vmem(3),
        out_specs=vmem(1) + [pl.BlockSpec(memory_space=pltpu.SMEM)],
        out_shape=[
            jax.ShapeDtypeStruct((192, 128), jnp.float32),
            jax.ShapeDtypeStruct((vectors + 1,), jnp.float32),
        ],
    )(messages, advanced, basis_rows)
    return out.reshape(field.shape), hessenberg


def solution(mesh):
    return jax.shard_map(
        local,
        mesh=mesh,
        in_specs=(
            P("groups", "row", "phi", "gz"),
            P("groups", "row", "phi", "gz"),
            P("groups", None, "row", "phi", "gz"),
            P(("groups", "phi"), "gz"),
            P("groups"),
        ),
        out_specs=(P("groups", "row", "phi", "gz"), P("groups")),
        check_vma=False,
    )
```

```python
import functools

import jax
import jax.numpy as jnp
import numpy as np
from jax import lax
from jax.experimental import pallas as pl
from jax.experimental.pallas import tpu as pltpu
from jax.sharding import PartitionSpec as P

advect = 0.2
diffuse = 0.1
epsilon = 1e-06
signs = (-1.0, -1.0, 1.0)
wall_signs = (-1.0, 1.0, 1.0)

tiles = 15
wall_row = 8 * tiles
corner_row = wall_row + 8
axis_row = corner_row + 24
side_rows = axis_row + 24
window = 14
sub = 16


def row_of(component, w):
    return (component * window + w) * sub


def vmem(count):
    return [pl.BlockSpec(memory_space=pltpu.VMEM)] * count


def shape(*dims):
    return pltpu.VMEM(dims, jnp.float32)


def near(*values):
    return [pltpu.with_memory_space_constraint(value, pltpu.VMEM) for value in values]


def lanes(rows):
    return lax.broadcasted_iota(jnp.int32, (rows, 128), 1)


def layer(source, c, r):
    return source[pl.ds(c * 64 + r * 8, 8), :]


def first_kernel(conductance, region, field, velocity, inner, reflect, field_copy, flow_copy):
    middle = lax.axis_index("row").astype(jnp.float32) * 8.0 + 1.5
    pull = diffuse * (middle + 0.5) / jnp.full((8, 128), middle)
    carry = pull - advect * jnp.minimum(layer(velocity, 0, 1), 0.0)
    stretch = (0.5 * advect) * layer(field, 0, 1)
    for c in range(3):
        inner[pl.ds(8 * c, 8), :] = layer(field, c, 0)
        inner[pl.ds(8 * (3 + c), 8), :] = layer(velocity, c, 0)
        inner[pl.ds(8 * (6 + c), 8), :] = layer(field, c, 1)
        inner[pl.ds(8 * (9 + c), 8), :] = layer(velocity, c, 1)
        inner[pl.ds(8 * (12 + c), 8), :] = carry * layer(field, c, 2) + stretch * layer(
            velocity, c, 2
        )
    kinds = region[...]
    value = jnp.zeros(kinds.shape, jnp.float32)
    for kind in range(conductance.shape[0]):
        value = jnp.where(kinds == kind, conductance[kind], value)
    reflect[...] = 1.0 - 2.0 * value / (1.0 + value)
    field_copy[...] = field[...]
    flow_copy[...] = velocity[...]


def sides_kernel(
    fold, field, velocity, far_field, far_flow, reflect, up, down, *corners
):
    top = lax.axis_index("row")

    def column(source, c, q):
        return source[pl.ds(c * 64 + q, 8, stride=8), :]

    def cell(source, r, q):
        return source[pl.ds(r * 8 + q, 3, stride=64), :]

    radius = lax.broadcasted_iota(jnp.int32, (8, 128), 0).astype(jnp.float32)
    turn = diffuse / (radius + (top.astype(jnp.float32) * 8.0 + 0.5))
    for out, (one, two, three), direction in ((up, (7, 6, 5), -1.0), (down, (0, 1, 2), 1.0)):
        for c in range(3):
            out[pl.ds(8 * c, 8), :] = column(field, c, one)
            out[pl.ds(8 * (3 + c), 8), :] = column(velocity, c, one)
            out[pl.ds(8 * (6 + c), 8), :] = column(field, c, two)
            out[pl.ds(8 * (9 + c), 8), :] = column(velocity, c, two)
        speed = column(velocity, 1, two)
        carry = diffuse + advect * jnp.maximum(-direction * speed, 0.0)
        stretch = (0.5 * advect * direction) * column(field, 1, two)
        far = [column(field, c, three) for c in range(3)]
        term = [carry * far[c] + stretch * column(velocity, c, three) for c in range(3)]
        term[0] = term[0] - (direction * turn) * far[1]
        term[1] = term[1] + (direction * turn) * far[0]
        for c in range(3):
            out[pl.ds(8 * (12 + c), 8), :] = term[c]
        out[pl.ds(wall_row, 1), :] = reflect[pl.ds(one, 1), :]
        out[pl.ds(wall_row + 1, 1), :] = reflect[pl.ds(two, 1), :]
        for place, (r, q) in enumerate(((0, one), (0, two), (1, one))):
            for part, source in enumerate((far_field, far_flow)):
                out[pl.ds(corner_row + 8 * place + 3 * part, 3), :] = jnp.where(
                    top == 0, cell(source, r, q), cell(source, 7 - r, q)
                )
    for side, (one, two) in ((0, (7, 6)), (1, (0, 1))):
        if fold:
            out, base = (down, up)[side], axis_row
        else:
            out, base = corners[side], 0
        for place, (r, q) in enumerate(((0, one), (0, two), (1, one))):
            out[pl.ds(base + 8 * place, 3), :] = cell(field, r, q)
            out[pl.ds(base + 8 * place + 3, 3), :] = cell(velocity, r, q)


def packed_row(strip, value, w):
    slot = lanes(value.shape[0]) // 8
    return jnp.where(slot == w - 1, pltpu.roll(value, (8 * (w - 1) + 4) % 128, 1), strip)


def frame_kernel(field, velocity, far_field, far_flow, strip, cells):
    low_half = lax.axis_index("row") == 0
    nothing = jnp.zeros((8, 128), jnp.float32)
    for c in range(6):
        source, far = (field, far_field) if c < 3 else (velocity, far_flow)
        packed = nothing
        for w in range(window):
            if w < 3:
                value = jnp.where(low_half, 0.0, layer(far, c % 3, 5 + w))
            elif w < 11:
                value = layer(source, c % 3, w - 3)
            else:
                value = jnp.where(low_half, layer(far, c % 3, w - 11), 0.0)
            cells[pl.ds(row_of(c, w), 8), :] = value
            cells[pl.ds(row_of(c, w) + 8, 8), :] = nothing
            if 0 < w < window - 1:
                packed = packed_row(packed, value, w)
        strip[pl.ds(sub * c, 8), :] = packed
        strip[pl.ds(sub * c + 8, 8), :] = nothing


def window_kernel(fold, below, above, behind, reflect, frame_strip, frame, *rest):
    if fold:
        axis_low, axis_high, axis_base = above, below, axis_row
    else:
        axis_low, axis_high, axis_base = rest[0], rest[1], 0
    walls, strip, cells = rest[-3:]
    low_half = lax.axis_index("row") == 0
    for c in range(6):
        for depth in range(2):
            place = pl.ds(48 * depth + 8 * c, 8)
            cells[pl.ds(row_of(c, 3) + 15 - depth, 8, stride=sub), :] = below[place, :]
            cells[pl.ds(row_of(c, 3) + 8 + depth, 8, stride=sub), :] = above[place, :]
    flip = lax.broadcasted_iota(jnp.int32, (6, 128), 0)
    flip = jnp.where((flip == 2) | (flip == 5), 1.0, -1.0)
    for place, (w, step) in enumerate(((2, 0), (2, 1), (1, 0))):
        for axis_source, source, q in ((axis_low, below, 15 - step), (axis_high, above, 8 + step)):
            ghost = flip * axis_source[pl.ds(axis_base + 8 * place, 6), :]
            other = source[pl.ds(corner_row + 8 * place, 6), :]
            low = pl.ds(row_of(0, w) + q, 6, stride=window * sub)
            high = pl.ds(row_of(0, 13 - w) + q, 6, stride=window * sub)
            cells[low, :] = jnp.where(low_half, ghost, other)
            cells[high, :] = jnp.where(low_half, other, 0.0)
    walls[pl.ds(0, 8), :] = reflect[...]
    walls[pl.ds(8, 8), :] = jnp.zeros((8, 128), jnp.float32)
    walls[pl.ds(8, 2), :] = above[pl.ds(wall_row, 2), :]
    walls[pl.ds(15, 1), :] = below[pl.ds(wall_row, 1), :]
    walls[pl.ds(14, 1), :] = below[pl.ds(wall_row + 1, 1), :]
    slot = lanes(8) // 8
    for c in range(6):
        packed = strip[pl.ds(sub * c, 8), :]
        for w in range(1, 3):
            place = pl.ds(row_of(c, w), 8)
            ghost = signs[c % 3] * behind[pl.ds(48 * (2 - w) + 8 * c, 8), :]
            ghost = jnp.where(low_half, ghost, cells[place, :])
            cells[place, :] = ghost
            packed = packed_row(packed, ghost, w)
        beyond = jnp.zeros((8, 128), jnp.float32)
        for w in range(1, window - 1):
            beyond = packed_row(beyond, cells[pl.ds(row_of(c, w) + 8, 8), :], w)
        if c == 0:
            packed = jnp.where(slot == 12, pltpu.roll(walls[pl.ds(0, 8), :], 100, 1), packed)
            beyond = jnp.where(slot == 12, pltpu.roll(walls[pl.ds(8, 8), :], 100, 1), beyond)
        strip[pl.ds(sub * c, 8), :] = packed
        strip[pl.ds(sub * c + 8, 8), :] = beyond


def back(value, axis, step=1):
    return pltpu.roll(value, step, axis)


def ahead(value, axis, step=1):
    return pltpu.roll(value, value.shape[axis] - step, axis)


def rate(center, sides, coefficients):
    inward, outward, before, after, under, over = sides
    pull_in, pull_out, pull_before, pull_after, pull_under, pull_over, keep, mix, turn = coefficients
    result = []
    for c in range(3):
        value = (
            (pull_in * inward[c] + pull_out * outward[c])
            + (pull_before * before[c] + pull_after * after[c])
            + (pull_under * under[c] + pull_over * over[c])
            + keep * center[c]
        )
        for d in range(3):
            value = value + mix[c][d] * center[d]
        result.append(value)
    result[0] = result[0] - turn * (after[1] - before[1])
    result[1] = result[1] + turn * (after[0] - before[0])
    return result


def coefficients_of(speed, sides, sense, inner_pull, outer_pull, bend, inverse_square, turn):
    inward, outward, before, after, under, over = sides
    radial, around, axial = speed
    around_here = sense * around
    pulls = (
        inner_pull + advect * jnp.maximum(radial, 0.0),
        outer_pull - advect * jnp.minimum(radial, 0.0),
        diffuse + advect * jnp.maximum(around_here, 0.0),
        diffuse - advect * jnp.minimum(around_here, 0.0),
        diffuse + advect * jnp.maximum(axial, 0.0),
        diffuse - advect * jnp.minimum(axial, 0.0),
    )
    keep = -6.0 * diffuse - advect * (jnp.abs(radial) + jnp.abs(around) + jnp.abs(axial))
    half = 0.5 * advect
    mix = []
    for c in range(3):
        mix.append(
            [
                half * (outward[c] - inward[c]),
                (half * sense) * (after[c] - before[c]),
                half * (over[c] - under[c]),
            ]
        )
    mix[0][0] = mix[0][0] - diffuse * inverse_square
    mix[1][1] = mix[1][1] - diffuse * inverse_square + bend * radial
    mix[1][0] = mix[1][0] - bend * around
    return pulls + (keep, mix, turn)


def stage_kernel(
    many, below, above, behind, walls, strip, *rest
):
    others = rest[: 2 if many else 1]
    (cells, basis, gram, message, advanced, first, second, edge_low, edge_high) = rest[len(others) :]
    top = lax.axis_index("row")
    low_half = top == 0
    place = lax.axis_index("gz")
    has_low = place > 0
    has_high = place < lax.axis_size("gz") - 1
    lane = lanes(sub)
    slot, inside = lane // 8, lane % 8
    mine = [strip[pl.ds(sub * c, sub), :] for c in range(6)]
    if many:
        from_low = [others[0][pl.ds(sub * c, sub), :] for c in range(6)]
        from_high = [others[1][pl.ds(sub * c, sub), :] for c in range(6)]
        strips = [
            [jnp.where(inside < 4, b, a) for a, b in zip(mine, from_low)],
            [jnp.where(inside < 4, a, b) for a, b in zip(mine, from_high)],
        ]
    else:
        other = [others[0][pl.ds(sub * c, sub), :] for c in range(6)]
        strips = [[jnp.where((inside < 4) == has_high, a, b) for a, b in zip(mine, other)]]

    number = (slot - 2).astype(jnp.float32) + top.astype(jnp.float32) * 8.0 + 0.5
    inverse = 1.0 / number
    strip_scalars = (
        jnp.where(number < 0.0, -1.0, 1.0),
        diffuse * (number - 0.5) * inverse,
        diffuse * (number + 0.5) * inverse,
        advect * inverse,
        inverse * inverse,
        diffuse * jnp.abs(inverse),
    )
    strip_wall = jnp.logical_and(slot == 10, top == 1)

    def strip_sides(values):
        return (
            [back(v, 1, 8) for v in values],
            [ahead(v, 1, 8) for v in values],
            [back(v, 0) for v in values],
            [ahead(v, 0) for v in values],
            [back(v, 1) for v in values],
            [ahead(v, 1) for v in values],
        )

    def walled(values, factors):
        return [jnp.where(strip_wall, f * back(v, 1, 8), v) for v, f in zip(values, factors)]

    levels = []
    flows = []
    for line in strips:
        factor = ahead(line[0], 1, 16)
        flow = walled(line[3:], wall_signs)
        flows.append(flow)
        table = coefficients_of(flow, strip_sides(flow), *strip_scalars)
        start = walled(line[:3], [factor] * 3)
        one = rate(start, strip_sides(start), table)
        one = walled([a + b for a, b in zip(start, one)], [factor] * 3)
        two = rate(one, strip_sides(one), table)
        two = [0.75 * s + 0.25 * (a + b) for s, a, b in zip(start, one, two)]
        levels.append((start, one, two))

    def store_edges(low_values, high_values):
        for c in range(3):
            edge_low[pl.ds(sub * c, sub), :] = jnp.where(has_low, low_values[c], 0.0)
            edge_high[pl.ds(sub * c, sub), :] = jnp.where(has_high, high_values[c], 0.0)

    def axial(value, c, w, size):
        low = pltpu.roll(edge_low[pl.ds(sub * c, size), :], (128 - (8 * (w - 1) + 3)) % 128, 1)
        high = pltpu.roll(edge_high[pl.ds(sub * c, size), :], (127 - (8 * (w - 1) + 4)) % 128, 1)
        at = lane[:size]
        return jnp.where(at == 0, low, back(value, 1)), jnp.where(at == 127, high, ahead(value, 1))

    def pick(low, high):
        return jnp.where(low_half, np.float32(low), np.float32(high))

    def scalars(w):
        options = []
        for half in range(2):
            r = half * 8 + (w - 3) + 0.5
            options.append(
                (
                    -1.0 if r < 0 else 1.0,
                    diffuse * (r - 0.5) / r,
                    diffuse * (r + 0.5) / r,
                    advect / r,
                    1.0 / (r * r),
                    diffuse / abs(r),
                )
            )
        return [pick(a, b) for a, b in zip(*options)]

    def read(source, c, w, size=sub):
        return source[pl.ds(row_of(c, w), size), :]

    for c in range(6):
        last = read(cells, c, 10)
        factor = walls[...] if c < 3 else wall_signs[c - 3]
        cells[pl.ds(row_of(c, 11), sub), :] = jnp.where(low_half, read(cells, c, 11), factor * last)

    flow_low, flow_high = flows[0], flows[-1]

    def flow_table(w, size):
        speed, sides = [], [[], [], [], [], [], []]
        for c in range(3):
            value = read(cells, 3 + c, w)
            low = pltpu.roll(jnp.where(has_low, flow_low[c], 0.0), (128 - (8 * (w - 1) + 3)) % 128, 1)
            high = pltpu.roll(jnp.where(has_high, flow_high[c], 0.0), (127 - (8 * (w - 1) + 4)) % 128, 1)
            under = jnp.where(lane == 0, low, back(value, 1))
            over = jnp.where(lane == 127, high, ahead(value, 1))
            for side, part in zip(
                sides,
                (
                    read(cells, 3 + c, w - 1),
                    read(cells, 3 + c, w + 1),
                    back(value, 0),
                    ahead(value, 0),
                    under,
                    over,
                ),
            ):
                side.append(part[:size])
            speed.append(value[:size])
        return coefficients_of(speed, sides, *scalars(w))

    def field_rate(source, w, size):
        center, sides = [], [[], [], [], [], [], []]
        for c in range(3):
            value = read(source, c, w)
            under, over = axial(value[:size], c, w, size)
            for side, part in zip(
                sides,
                (
                    read(source, c, w - 1, size),
                    read(source, c, w + 1, size),
                    back(value, 0)[:size],
                    ahead(value, 0)[:size],
                    under,
                    over,
                ),
            ):
                side.append(part)
            center.append(value[:size])
        return center, rate(center, sides, flow_table(w, size))

    store_edges(levels[0][0], levels[-1][0])
    for w in range(1, 13):
        center, change = field_rate(cells, w, sub)
        for c in range(3):
            first[pl.ds(row_of(c, w), sub), :] = center[c] + change[c]
    for c in range(3):
        rows = pl.ds(8 * (12 + c), 8)
        low = pl.ds(row_of(c, 1), 8)
        first[low, :] = first[low, :] + jnp.where(low_half, signs[c] * behind[rows, :], 0.0)
        before = pl.ds(row_of(c, 3) + 14, 8, stride=sub)
        after = pl.ds(row_of(c, 3) + 9, 8, stride=sub)
        first[before, :] = first[before, :] + below[rows, :]
        first[after, :] = first[after, :] + above[rows, :]

    def close_wall(source):
        for c in range(3):
            source[pl.ds(row_of(c, 11), sub), :] = jnp.where(
                low_half, read(source, c, 11), walls[...] * read(source, c, 10)
            )

    close_wall(first)
    store_edges(levels[0][1], levels[-1][1])
    for w in range(2, 12):
        center, change = field_rate(first, w, sub)
        for c in range(3):
            second[pl.ds(row_of(c, w), sub), :] = 0.75 * read(cells, c, w) + 0.25 * (
                center[c] + change[c]
            )
    close_wall(second)
    store_edges(levels[0][2], levels[-1][2])
    count = basis.shape[0] // 192
    sums = [jnp.zeros((8, 128), jnp.float32) for _ in range(count + 1)]
    for w in range(3, 11):
        center, change = field_rate(second, w, 8)
        for c in range(3):
            rows = pl.ds(64 * c + 8 * (w - 3), 8)
            value = read(cells, c, w, 8) / 3.0 + (2.0 / 3.0) * (center[c] + change[c])
            advanced[rows, :] = value
            for m in range(count):
                sums[m] += basis[pl.ds(192 * m + 64 * c + 8 * (w - 3), 8), :] * value
            sums[count] += value * value
    spot = lanes(1)
    line = gram[...]
    for m in range(count + 1):
        total = jnp.sum(jnp.sum(sums[m], axis=0, keepdims=True), axis=1, keepdims=True)
        line = jnp.where(spot == m, total, line)
    for device in range(message.shape[0]):
        message[device] = line


def gram_place(m, n):
    return 16 + m * (m + 1) // 2 + n


def gram_kernel(basis, out):
    count = basis.shape[0] // 192
    spot = lanes(1)
    line = jnp.zeros((1, 128), jnp.float32)
    for m in range(count):
        sums = [jnp.zeros((8, 128), jnp.float32) for _ in range(m + 1)]
        for tile in range(24):
            value = basis[pl.ds(192 * m + 8 * tile, 8), :]
            for n in range(m + 1):
                sums[n] += value * basis[pl.ds(192 * n + 8 * tile, 8), :]
        for n in range(m + 1):
            total = jnp.sum(jnp.sum(sums[n], axis=0, keepdims=True), axis=1, keepdims=True)
            line = jnp.where(spot == gram_place(m, n), total, line)
    out[...] = line


def finish_kernel(cell_count, messages, advanced, basis, out, hessenberg):
    count = basis.shape[0] // 192
    total = messages[0]
    for device in range(1, messages.shape[0]):
        total = total + messages[device]

    def entry(index):
        return jnp.broadcast_to(total[:, index : index + 1], (8, 128))

    pending = [entry(m) for m in range(count)]
    energy = entry(count)
    weights = []
    for m in range(count):
        diagonal = entry(gram_place(m, m))
        weight = pending[m] / diagonal
        weights.append(weight)
        energy = energy - weight * (2.0 * pending[m] - weight * diagonal)
        for n in range(m + 1, count):
            pending[n] = pending[n] - weight * entry(gram_place(n, m))
    spread = jnp.sqrt(jnp.maximum(energy, 0.0) / cell_count + epsilon)
    scale = 1.0 / spread
    for tile in range(24):
        rows = pl.ds(8 * tile, 8)
        value = advanced[rows, :]
        for m in range(count):
            value = value - weights[m] * basis[pl.ds(192 * m + 8 * tile, 8), :]
        out[rows, :] = value * scale
    for m in range(count):
        hessenberg[m] = weights[m][0, 0]
    hessenberg[count] = spread[0, 0]


def shift(value, axis, step):
    count = lax.axis_size(axis)
    return lax.ppermute(value, axis, [(i, (i + step) % count) for i in range(count)])


def local(field, velocity, basis, wall_region, wall_conductance):
    loop = lax.axis_size("phi")
    ends = lax.axis_size("gz")
    halves = lax.axis_size("row")
    fold = loop == 4
    many = ends > 2
    vectors = basis.shape[0]
    field_rows = field.reshape(192, 128)
    flow_rows = velocity.reshape(192, 128)
    swap = [(0, 1), (1, 0)]
    far_field = lax.ppermute(field_rows, "row", swap)
    far_flow = lax.ppermute(flow_rows, "row", swap)
    (basis_rows,) = near(basis.reshape(vectors * 192, 128))
    inner, reflect, field_rows, flow_rows = pl.pallas_call(
        first_kernel,
        in_specs=[pl.BlockSpec(memory_space=pltpu.SMEM)] + vmem(3),
        out_specs=vmem(4),
        out_shape=[shape(8 * tiles, 128), shape(8, 128), shape(192, 128), shape(192, 128)],
    )(wall_conductance, wall_region, field_rows, flow_rows)
    half = loop // 2
    turned = []
    for p in range(loop):
        for r in range(halves):
            turned.append((p * halves + r, ((p + half) % loop if r == 0 else p) * halves + r))
    behind = lax.ppermute(inner, ("phi", "row"), turned)
    field_rows, flow_rows, far_field, far_flow, reflect = near(
        field_rows, flow_rows, far_field, far_flow, reflect
    )
    side = side_rows if fold else axis_row
    packed = pl.pallas_call(
        functools.partial(sides_kernel, fold),
        in_specs=vmem(5),
        out_specs=vmem(2 if fold else 4),
        out_shape=[shape(side, 128)] * 2 + ([] if fold else [shape(24, 128)] * 2),
    )(field_rows, flow_rows, far_field, far_flow, reflect)
    below = shift(packed[0], "phi", 1)
    above = shift(packed[1], "phi", -1)
    corners = []
    if not fold:
        corners = [shift(packed[2], "phi", half + 1), shift(packed[3], "phi", half - 1)]
    gram = pl.pallas_call(
        gram_kernel, in_specs=vmem(1), out_specs=vmem(1)[0], out_shape=shape(1, 128)
    )(basis_rows)
    window_shapes = [shape(6 * sub, 128), shape(6 * window * sub, 128)]
    strip, cells = pl.pallas_call(
        frame_kernel, in_specs=vmem(4), out_specs=vmem(2), out_shape=window_shapes
    )(field_rows, flow_rows, far_field, far_flow)
    received = near(
        *lax.optimization_barrier((below, above, behind, gram, strip, cells, *corners))
    )
    below, above, behind, gram, strip, cells = received[:6]
    walls, strip, cells = pl.pallas_call(
        functools.partial(window_kernel, fold),
        in_specs=vmem(6 + len(corners)),
        out_specs=vmem(3),
        out_shape=[shape(sub, 128)] + window_shapes,
        input_output_aliases={4: 1, 5: 2},
    )(below, above, behind, reflect, strip, cells, *received[6:])
    if many:
        up_pairs = [(i, i + 1) for i in range(ends - 1)]
        others = [
            lax.ppermute(strip, "gz", up_pairs),
            lax.ppermute(strip, "gz", [(b, a) for a, b in up_pairs]),
        ]
    else:
        others = [lax.ppermute(strip, "gz", swap)]
    walls, strip, cells, *others = near(walls, strip, cells, *others)
    axes = ("phi", "gz", "row")
    devices = lax.axis_size(axes)
    message, advanced = pl.pallas_call(
        functools.partial(stage_kernel, many),
        in_specs=vmem(8 + len(others)),
        out_specs=vmem(2),
        out_shape=[shape(devices, 1, 128), shape(192, 128)],
        scratch_shapes=[
            pltpu.VMEM((3 * window * sub, 128), jnp.float32),
            pltpu.VMEM((3 * window * sub, 128), jnp.float32),
            pltpu.VMEM((3 * sub, 128), jnp.float32),
            pltpu.VMEM((3 * sub, 128), jnp.float32),
        ],
    )(below, above, behind, walls, strip, *others, cells, basis_rows, gram)
    messages = lax.all_to_all(message, axes, 0, 0, tiled=True)
    messages, advanced = near(messages, advanced)
    out, hessenberg = pl.pallas_call(
        functools.partial(finish_kernel, float(field.size * devices)),
        in_specs=vmem(3),
        out_specs=vmem(1) + [pl.BlockSpec(memory_space=pltpu.SMEM)],
        out_shape=[
            jax.ShapeDtypeStruct((192, 128), jnp.float32),
            jax.ShapeDtypeStruct((vectors + 1,), jnp.float32),
        ],
    )(messages, advanced, basis_rows)
    return out.reshape(field.shape), hessenberg


def solution(mesh):
    return jax.shard_map(
        local,
        mesh=mesh,
        in_specs=(
            P("groups", "row", "phi", "gz"),
            P("groups", "row", "phi", "gz"),
            P("groups", None, "row", "phi", "gz"),
            P(("groups", "phi"), "gz"),
            P("groups"),
        ),
        out_specs=(P("groups", "row", "phi", "gz"), P("groups")),
        check_vma=False,
    )
```

```python
import functools

import jax
import jax.numpy as jnp
import numpy as np
from jax import lax
from jax.experimental import pallas as pl
from jax.experimental.pallas import tpu as pltpu
from jax.sharding import PartitionSpec as P

advect = 0.2
diffuse = 0.1
epsilon = 1e-06
signs = (-1.0, -1.0, 1.0)
wall_signs = (-1.0, 1.0, 1.0)

tiles = 15
wall_row = 8 * tiles
corner_row = wall_row + 8
axis_row = corner_row + 24
side_rows = axis_row + 24
window = 14
sub = 16


def row_of(component, w):
    return (component * window + w) * sub


def vmem(count):
    return [pl.BlockSpec(memory_space=pltpu.VMEM)] * count


def shape(*dims):
    return pltpu.VMEM(dims, jnp.float32)


def near(*values):
    return [pltpu.with_memory_space_constraint(value, pltpu.VMEM) for value in values]


def lanes(rows):
    return lax.broadcasted_iota(jnp.int32, (rows, 128), 1)


def layer(source, c, r):
    return source[pl.ds(c * 64 + r * 8, 8), :]


def inner_kernel(field, velocity, inner):
    middle = lax.axis_index("row").astype(jnp.float32) * 8.0 + 1.5
    pull = diffuse * (middle + 0.5) / jnp.full((8, 128), middle)
    carry = pull - advect * jnp.minimum(layer(velocity, 0, 1), 0.0)
    stretch = (0.5 * advect) * layer(field, 0, 1)
    for c in range(3):
        inner[pl.ds(8 * c, 8), :] = layer(field, c, 0)
        inner[pl.ds(8 * (3 + c), 8), :] = layer(velocity, c, 0)
        inner[pl.ds(8 * (6 + c), 8), :] = layer(field, c, 1)
        inner[pl.ds(8 * (9 + c), 8), :] = layer(velocity, c, 1)
        inner[pl.ds(8 * (12 + c), 8), :] = carry * layer(field, c, 2) + stretch * layer(
            velocity, c, 2
        )


def sides_kernel(
    fold, conductance, region, field, velocity, far_field, far_flow, up, down, reflect, *corners
):
    top = lax.axis_index("row")
    kinds = region[...]
    value = jnp.zeros(kinds.shape, jnp.float32)
    for kind in range(conductance.shape[0]):
        value = jnp.where(kinds == kind, conductance[kind], value)
    reflect[...] = 1.0 - 2.0 * value / (1.0 + value)

    def column(source, c, q):
        return source[pl.ds(c * 64 + q, 8, stride=8), :]

    def cell(source, r, q):
        return source[pl.ds(r * 8 + q, 3, stride=64), :]

    radius = lax.broadcasted_iota(jnp.int32, (8, 128), 0).astype(jnp.float32)
    turn = diffuse / (radius + (top.astype(jnp.float32) * 8.0 + 0.5))
    for out, (one, two, three), direction in ((up, (7, 6, 5), -1.0), (down, (0, 1, 2), 1.0)):
        for c in range(3):
            out[pl.ds(8 * c, 8), :] = column(field, c, one)
            out[pl.ds(8 * (3 + c), 8), :] = column(velocity, c, one)
            out[pl.ds(8 * (6 + c), 8), :] = column(field, c, two)
            out[pl.ds(8 * (9 + c), 8), :] = column(velocity, c, two)
        speed = column(velocity, 1, two)
        carry = diffuse + advect * jnp.maximum(-direction * speed, 0.0)
        stretch = (0.5 * advect * direction) * column(field, 1, two)
        far = [column(field, c, three) for c in range(3)]
        term = [carry * far[c] + stretch * column(velocity, c, three) for c in range(3)]
        term[0] = term[0] - (direction * turn) * far[1]
        term[1] = term[1] + (direction * turn) * far[0]
        for c in range(3):
            out[pl.ds(8 * (12 + c), 8), :] = term[c]
        out[pl.ds(wall_row, 1), :] = reflect[pl.ds(one, 1), :]
        out[pl.ds(wall_row + 1, 1), :] = reflect[pl.ds(two, 1), :]
        for place, (r, q) in enumerate(((0, one), (0, two), (1, one))):
            for part, source in enumerate((far_field, far_flow)):
                out[pl.ds(corner_row + 8 * place + 3 * part, 3), :] = jnp.where(
                    top == 0, cell(source, r, q), cell(source, 7 - r, q)
                )
    for side, (one, two) in ((0, (7, 6)), (1, (0, 1))):
        if fold:
            out, base = (down, up)[side], axis_row
        else:
            out, base = corners[side], 0
        for place, (r, q) in enumerate(((0, one), (0, two), (1, one))):
            out[pl.ds(base + 8 * place, 3), :] = cell(field, r, q)
            out[pl.ds(base + 8 * place + 3, 3), :] = cell(velocity, r, q)


def window_kernel(
    fold, field, velocity, far_field, far_flow, below, above, behind, reflect, *rest
):
    if fold:
        axis_low, axis_high, axis_base = above, below, axis_row
    else:
        axis_low, axis_high, axis_base = rest[0], rest[1], 0
    walls, strip, cells = rest[-3:]
    low_half = lax.axis_index("row") == 0
    nothing = jnp.zeros((8, 128), jnp.float32)
    for c in range(6):
        source, far = (field, far_field) if c < 3 else (velocity, far_flow)
        sign = signs[c % 3]
        for r in range(8):
            cells[pl.ds(row_of(c, r + 3), 8), :] = layer(source, c % 3, r)
        for w in range(window):
            cells[pl.ds(row_of(c, w) + 8, 8), :] = nothing
        for w in range(3):
            ghost = sign * behind[pl.ds(48 * (2 - w) + 8 * c, 8), :] if w > 0 else 0.0
            cells[pl.ds(row_of(c, w), 8), :] = jnp.where(low_half, ghost, layer(far, c % 3, 5 + w))
            cells[pl.ds(row_of(c, 11 + w), 8), :] = jnp.where(low_half, layer(far, c % 3, w), 0.0)
        for depth in range(2):
            place = pl.ds(48 * depth + 8 * c, 8)
            cells[pl.ds(row_of(c, 3) + 15 - depth, 8, stride=sub), :] = below[place, :]
            cells[pl.ds(row_of(c, 3) + 8 + depth, 8, stride=sub), :] = above[place, :]
    flip = lax.broadcasted_iota(jnp.int32, (6, 128), 0)
    flip = jnp.where((flip == 2) | (flip == 5), 1.0, -1.0)
    for place, (w, step) in enumerate(((2, 0), (2, 1), (1, 0))):
        for axis_source, source, q in ((axis_low, below, 15 - step), (axis_high, above, 8 + step)):
            ghost = flip * axis_source[pl.ds(axis_base + 8 * place, 6), :]
            other = source[pl.ds(corner_row + 8 * place, 6), :]
            low = jnp.where(low_half, ghost, other)
            high = jnp.where(low_half, other, 0.0)
            for c in range(6):
                cells[pl.ds(row_of(c, w) + q, 1), :] = low[c : c + 1]
                cells[pl.ds(row_of(c, 13 - w) + q, 1), :] = high[c : c + 1]
    walls[pl.ds(0, 8), :] = reflect[...]
    walls[pl.ds(8, 8), :] = nothing
    walls[pl.ds(8, 2), :] = above[pl.ds(wall_row, 2), :]
    walls[pl.ds(15, 1), :] = below[pl.ds(wall_row, 1), :]
    walls[pl.ds(14, 1), :] = below[pl.ds(wall_row + 1, 1), :]
    slot = lanes(sub) // 8
    for c in range(6):
        packed = jnp.where(slot == 12, pltpu.roll(walls[...], 100, 1), 0.0)
        for w in range(1, window - 1):
            row = cells[pl.ds(row_of(c, w), sub), :]
            packed = jnp.where(slot == w - 1, pltpu.roll(row, (8 * (w - 1) + 4) % 128, 1), packed)
        strip[pl.ds(sub * c, sub), :] = packed


def back(value, axis, step=1):
    return pltpu.roll(value, step, axis)


def ahead(value, axis, step=1):
    return pltpu.roll(value, value.shape[axis] - step, axis)


def rate(center, sides, coefficients):
    inward, outward, before, after, under, over = sides
    pull_in, pull_out, pull_before, pull_after, pull_under, pull_over, keep, mix, turn = coefficients
    result = []
    for c in range(3):
        value = (
            (pull_in * inward[c] + pull_out * outward[c])
            + (pull_before * before[c] + pull_after * after[c])
            + (pull_under * under[c] + pull_over * over[c])
            + keep * center[c]
        )
        for d in range(3):
            value = value + mix[c][d] * center[d]
        result.append(value)
    result[0] = result[0] - turn * (after[1] - before[1])
    result[1] = result[1] + turn * (after[0] - before[0])
    return result


def coefficients_of(speed, sides, sense, inner_pull, outer_pull, bend, inverse_square, turn):
    inward, outward, before, after, under, over = sides
    radial, around, axial = speed
    around_here = sense * around
    pulls = (
        inner_pull + advect * jnp.maximum(radial, 0.0),
        outer_pull - advect * jnp.minimum(radial, 0.0),
        diffuse + advect * jnp.maximum(around_here, 0.0),
        diffuse - advect * jnp.minimum(around_here, 0.0),
        diffuse + advect * jnp.maximum(axial, 0.0),
        diffuse - advect * jnp.minimum(axial, 0.0),
    )
    keep = -6.0 * diffuse - advect * (jnp.abs(radial) + jnp.abs(around) + jnp.abs(axial))
    half = 0.5 * advect
    mix = []
    for c in range(3):
        mix.append(
            [
                half * (outward[c] - inward[c]),
                (half * sense) * (after[c] - before[c]),
                half * (over[c] - under[c]),
            ]
        )
    mix[0][0] = mix[0][0] - diffuse * inverse_square
    mix[1][1] = mix[1][1] - diffuse * inverse_square + bend * radial
    mix[1][0] = mix[1][0] - bend * around
    return pulls + (keep, mix, turn)


def stage_kernel(many, below, above, behind, walls, strip, *rest):
    others = rest[: 2 if many else 1]
    cells, basis, gram, message, advanced, first, second, edge_low, edge_high = rest[len(others) :]
    has_high = lax.axis_index("gz") < lax.axis_size("gz") - 1
    inside = lanes(sub) % 8
    mine = [strip[pl.ds(sub * c, sub), :] for c in range(6)]
    if many:
        from_low = [others[0][pl.ds(sub * c, sub), :] for c in range(6)]
        from_high = [others[1][pl.ds(sub * c, sub), :] for c in range(6)]
        strips = [
            [jnp.where(inside < 4, b, a) for a, b in zip(mine, from_low)],
            [jnp.where(inside < 4, a, b) for a, b in zip(mine, from_high)],
        ]
    else:
        other = [others[0][pl.ds(sub * c, sub), :] for c in range(6)]
        strips = [[jnp.where((inside < 4) == has_high, a, b) for a, b in zip(mine, other)]]
    strips = [line + [ahead(line[0], 1, 16)] for line in strips]
    low_half = lax.axis_index("row") == 0
    ghosts = [jnp.where(low_half, signs[c] * layer(behind, 0, 12 + c), 0.0) for c in range(3)]
    lows = [layer(below, 0, 12 + c) for c in range(3)]
    highs = [layer(above, 0, 12 + c) for c in range(3)]
    march(
        strips, ghosts, lows, highs, walls, cells, basis, gram, message, advanced,
        first, second, edge_low, edge_high,
    )


def march(
    strips, ghosts, lows, highs, walls, cells, basis, gram, message, advanced,
    first, second, edge_low, edge_high,
):
    top = lax.axis_index("row")
    low_half = top == 0
    place = lax.axis_index("gz")
    has_low = place > 0
    has_high = place < lax.axis_size("gz") - 1
    lane = lanes(sub)
    slot = lane // 8

    number = (slot - 2).astype(jnp.float32) + top.astype(jnp.float32) * 8.0 + 0.5
    inverse = 1.0 / number
    strip_scalars = (
        jnp.where(number < 0.0, -1.0, 1.0),
        diffuse * (number - 0.5) * inverse,
        diffuse * (number + 0.5) * inverse,
        advect * inverse,
        inverse * inverse,
        diffuse * jnp.abs(inverse),
    )
    strip_wall = jnp.logical_and(slot == 10, top == 1)

    def strip_sides(values):
        return (
            [back(v, 1, 8) for v in values],
            [ahead(v, 1, 8) for v in values],
            [back(v, 0) for v in values],
            [ahead(v, 0) for v in values],
            [back(v, 1) for v in values],
            [ahead(v, 1) for v in values],
        )

    def walled(values, factors):
        return [jnp.where(strip_wall, f * back(v, 1, 8), v) for v, f in zip(values, factors)]

    levels = []
    flows = []
    for line in strips:
        factor = line[6]
        flow = walled(line[3:6], wall_signs)
        flows.append(flow)
        table = coefficients_of(flow, strip_sides(flow), *strip_scalars)
        start = walled(line[:3], [factor] * 3)
        one = rate(start, strip_sides(start), table)
        one = walled([a + b for a, b in zip(start, one)], [factor] * 3)
        two = rate(one, strip_sides(one), table)
        two = [0.75 * s + 0.25 * (a + b) for s, a, b in zip(start, one, two)]
        levels.append((start, one, two))

    def store_edges(low_values, high_values):
        for c in range(3):
            edge_low[pl.ds(sub * c, sub), :] = jnp.where(has_low, low_values[c], 0.0)
            edge_high[pl.ds(sub * c, sub), :] = jnp.where(has_high, high_values[c], 0.0)

    def axial(value, c, w, size):
        low = pltpu.roll(edge_low[pl.ds(sub * c, size), :], (128 - (8 * (w - 1) + 3)) % 128, 1)
        high = pltpu.roll(edge_high[pl.ds(sub * c, size), :], (127 - (8 * (w - 1) + 4)) % 128, 1)
        at = lane[:size]
        return jnp.where(at == 0, low, back(value, 1)), jnp.where(at == 127, high, ahead(value, 1))

    def pick(low, high):
        return jnp.where(low_half, np.float32(low), np.float32(high))

    def scalars(w):
        options = []
        for half in range(2):
            r = half * 8 + (w - 3) + 0.5
            options.append(
                (
                    -1.0 if r < 0 else 1.0,
                    diffuse * (r - 0.5) / r,
                    diffuse * (r + 0.5) / r,
                    advect / r,
                    1.0 / (r * r),
                    diffuse / abs(r),
                )
            )
        return [pick(a, b) for a, b in zip(*options)]

    def read(source, c, w, size=sub):
        return source[pl.ds(row_of(c, w), size), :]

    for c in range(6):
        last = read(cells, c, 10)
        factor = walls[...] if c < 3 else wall_signs[c - 3]
        cells[pl.ds(row_of(c, 11), sub), :] = jnp.where(low_half, read(cells, c, 11), factor * last)

    flow_low, flow_high = flows[0], flows[-1]

    def flow_table(w, size):
        speed, sides = [], [[], [], [], [], [], []]
        for c in range(3):
            value = read(cells, 3 + c, w)
            low = pltpu.roll(jnp.where(has_low, flow_low[c], 0.0), (128 - (8 * (w - 1) + 3)) % 128, 1)
            high = pltpu.roll(jnp.where(has_high, flow_high[c], 0.0), (127 - (8 * (w - 1) + 4)) % 128, 1)
            under = jnp.where(lane == 0, low, back(value, 1))
            over = jnp.where(lane == 127, high, ahead(value, 1))
            for side, part in zip(
                sides,
                (
                    read(cells, 3 + c, w - 1),
                    read(cells, 3 + c, w + 1),
                    back(value, 0),
                    ahead(value, 0),
                    under,
                    over,
                ),
            ):
                side.append(part[:size])
            speed.append(value[:size])
        return coefficients_of(speed, sides, *scalars(w))

    def field_rate(source, w, size):
        center, sides = [], [[], [], [], [], [], []]
        for c in range(3):
            value = read(source, c, w)
            under, over = axial(value[:size], c, w, size)
            for side, part in zip(
                sides,
                (
                    read(source, c, w - 1, size),
                    read(source, c, w + 1, size),
                    back(value, 0)[:size],
                    ahead(value, 0)[:size],
                    under,
                    over,
                ),
            ):
                side.append(part)
            center.append(value[:size])
        return center, rate(center, sides, flow_table(w, size))

    store_edges(levels[0][0], levels[-1][0])
    for w in range(1, 13):
        center, change = field_rate(cells, w, sub)
        for c in range(3):
            first[pl.ds(row_of(c, w), sub), :] = center[c] + change[c]
    for c in range(3):
        low = pl.ds(row_of(c, 1), 8)
        first[low, :] = first[low, :] + ghosts[c]
        before = pl.ds(row_of(c, 3) + 14, 8, stride=sub)
        after = pl.ds(row_of(c, 3) + 9, 8, stride=sub)
        first[before, :] = first[before, :] + lows[c]
        first[after, :] = first[after, :] + highs[c]

    def close_wall(source):
        for c in range(3):
            source[pl.ds(row_of(c, 11), sub), :] = jnp.where(
                low_half, read(source, c, 11), walls[...] * read(source, c, 10)
            )

    close_wall(first)
    store_edges(levels[0][1], levels[-1][1])
    for w in range(2, 12):
        center, change = field_rate(first, w, sub)
        for c in range(3):
            second[pl.ds(row_of(c, w), sub), :] = 0.75 * read(cells, c, w) + 0.25 * (
                center[c] + change[c]
            )
    close_wall(second)
    store_edges(levels[0][2], levels[-1][2])
    count = basis.shape[0] // 192
    sums = [jnp.zeros((8, 128), jnp.float32) for _ in range(count + 1)]
    for w in range(3, 11):
        center, change = field_rate(second, w, 8)
        for c in range(3):
            rows = pl.ds(64 * c + 8 * (w - 3), 8)
            value = read(cells, c, w, 8) / 3.0 + (2.0 / 3.0) * (center[c] + change[c])
            advanced[rows, :] = value
            for m in range(count):
                sums[m] += basis[pl.ds(192 * m + 64 * c + 8 * (w - 3), 8), :] * value
            sums[count] += value * value
    spot = lanes(1)
    line = gram[...]
    for m in range(count + 1):
        total = jnp.sum(jnp.sum(sums[m], axis=0, keepdims=True), axis=1, keepdims=True)
        line = jnp.where(spot == m, total, line)
    for device in range(message.shape[0]):
        message[device] = line


side_wall = 16 * tiles
side_strip = side_wall + 8
side_axis = side_strip + 16
side_length = side_axis + 24
diagonal_wall = 24
diagonal_length = 32
share_corner = 8 * tiles
share_rest = share_corner + 24
share_turn = share_rest + side_length - side_wall
share_diagonal = share_turn + 8 * tiles
share_length = share_diagonal + diagonal_length


def faces_up():
    return (lax.axis_index("phi") + lax.axis_index("row")) % 2 == 0


def load_kernel(conductance, region, field, velocity, reflect, field_copy, flow_copy):
    kinds = region[...]
    value = jnp.zeros(kinds.shape, jnp.float32)
    for kind in range(conductance.shape[0]):
        value = jnp.where(kinds == kind, conductance[kind], value)
    reflect[...] = 1.0 - 2.0 * value / (1.0 + value)
    field_copy[...] = field[...]
    flow_copy[...] = velocity[...]


def send_kernel(field, velocity, far_field, far_flow, reflect, side, turn, diagonal, strip):
    top = lax.axis_index("row")
    upper = faces_up()
    slot = lanes(8) // 8

    def facing(load, depth):
        return jnp.where(upper, load(8 - depth), load(depth - 1))

    def column(source, c, depth):
        return facing(lambda q: source[pl.ds(c * 64 + q, 8, stride=8), :], depth)

    direction = jnp.where(upper, -1.0, 1.0)
    index = lax.broadcasted_iota(jnp.int32, (8, 128), 0).astype(jnp.float32)
    for source, flow, half in ((field, velocity, top), (far_field, far_flow, 1 - top)):
        base = half * (8 * tiles)

        def put(tile, value):
            side[pl.ds(pl.multiple_of(base + 8 * tile, 8), 8), :] = value

        bend = (diffuse * direction) / (index + (half.astype(jnp.float32) * 8.0 + 0.5))
        near_two = [column(source, c, 2) for c in range(3)]
        flow_two = [column(flow, c, 2) for c in range(3)]
        distant = [column(source, c, 3) for c in range(3)]
        carry = diffuse + advect * jnp.maximum(-direction * flow_two[1], 0.0)
        stretch = (0.5 * advect * direction) * near_two[1]
        term = [carry * distant[c] + stretch * column(flow, c, 3) for c in range(3)]
        term[0] = term[0] - bend * distant[1]
        term[1] = term[1] + bend * distant[0]
        for c in range(3):
            put(c, column(source, c, 1))
            put(3 + c, column(flow, c, 1))
            put(6 + c, near_two[c])
            put(9 + c, flow_two[c])
            put(12 + c, term[c])
    for depth in (1, 2):
        wall = facing(lambda q: reflect[pl.ds(q, 1), :], depth)
        side[pl.ds(side_wall + depth - 1, 1), :] = wall
        diagonal[pl.ds(diagonal_wall + depth - 1, 1), :] = wall

    for c in range(6):
        own, far = (field, far_field) if c < 3 else (velocity, far_flow)
        parts = []
        for source in (own, far):
            part = jnp.zeros((8, 128), jnp.float32)
            for r in range(8):
                part = jnp.where(
                    slot == r, pltpu.roll(layer(source, c % 3, r), (8 * r + 4) % 128, 1), part
                )
            parts.append(part)
        low = jnp.where(top == 0, parts[0], parts[1])
        high = jnp.where(top == 0, parts[1], parts[0])
        strip[pl.ds(8 * c, 8), :] = jnp.where(slot < 8, low, pltpu.roll(high, 64, 1))
    for depth in (1, 2):
        edge = facing(lambda q: strip[pl.ds(q, 6, stride=8), :], depth)
        side[pl.ds(side_strip + 8 * (depth - 1), 6), :] = edge
        diagonal[pl.ds(8 * (depth - 1), 6), :] = edge
    diagonal[pl.ds(16, 6), :] = jnp.where(
        upper, strip[pl.ds(0, 6, stride=8), :], strip[pl.ds(7, 6, stride=8), :]
    )

    def inner_cell(own, far, start, count, step):
        rows = pl.ds(start, count, stride=step)
        return jnp.where(top == 0, own[rows, :], far[rows, :])

    for place, (r, depth) in enumerate(((0, 1), (0, 2), (1, 1))):
        for part, (own, far) in enumerate(((field, far_field), (velocity, far_flow))):
            side[pl.ds(side_axis + 8 * place + 3 * part, 3), :] = jnp.where(
                upper,
                inner_cell(own, far, r * 8 + depth - 1, 3, 64),
                inner_cell(own, far, r * 8 + 8 - depth, 3, 64),
            )
    carry = (diffuse * 2.0 / 1.5) - advect * jnp.minimum(layer(far_flow, 0, 1), 0.0)
    stretch = (0.5 * advect) * layer(far_field, 0, 1)
    content = []
    for r in range(2):
        content += [layer(far_field, c, r) for c in range(3)]
        content += [layer(far_flow, c, r) for c in range(3)]
    content += [
        carry * layer(far_field, c, 2) + stretch * layer(far_flow, c, 2) for c in range(3)
    ]
    for tile in range(tiles):
        value = content[tile]
        if tile < 6:
            value = jnp.where(top == 0, strip[pl.ds(8 * tile, 8), :], value)
        elif tile == 6:
            value = jnp.where(top == 0, reflect[...], value)
        turn[pl.ds(8 * tile, 8), :] = value


def other_corner(side, first, step):
    top = lax.axis_index("row")
    low = side[pl.ds(8 * tiles + first + step, 6, stride=8), :]
    high = side[pl.ds(first + 7 - step, 6, stride=8), :]
    return jnp.where(top == 0, low, high)


def share_kernel(side, turn, diagonal, out):
    top = lax.axis_index("row")
    half = pl.multiple_of((1 - top) * (8 * tiles), 8)
    out[pl.ds(0, 8 * tiles), :] = side[pl.ds(half, 8 * tiles), :]
    for place, (first, step) in enumerate(((0, 0), (48, 0), (0, 1))):
        low = side[pl.ds(first + 7 - step, 6, stride=8), :]
        high = side[pl.ds(8 * tiles + first + step, 6, stride=8), :]
        out[pl.ds(share_corner + 8 * place, 6), :] = jnp.where(top == 0, low, high)
    out[pl.ds(share_rest, side_length - side_wall), :] = side[
        pl.ds(side_wall, side_length - side_wall), :
    ]
    out[pl.ds(share_turn, 8 * tiles), :] = turn[...]
    out[pl.ds(share_diagonal, diagonal_length), :] = diagonal[...]


def compact_kernel(
    field, velocity, far_field, far_flow, reflect, strip, side, turn, diagonal, opposite, shared,
    basis, gram, message, advanced, cells, walls, line, first, second, edge_low, edge_high,
):
    top = lax.axis_index("row")
    low_half = top == 0
    upper = faces_up()
    mine_low = lax.axis_index("gz") == 0

    def both(own, other):
        return jnp.where(upper, other, own), jnp.where(upper, own, other)

    own_half = pl.multiple_of(top * (8 * tiles), 8)

    def tile_pair(tile):
        return both(
            side[pl.ds(pl.multiple_of(own_half + 8 * tile, 8), 8), :], shared[pl.ds(8 * tile, 8), :]
        )

    def rest_pair(start, count):
        return both(
            side[pl.ds(start, count), :], shared[pl.ds(share_rest + start - side_wall, count), :]
        )

    def diagonal_pair(start, count):
        return both(
            diagonal[pl.ds(start, count), :], shared[pl.ds(share_diagonal + start, count), :]
        )

    behind = [shared[pl.ds(share_turn + 8 * tile, 8), :] for tile in range(tiles)]
    nothing = jnp.zeros((8, 128), jnp.float32)
    for c in range(6):
        source, far = (field, far_field) if c < 3 else (velocity, far_flow)
        sign = signs[c % 3]
        for r in range(8):
            cells[pl.ds(row_of(c, r + 3), 8), :] = layer(source, c % 3, r)
        for w in range(window):
            cells[pl.ds(row_of(c, w) + 8, 8), :] = nothing
        for w in range(3):
            ghost = sign * behind[6 * (2 - w) + c] if w > 0 else 0.0
            cells[pl.ds(row_of(c, w), 8), :] = jnp.where(low_half, ghost, layer(far, c % 3, 5 + w))
            cells[pl.ds(row_of(c, 11 + w), 8), :] = jnp.where(low_half, layer(far, c % 3, w), 0.0)
        for depth in range(2):
            below, above = tile_pair(6 * depth + c)
            cells[pl.ds(row_of(c, 3) + 15 - depth, 8, stride=sub), :] = below
            cells[pl.ds(row_of(c, 3) + 8 + depth, 8, stride=sub), :] = above
    flip = lax.broadcasted_iota(jnp.int32, (6, 128), 0)
    flip = jnp.where((flip == 2) | (flip == 5), 1.0, -1.0)
    for place, (w, first_row, step, depth) in enumerate(((2, 0, 0, 0), (2, 48, 0, 1), (1, 0, 1, 0))):
        axis_high, axis_low = rest_pair(side_axis + 8 * place, 6)
        below, above = both(
            other_corner(side, first_row, step), shared[pl.ds(share_corner + 8 * place, 6), :]
        )
        for axis_part, other, q in ((axis_low, below, 15 - depth), (axis_high, above, 8 + depth)):
            low = pl.ds(row_of(0, w) + q, 6, stride=window * sub)
            high = pl.ds(row_of(0, 13 - w) + q, 6, stride=window * sub)
            cells[low, :] = jnp.where(low_half, flip * axis_part, other)
            cells[high, :] = jnp.where(low_half, other, 0.0)

    slot, inside = lanes(sub) // 8, lanes(sub) % 8
    axial_turn = [
        jnp.where(
            low_half, turn[pl.ds(8 * tile, 8), :], shared[pl.ds(share_turn + 8 * tile, 8), :]
        )
        for tile in range(7)
    ]
    own_side = (inside < 4) == mine_low

    def merge(own, other):
        return jnp.where(own_side[: own.shape[0]], own, other)

    for part, (tile, pair) in enumerate(
        ((reflect[...], rest_pair(side_wall, 2)), (axial_turn[6], diagonal_pair(diagonal_wall, 2)))
    ):
        below, above = pair
        base = sub * part
        walls[pl.ds(base, 8), :] = tile
        walls[pl.ds(base + 8, 8), :] = nothing
        walls[pl.ds(base + 8, 2), :] = above
        walls[pl.ds(base + 15, 1), :] = below[0:1]
        walls[pl.ds(base + 14, 1), :] = below[1:2]
    factor = merge(
        pltpu.roll(walls[pl.ds(0, sub), :], 84, 1), pltpu.roll(walls[pl.ds(sub, sub), :], 84, 1)
    )

    for c in range(6):
        own = strip[pl.ds(8 * c, 8), :]
        line[pl.ds(sub * c, 8), :] = merge(own, axial_turn[c])
        line[pl.ds(sub * c + 8, 8), :] = nothing
    for depth in (1, 2):
        below, above = rest_pair(side_strip + 8 * (depth - 1), 6)
        beyond_below, beyond_above = diagonal_pair(8 * (depth - 1), 6)
        line[pl.ds(16 - depth, 6, stride=sub), :] = merge(below, beyond_below)
        line[pl.ds(7 + depth, 6, stride=sub), :] = merge(above, beyond_above)
    axis_high, axis_low = diagonal_pair(16, 6)
    combined = []
    for c in range(6):
        value = line[pl.ds(sub * c, sub), :]
        combined.append(jnp.where(low_half, pltpu.roll(value, 16, 1), pltpu.roll(value, 80, 1)))
    for c in range(6):
        sign = signs[c % 3]
        across = opposite[pl.ds(8 * c, 8), :]
        own = jnp.where(
            slot[:8] == 1,
            pltpu.roll(behind[c], 12, 1),
            pltpu.roll(behind[6 + c], 4, 1),
        )
        other = jnp.where(slot[:8] == 1, pltpu.roll(across, 8, 1), pltpu.roll(across, 120, 1))
        line[pl.ds(sub * c, 8), :] = sign * merge(own, other)
        line[pl.ds(sub * c + 8, 8), :] = nothing
        line[pl.ds(sub * c + 8, 1), :] = sign * pltpu.roll(axis_high, 8, 1)[c : c + 1]
        line[pl.ds(sub * c + 15, 1), :] = sign * pltpu.roll(axis_low, 8, 1)[c : c + 1]
        ghost = line[pl.ds(sub * c, sub), :]
        combined[c] = jnp.where(jnp.logical_and(slot < 2, low_half), ghost, combined[c])
    combined.append(factor)
    ghosts = [jnp.where(low_half, signs[c] * behind[12 + c], 0.0) for c in range(3)]
    lows, highs = zip(*[tile_pair(12 + c) for c in range(3)])
    march(
        [combined], ghosts, lows, highs, walls.at[pl.ds(0, sub), :], cells, basis, gram, message,
        advanced, first, second, edge_low, edge_high,
    )


def gram_place(m, n):
    return 16 + m * (m + 1) // 2 + n


def gram_kernel(basis, out):
    count = basis.shape[0] // 192
    spot = lanes(1)
    line = jnp.zeros((1, 128), jnp.float32)
    for m in range(count):
        sums = [jnp.zeros((8, 128), jnp.float32) for _ in range(m + 1)]
        for tile in range(24):
            value = basis[pl.ds(192 * m + 8 * tile, 8), :]
            for n in range(m + 1):
                sums[n] += value * basis[pl.ds(192 * n + 8 * tile, 8), :]
        for n in range(m + 1):
            total = jnp.sum(jnp.sum(sums[n], axis=0, keepdims=True), axis=1, keepdims=True)
            line = jnp.where(spot == gram_place(m, n), total, line)
    out[...] = line


def finish_kernel(cell_count, messages, advanced, basis, out, hessenberg):
    count = basis.shape[0] // 192
    total = messages[0]
    for device in range(1, messages.shape[0]):
        total = total + messages[device]

    def entry(index):
        return jnp.broadcast_to(total[:, index : index + 1], (8, 128))

    pending = [entry(m) for m in range(count)]
    energy = entry(count)
    weights = []
    for m in range(count):
        diagonal = entry(gram_place(m, m))
        weight = pending[m] / diagonal
        weights.append(weight)
        energy = energy - weight * (2.0 * pending[m] - weight * diagonal)
        for n in range(m + 1, count):
            pending[n] = pending[n] - weight * entry(gram_place(n, m))
    spread = jnp.sqrt(jnp.maximum(energy, 0.0) / cell_count + epsilon)
    scale = 1.0 / spread
    for tile in range(24):
        rows = pl.ds(8 * tile, 8)
        value = advanced[rows, :]
        for m in range(count):
            value = value - weights[m] * basis[pl.ds(192 * m + 8 * tile, 8), :]
        out[rows, :] = value * scale
    for m in range(count):
        hessenberg[m] = weights[m][0, 0]
    hessenberg[count] = spread[0, 0]


def shift(value, axis, step):
    count = lax.axis_size(axis)
    return lax.ppermute(value, axis, [(i, (i + step) % count) for i in range(count)])


def march_scratch():
    return [
        shape(3 * window * sub, 128),
        shape(3 * window * sub, 128),
        shape(3 * sub, 128),
        shape(3 * sub, 128),
    ]


def general_plan(field, velocity, basis, wall_region, wall_conductance):
    loop = lax.axis_size("phi")
    ends = lax.axis_size("gz")
    halves = lax.axis_size("row")
    fold = loop == 4
    many = ends > 2
    vectors = basis.shape[0]
    field_rows = field.reshape(192, 128)
    flow_rows = velocity.reshape(192, 128)
    swap = [(0, 1), (1, 0)]
    far_field = lax.ppermute(field_rows, "row", swap)
    far_flow = lax.ppermute(flow_rows, "row", swap)
    field_rows, flow_rows, basis_rows = near(
        field_rows, flow_rows, basis.reshape(vectors * 192, 128)
    )
    inner = pl.pallas_call(
        inner_kernel, in_specs=vmem(2), out_specs=vmem(1)[0], out_shape=shape(8 * tiles, 128)
    )(field_rows, flow_rows)
    half = loop // 2
    turned = []
    for p in range(loop):
        for r in range(halves):
            turned.append((p * halves + r, ((p + half) % loop if r == 0 else p) * halves + r))
    behind = lax.ppermute(inner, ("phi", "row"), turned)
    far_field, far_flow = near(far_field, far_flow)
    side = side_rows if fold else axis_row
    packed = pl.pallas_call(
        functools.partial(sides_kernel, fold),
        in_specs=[pl.BlockSpec(memory_space=pltpu.SMEM)] + vmem(5),
        out_specs=vmem(3 if fold else 5),
        out_shape=[shape(side, 128), shape(side, 128), shape(8, 128)]
        + ([] if fold else [shape(24, 128)] * 2),
    )(wall_conductance, wall_region, field_rows, flow_rows, far_field, far_flow)
    up, down, reflect = packed[:3]
    below = shift(up, "phi", 1)
    above = shift(down, "phi", -1)
    corners = []
    if not fold:
        corners = [shift(packed[3], "phi", half + 1), shift(packed[4], "phi", half - 1)]
    gram = pl.pallas_call(
        gram_kernel, in_specs=vmem(1), out_specs=vmem(1)[0], out_shape=shape(1, 128)
    )(basis_rows)
    below, above, behind, gram, *corners = lax.optimization_barrier(
        (below, above, behind, gram, *corners)
    )
    below, above, behind, gram, *corners = near(below, above, behind, gram, *corners)
    walls, strip, cells = pl.pallas_call(
        functools.partial(window_kernel, fold),
        in_specs=vmem(8 + len(corners)),
        out_specs=vmem(3),
        out_shape=[shape(sub, 128), shape(6 * sub, 128), shape(6 * window * sub, 128)],
    )(field_rows, flow_rows, far_field, far_flow, below, above, behind, reflect, *corners)
    if many:
        up_pairs = [(i, i + 1) for i in range(ends - 1)]
        others = [
            lax.ppermute(strip, "gz", up_pairs),
            lax.ppermute(strip, "gz", [(b, a) for a, b in up_pairs]),
        ]
    else:
        others = [lax.ppermute(strip, "gz", swap)]
    walls, strip, cells, *others = near(walls, strip, cells, *others)
    devices = lax.axis_size(("phi", "gz", "row"))
    return pl.pallas_call(
        functools.partial(stage_kernel, many),
        in_specs=vmem(8 + len(others)),
        out_specs=vmem(2),
        out_shape=[shape(devices, 1, 128), shape(192, 128)],
        scratch_shapes=march_scratch(),
    )(below, above, behind, walls, strip, *others, cells, basis_rows, gram)


def compact_plan(field, velocity, basis, wall_region, wall_conductance):
    vectors = basis.shape[0]
    field_rows = field.reshape(192, 128)
    flow_rows = velocity.reshape(192, 128)
    axes = ("phi", "gz", "row")
    devices = lax.axis_size(axes)

    def exchange(value, partner):
        pairs = []
        for p in range(4):
            for g in range(2):
                for r in range(2):
                    q, h = partner(p, g, r)
                    pairs.append(((p * 2 + g) * 2 + r, (q % 4 * 2 + h) * 2 + r))
        return lax.ppermute(value, axes, pairs)

    def beside(p, r):
        return p + 1 if (p + r) % 2 == 0 else p - 1

    swap = [(0, 1), (1, 0)]
    far_field = lax.ppermute(field_rows, "row", swap)
    far_flow = lax.ppermute(flow_rows, "row", swap)
    reflect, field_rows, flow_rows = pl.pallas_call(
        load_kernel,
        in_specs=[pl.BlockSpec(memory_space=pltpu.SMEM)] + vmem(3),
        out_specs=vmem(3),
        out_shape=[shape(8, 128), shape(192, 128), shape(192, 128)],
    )(wall_conductance, wall_region, field_rows, flow_rows)
    blocks = near(field_rows, flow_rows, far_field, far_flow, reflect)
    side, turn, diagonal, strip = pl.pallas_call(
        send_kernel,
        in_specs=vmem(5),
        out_specs=vmem(4),
        out_shape=[
            shape(side_length, 128),
            shape(8 * tiles, 128),
            shape(diagonal_length, 128),
            shape(48, 128),
        ],
    )(*blocks)
    opposite = exchange(strip, lambda p, g, r: (p + 2, 1 - g))
    turn = exchange(turn, lambda p, g, r: (p, 1 - g) if r == 0 else (p + 2, g))
    diagonal = exchange(diagonal, lambda p, g, r: (beside(p, r), 1 - g))
    side = exchange(side, lambda p, g, r: (beside(p, r), g))
    (basis_rows,) = near(basis.reshape(vectors * 192, 128))
    gram = pl.pallas_call(
        gram_kernel, in_specs=vmem(1), out_specs=vmem(1)[0], out_shape=shape(1, 128)
    )(basis_rows)
    side, turn, diagonal, opposite, gram = near(
        *lax.optimization_barrier((side, turn, diagonal, opposite, gram))
    )
    share = pl.pallas_call(
        share_kernel, in_specs=vmem(3), out_specs=vmem(1)[0], out_shape=shape(share_length, 128)
    )(side, turn, diagonal)
    shared = lax.ppermute(share, "row", swap)
    strip, shared = near(strip, shared)
    return pl.pallas_call(
        compact_kernel,
        in_specs=vmem(13),
        out_specs=vmem(2),
        out_shape=[shape(devices, 1, 128), shape(192, 128)],
        scratch_shapes=[
            shape(6 * window * sub, 128),
            shape(2 * sub, 128),
            shape(6 * sub, 128),
        ]
        + march_scratch(),
    )(*blocks, strip, side, turn, diagonal, opposite, shared, basis_rows, gram)


def local(field, velocity, basis, wall_region, wall_conductance):
    axes = ("phi", "gz", "row")
    vectors = basis.shape[0]
    devices = lax.axis_size(axes)
    compact = tuple(lax.axis_size(axis) for axis in axes) == (4, 2, 2)
    plan = compact_plan if compact else general_plan
    message, advanced = plan(field, velocity, basis, wall_region, wall_conductance)
    (basis_rows,) = near(basis.reshape(vectors * 192, 128))
    messages = lax.all_to_all(message, axes, 0, 0, tiled=True)
    messages, advanced = near(messages, advanced)
    out, hessenberg = pl.pallas_call(
        functools.partial(finish_kernel, float(field.size * devices)),
        in_specs=vmem(3),
        out_specs=vmem(1) + [pl.BlockSpec(memory_space=pltpu.SMEM)],
        out_shape=[
            jax.ShapeDtypeStruct((192, 128), jnp.float32),
            jax.ShapeDtypeStruct((vectors + 1,), jnp.float32),
        ],
    )(messages, advanced, basis_rows)
    return out.reshape(field.shape), hessenberg


def solution(mesh):
    return jax.shard_map(
        local,
        mesh=mesh,
        in_specs=(
            P("groups", "row", "phi", "gz"),
            P("groups", "row", "phi", "gz"),
            P("groups", None, "row", "phi", "gz"),
            P(("groups", "phi"), "gz"),
            P("groups"),
        ),
        out_specs=(P("groups", "row", "phi", "gz"), P("groups")),
        check_vma=False,
    )
```

```python
import functools

import jax
import jax.numpy as jnp
import numpy as np
from jax import lax
from jax.experimental import pallas as pl
from jax.experimental.pallas import tpu as pltpu
from jax.sharding import PartitionSpec as P

advect = 0.2
diffuse = 0.1
epsilon = 1e-06
signs = (-1.0, -1.0, 1.0)
wall_signs = (-1.0, 1.0, 1.0)

tiles = 15
wall_row = 8 * tiles
corner_row = wall_row + 8
axis_row = corner_row + 24
side_rows = axis_row + 24
window = 14
sub = 16
kinds_of_coefficient = 15


def row_of(component, w):
    return (component * window + w) * sub


def vmem(count):
    return [pl.BlockSpec(memory_space=pltpu.VMEM)] * count


def shape(*dims):
    return pltpu.VMEM(dims, jnp.float32)


def near(*values):
    return [pltpu.with_memory_space_constraint(value, pltpu.VMEM) for value in values]


def lanes(rows):
    return lax.broadcasted_iota(jnp.int32, (rows, 128), 1)


def layer(source, c, r):
    return source[pl.ds(c * 64 + r * 8, 8), :]


def inner_kernel(field, velocity, inner):
    middle = lax.axis_index("row").astype(jnp.float32) * 8.0 + 1.5
    pull = diffuse * (middle + 0.5) / jnp.full((8, 128), middle)
    carry = pull - advect * jnp.minimum(layer(velocity, 0, 1), 0.0)
    stretch = (0.5 * advect) * layer(field, 0, 1)
    for c in range(3):
        inner[pl.ds(8 * c, 8), :] = layer(field, c, 0)
        inner[pl.ds(8 * (3 + c), 8), :] = layer(velocity, c, 0)
        inner[pl.ds(8 * (6 + c), 8), :] = layer(field, c, 1)
        inner[pl.ds(8 * (9 + c), 8), :] = layer(velocity, c, 1)
        inner[pl.ds(8 * (12 + c), 8), :] = carry * layer(field, c, 2) + stretch * layer(
            velocity, c, 2
        )


def sides_kernel(
    fold, conductance, region, field, velocity, far_field, far_flow, up, down, reflect, *corners
):
    top = lax.axis_index("row")
    kinds = region[...]
    value = jnp.zeros(kinds.shape, jnp.float32)
    for kind in range(conductance.shape[0]):
        value = jnp.where(kinds == kind, conductance[kind], value)
    reflect[...] = 1.0 - 2.0 * value / (1.0 + value)

    def column(source, c, q):
        return source[pl.ds(c * 64 + q, 8, stride=8), :]

    def cell(source, r, q):
        return source[pl.ds(r * 8 + q, 3, stride=64), :]

    radius = lax.broadcasted_iota(jnp.int32, (8, 128), 0).astype(jnp.float32)
    turn = diffuse / (radius + (top.astype(jnp.float32) * 8.0 + 0.5))
    for out, (one, two, three), direction in ((up, (7, 6, 5), -1.0), (down, (0, 1, 2), 1.0)):
        for c in range(3):
            out[pl.ds(8 * c, 8), :] = column(field, c, one)
            out[pl.ds(8 * (3 + c), 8), :] = column(velocity, c, one)
            out[pl.ds(8 * (6 + c), 8), :] = column(field, c, two)
            out[pl.ds(8 * (9 + c), 8), :] = column(velocity, c, two)
        speed = column(velocity, 1, two)
        carry = diffuse + advect * jnp.maximum(-direction * speed, 0.0)
        stretch = (0.5 * advect * direction) * column(field, 1, two)
        far = [column(field, c, three) for c in range(3)]
        term = [carry * far[c] + stretch * column(velocity, c, three) for c in range(3)]
        term[0] = term[0] - (direction * turn) * far[1]
        term[1] = term[1] + (direction * turn) * far[0]
        for c in range(3):
            out[pl.ds(8 * (12 + c), 8), :] = term[c]
        out[pl.ds(wall_row, 1), :] = reflect[pl.ds(one, 1), :]
        out[pl.ds(wall_row + 1, 1), :] = reflect[pl.ds(two, 1), :]
        for place, (r, q) in enumerate(((0, one), (0, two), (1, one))):
            for part, source in enumerate((far_field, far_flow)):
                out[pl.ds(corner_row + 8 * place + 3 * part, 3), :] = jnp.where(
                    top == 0, cell(source, r, q), cell(source, 7 - r, q)
                )
    for side, (one, two) in ((0, (7, 6)), (1, (0, 1))):
        if fold:
            out, base = (down, up)[side], axis_row
        else:
            out, base = corners[side], 0
        for place, (r, q) in enumerate(((0, one), (0, two), (1, one))):
            out[pl.ds(base + 8 * place, 3), :] = cell(field, r, q)
            out[pl.ds(base + 8 * place + 3, 3), :] = cell(velocity, r, q)


def window_kernel(
    fold, field, velocity, far_field, far_flow, below, above, behind, reflect, *rest
):
    if fold:
        axis_low, axis_high, axis_base = above, below, axis_row
    else:
        axis_low, axis_high, axis_base = rest[0], rest[1], 0
    walls, strip, cells = rest[-3:]
    low_half = lax.axis_index("row") == 0
    nothing = jnp.zeros((8, 128), jnp.float32)
    for c in range(6):
        source, far = (field, far_field) if c < 3 else (velocity, far_flow)
        sign = signs[c % 3]
        for r in range(8):
            cells[pl.ds(row_of(c, r + 3), 8), :] = layer(source, c % 3, r)
        for w in range(window):
            cells[pl.ds(row_of(c, w) + 8, 8), :] = nothing
        for w in range(3):
            ghost = sign * behind[pl.ds(48 * (2 - w) + 8 * c, 8), :] if w > 0 else 0.0
            cells[pl.ds(row_of(c, w), 8), :] = jnp.where(low_half, ghost, layer(far, c % 3, 5 + w))
            cells[pl.ds(row_of(c, 11 + w), 8), :] = jnp.where(low_half, layer(far, c % 3, w), 0.0)
        for depth in range(2):
            place = pl.ds(48 * depth + 8 * c, 8)
            cells[pl.ds(row_of(c, 3) + 15 - depth, 8, stride=sub), :] = below[place, :]
            cells[pl.ds(row_of(c, 3) + 8 + depth, 8, stride=sub), :] = above[place, :]
    flip = lax.broadcasted_iota(jnp.int32, (6, 128), 0)
    flip = jnp.where((flip == 2) | (flip == 5), 1.0, -1.0)
    for place, (w, step) in enumerate(((2, 0), (2, 1), (1, 0))):
        for axis_source, source, q in ((axis_low, below, 15 - step), (axis_high, above, 8 + step)):
            ghost = flip * axis_source[pl.ds(axis_base + 8 * place, 6), :]
            other = source[pl.ds(corner_row + 8 * place, 6), :]
            low = jnp.where(low_half, ghost, other)
            high = jnp.where(low_half, other, 0.0)
            for c in range(6):
                cells[pl.ds(row_of(c, w) + q, 1), :] = low[c : c + 1]
                cells[pl.ds(row_of(c, 13 - w) + q, 1), :] = high[c : c + 1]
    walls[pl.ds(0, 8), :] = reflect[...]
    walls[pl.ds(8, 8), :] = nothing
    walls[pl.ds(8, 2), :] = above[pl.ds(wall_row, 2), :]
    walls[pl.ds(15, 1), :] = below[pl.ds(wall_row, 1), :]
    walls[pl.ds(14, 1), :] = below[pl.ds(wall_row + 1, 1), :]
    slot = lanes(sub) // 8
    for c in range(6):
        packed = jnp.where(slot == 12, pltpu.roll(walls[...], 100, 1), 0.0)
        for w in range(1, window - 1):
            row = cells[pl.ds(row_of(c, w), sub), :]
            packed = jnp.where(slot == w - 1, pltpu.roll(row, (8 * (w - 1) + 4) % 128, 1), packed)
        strip[pl.ds(sub * c, sub), :] = packed


def back(value, axis, step=1):
    return pltpu.roll(value, step, axis)


def ahead(value, axis, step=1):
    return pltpu.roll(value, value.shape[axis] - step, axis)


def rate(center, sides, coefficients):
    inward, outward, before, after, under, over = sides
    pull_in, pull_out, pull_before, pull_after, pull_under, pull_over, mix, turn = coefficients
    result = []
    for c in range(3):
        value = (
            (pull_in * inward[c] + pull_out * outward[c])
            + (pull_before * before[c] + pull_after * after[c])
            + (pull_under * under[c] + pull_over * over[c])
        )
        for d in range(3):
            value = value + mix[c][d] * center[d]
        result.append(value)
    result[0] = result[0] - turn * (after[1] - before[1])
    result[1] = result[1] + turn * (after[0] - before[0])
    return result


def coefficients_of(speed, sides, sense, inner_pull, outer_pull, bend, inverse_square, turn):
    inward, outward, before, after, under, over = sides
    radial, around, axial = speed
    around_here = sense * around
    pulls = (
        inner_pull + advect * jnp.maximum(radial, 0.0),
        outer_pull - advect * jnp.minimum(radial, 0.0),
        diffuse + advect * jnp.maximum(around_here, 0.0),
        diffuse - advect * jnp.minimum(around_here, 0.0),
        diffuse + advect * jnp.maximum(axial, 0.0),
        diffuse - advect * jnp.minimum(axial, 0.0),
    )
    keep = -6.0 * diffuse - advect * (jnp.abs(radial) + jnp.abs(around) + jnp.abs(axial))
    half = 0.5 * advect
    mix = []
    for c in range(3):
        mix.append(
            [
                half * (outward[c] - inward[c]),
                (half * sense) * (after[c] - before[c]),
                half * (over[c] - under[c]),
            ]
        )
    mix[0][0] = mix[0][0] + (keep - diffuse * inverse_square)
    mix[1][1] = mix[1][1] + (keep - diffuse * inverse_square) + bend * radial
    mix[1][0] = mix[1][0] - bend * around
    mix[2][2] = mix[2][2] + keep
    return pulls + (mix, turn)


def stage_kernel(many, below, above, behind, walls, strip, *rest):
    others = rest[: 2 if many else 1]
    cells, basis, gram, message, advanced, first, second, edge, edge_flow, table = rest[len(others) :]
    has_high = lax.axis_index("gz") < lax.axis_size("gz") - 1
    inside = lanes(sub) % 8
    mine = [strip[pl.ds(sub * c, sub), :] for c in range(6)]
    if many:
        from_low = [others[0][pl.ds(sub * c, sub), :] for c in range(6)]
        from_high = [others[1][pl.ds(sub * c, sub), :] for c in range(6)]
        strips = [
            [jnp.where(inside < 4, b, a) for a, b in zip(mine, from_low)],
            [jnp.where(inside < 4, a, b) for a, b in zip(mine, from_high)],
        ]
    else:
        other = [others[0][pl.ds(sub * c, sub), :] for c in range(6)]
        strips = [[jnp.where((inside < 4) == has_high, a, b) for a, b in zip(mine, other)]]
    strips = [line + [ahead(line[0], 1, 16)] for line in strips]
    low_half = lax.axis_index("row") == 0
    ghosts = [jnp.where(low_half, signs[c] * layer(behind, 0, 12 + c), 0.0) for c in range(3)]
    lows = [layer(below, 0, 12 + c) for c in range(3)]
    highs = [layer(above, 0, 12 + c) for c in range(3)]
    march(
        strips, ghosts, lows, highs, walls, cells, basis, gram, message, advanced,
        first, second, edge, edge_flow, table,
    )


def march(
    strips, ghosts, lows, highs, walls, cells, basis, gram, message, advanced,
    first, second, edge, edge_flow, table,
):
    top = lax.axis_index("row")
    low_half = top == 0
    place = lax.axis_index("gz")
    has_low = place > 0
    has_high = place < lax.axis_size("gz") - 1
    lane = lanes(sub)
    slot = lane // 8

    number = (slot - 2).astype(jnp.float32) + top.astype(jnp.float32) * 8.0 + 0.5
    inverse = 1.0 / number
    strip_scalars = (
        jnp.where(number < 0.0, -1.0, 1.0),
        diffuse * (number - 0.5) * inverse,
        diffuse * (number + 0.5) * inverse,
        advect * inverse,
        inverse * inverse,
        diffuse * jnp.abs(inverse),
    )
    strip_wall = jnp.logical_and(slot == 10, top == 1)

    def strip_sides(values):
        return (
            [back(v, 1, 8) for v in values],
            [ahead(v, 1, 8) for v in values],
            [back(v, 0) for v in values],
            [ahead(v, 0) for v in values],
            [back(v, 1) for v in values],
            [ahead(v, 1) for v in values],
        )

    def walled(values, factors):
        return [jnp.where(strip_wall, f * back(v, 1, 8), v) for v, f in zip(values, factors)]

    levels = []
    flows = []
    for line in strips:
        factor = line[6]
        flow = walled(line[3:6], wall_signs)
        flows.append(flow)
        weights = coefficients_of(flow, strip_sides(flow), *strip_scalars)
        start = walled(line[:3], [factor] * 3)
        one = rate(start, strip_sides(start), weights)
        one = walled([a + b for a, b in zip(start, one)], [factor] * 3)
        two = rate(one, strip_sides(one), weights)
        two = [0.75 * s + 0.25 * (a + b) for s, a, b in zip(start, one, two)]
        levels.append((start, one, two))

    inner_side = lane % 8 < 4

    def store_edges(target, low_values, high_values):
        for c in range(3):
            low = jnp.where(has_low, back(low_values[c], 1), 0.0)
            high = jnp.where(has_high, ahead(high_values[c], 1), 0.0)
            target[pl.ds(sub * c, sub), :] = jnp.where(inner_side, high, low)

    def axial(value, source, c, w, start, size):
        ghost = source[pl.ds(sub * c + start, size), :]
        ghost = pltpu.roll(ghost, 128 - (8 * (w - 1) + 4), 1)
        at = lane[:size]
        return (
            jnp.where(at == 0, ghost, back(value, 1)),
            jnp.where(at == 127, ghost, ahead(value, 1)),
        )

    def pick(low, high):
        return jnp.where(low_half, np.float32(low), np.float32(high))

    def scalars(w):
        options = []
        for half in range(2):
            r = half * 8 + (w - 3) + 0.5
            options.append(
                (
                    -1.0 if r < 0 else 1.0,
                    diffuse * (r - 0.5) / r,
                    diffuse * (r + 0.5) / r,
                    advect / r,
                    1.0 / (r * r),
                    diffuse / abs(r),
                )
            )
        return [pick(a, b) for a, b in zip(*options)]

    def read(source, c, w, start=0, size=sub):
        return source[pl.ds(row_of(c, w) + start, size), :]

    for c in range(6):
        last = read(cells, c, 10)
        factor = walls[...] if c < 3 else wall_signs[c - 3]
        cells[pl.ds(row_of(c, 11), sub), :] = jnp.where(low_half, read(cells, c, 11), factor * last)

    def surroundings(source, first_component, ends, w, start, size):
        center, sides = [], [[], [], [], [], [], []]
        for c in range(3):
            at = first_component + c
            whole = read(source, at, w)
            value = whole[:size]
            under, over = axial(value, ends, c, w, start, size)
            for side, part in zip(
                sides,
                (
                    read(source, at, w - 1, start, size),
                    read(source, at, w + 1, start, size),
                    back(whole, 0)[:size],
                    ahead(whole, 0)[:size],
                    under,
                    over,
                ),
            ):
                side.append(part)
            center.append(value)
        return center, sides

    def table_rows(kind, w, start, size):
        return pl.ds((kind * 12 + w - 1) * sub + start, size)

    def make_table(w):
        weights = coefficients_of(*surroundings(cells, 3, edge_flow, w, 0, sub), *scalars(w))
        flat = list(weights[:6]) + [value for row in weights[6] for value in row]
        if w not in (1, 12):
            for kind, value in enumerate(flat):
                table[table_rows(kind, w, 0, sub), :] = value
        return weights

    def stored_table(w, start, size):
        flat = [table[table_rows(kind, w, start, size), :] for kind in range(kinds_of_coefficient)]
        mix = [flat[6:9], flat[9:12], flat[12:15]]
        return tuple(flat[:6]) + (mix, scalars(w)[-1])

    def field_rate(source, w, start=0, size=sub, weights=None):
        center, sides = surroundings(source, 0, edge, w, start, size)
        return center, rate(center, sides, weights or stored_table(w, start, size))

    store_edges(edge_flow, flows[0], flows[-1])
    store_edges(edge, levels[0][0], levels[-1][0])
    for w in range(1, 13):
        center, change = field_rate(cells, w, weights=make_table(w))
        for c in range(3):
            first[pl.ds(row_of(c, w), sub), :] = center[c] + change[c]
    for c in range(3):
        low = pl.ds(row_of(c, 1), 8)
        first[low, :] = first[low, :] + ghosts[c]
        before = pl.ds(row_of(c, 3) + 14, 8, stride=sub)
        after = pl.ds(row_of(c, 3) + 9, 8, stride=sub)
        first[before, :] = first[before, :] + lows[c]
        first[after, :] = first[after, :] + highs[c]

    def close_wall(source):
        for c in range(3):
            source[pl.ds(row_of(c, 11), sub), :] = jnp.where(
                low_half, read(source, c, 11), walls[...] * read(source, c, 10)
            )

    close_wall(first)
    store_edges(edge, levels[0][1], levels[-1][1])
    for w in range(2, 12):
        center, change = field_rate(first, w)
        for c in range(3):
            second[pl.ds(row_of(c, w), sub), :] = 0.75 * read(cells, c, w) + 0.25 * (
                center[c] + change[c]
            )
    close_wall(second)
    store_edges(edge, levels[0][2], levels[-1][2])
    count = basis.shape[0] // 192
    sums = [jnp.zeros((8, 128), jnp.float32) for _ in range(count + 1)]
    for w in range(3, 11):
        center, change = field_rate(second, w, 0, 8)
        for c in range(3):
            rows = pl.ds(64 * c + 8 * (w - 3), 8)
            value = read(cells, c, w, 0, 8) / 3.0 + (2.0 / 3.0) * (center[c] + change[c])
            advanced[rows, :] = value
            for m in range(count):
                sums[m] += basis[pl.ds(192 * m + 64 * c + 8 * (w - 3), 8), :] * value
            sums[count] += value * value
    spot = lanes(1)
    line = gram[...]
    for m in range(count + 1):
        total = jnp.sum(jnp.sum(sums[m], axis=0, keepdims=True), axis=1, keepdims=True)
        line = jnp.where(spot == m, total, line)
    for device in range(message.shape[0]):
        message[device] = line


side_wall = 16 * tiles
side_strip = side_wall + 8
side_axis = side_strip + 16
side_length = side_axis + 24
diagonal_wall = 24
diagonal_length = 32
share_corner = 8 * tiles
share_rest = share_corner + 24
share_turn = share_rest + side_length - side_wall
share_diagonal = share_turn + 8 * tiles
share_length = share_diagonal + diagonal_length


def faces_up():
    return (lax.axis_index("phi") + lax.axis_index("row")) % 2 == 0


def load_kernel(conductance, region, field, velocity, reflect, field_copy, flow_copy):
    kinds = region[...]
    value = jnp.zeros(kinds.shape, jnp.float32)
    for kind in range(conductance.shape[0]):
        value = jnp.where(kinds == kind, conductance[kind], value)
    reflect[...] = 1.0 - 2.0 * value / (1.0 + value)
    field_copy[...] = field[...]
    flow_copy[...] = velocity[...]


def send_kernel(field, velocity, far_field, far_flow, reflect, side, turn, diagonal, strip):
    top = lax.axis_index("row")
    upper = faces_up()
    slot = lanes(8) // 8

    def facing(load, depth):
        return jnp.where(upper, load(8 - depth), load(depth - 1))

    def column(source, c, depth):
        return facing(lambda q: source[pl.ds(c * 64 + q, 8, stride=8), :], depth)

    direction = jnp.where(upper, -1.0, 1.0)
    index = lax.broadcasted_iota(jnp.int32, (8, 128), 0).astype(jnp.float32)
    for source, flow, half in ((field, velocity, top), (far_field, far_flow, 1 - top)):
        base = half * (8 * tiles)

        def put(tile, value):
            side[pl.ds(pl.multiple_of(base + 8 * tile, 8), 8), :] = value

        bend = (diffuse * direction) / (index + (half.astype(jnp.float32) * 8.0 + 0.5))
        near_two = [column(source, c, 2) for c in range(3)]
        flow_two = [column(flow, c, 2) for c in range(3)]
        distant = [column(source, c, 3) for c in range(3)]
        carry = diffuse + advect * jnp.maximum(-direction * flow_two[1], 0.0)
        stretch = (0.5 * advect * direction) * near_two[1]
        term = [carry * distant[c] + stretch * column(flow, c, 3) for c in range(3)]
        term[0] = term[0] - bend * distant[1]
        term[1] = term[1] + bend * distant[0]
        for c in range(3):
            put(c, column(source, c, 1))
            put(3 + c, column(flow, c, 1))
            put(6 + c, near_two[c])
            put(9 + c, flow_two[c])
            put(12 + c, term[c])
    for depth in (1, 2):
        wall = facing(lambda q: reflect[pl.ds(q, 1), :], depth)
        side[pl.ds(side_wall + depth - 1, 1), :] = wall
        diagonal[pl.ds(diagonal_wall + depth - 1, 1), :] = wall

    for c in range(6):
        own, far = (field, far_field) if c < 3 else (velocity, far_flow)
        parts = []
        for source in (own, far):
            part = jnp.zeros((8, 128), jnp.float32)
            for r in range(8):
                part = jnp.where(
                    slot == r, pltpu.roll(layer(source, c % 3, r), (8 * r + 4) % 128, 1), part
                )
            parts.append(part)
        low = jnp.where(top == 0, parts[0], parts[1])
        high = jnp.where(top == 0, parts[1], parts[0])
        strip[pl.ds(8 * c, 8), :] = jnp.where(slot < 8, low, pltpu.roll(high, 64, 1))
    for depth in (1, 2):
        edge = facing(lambda q: strip[pl.ds(q, 6, stride=8), :], depth)
        side[pl.ds(side_strip + 8 * (depth - 1), 6), :] = edge
        diagonal[pl.ds(8 * (depth - 1), 6), :] = edge
    diagonal[pl.ds(16, 6), :] = jnp.where(
        upper, strip[pl.ds(0, 6, stride=8), :], strip[pl.ds(7, 6, stride=8), :]
    )

    def inner_cell(own, far, start, count, step):
        rows = pl.ds(start, count, stride=step)
        return jnp.where(top == 0, own[rows, :], far[rows, :])

    for place, (r, depth) in enumerate(((0, 1), (0, 2), (1, 1))):
        for part, (own, far) in enumerate(((field, far_field), (velocity, far_flow))):
            side[pl.ds(side_axis + 8 * place + 3 * part, 3), :] = jnp.where(
                upper,
                inner_cell(own, far, r * 8 + depth - 1, 3, 64),
                inner_cell(own, far, r * 8 + 8 - depth, 3, 64),
            )
    carry = (diffuse * 2.0 / 1.5) - advect * jnp.minimum(layer(far_flow, 0, 1), 0.0)
    stretch = (0.5 * advect) * layer(far_field, 0, 1)
    content = []
    for r in range(2):
        content += [layer(far_field, c, r) for c in range(3)]
        content += [layer(far_flow, c, r) for c in range(3)]
    content += [
        carry * layer(far_field, c, 2) + stretch * layer(far_flow, c, 2) for c in range(3)
    ]
    for tile in range(tiles):
        value = content[tile]
        if tile < 6:
            value = jnp.where(top == 0, strip[pl.ds(8 * tile, 8), :], value)
        elif tile == 6:
            value = jnp.where(top == 0, reflect[...], value)
        turn[pl.ds(8 * tile, 8), :] = value


def other_corner(side, first, step):
    top = lax.axis_index("row")
    low = side[pl.ds(8 * tiles + first + step, 6, stride=8), :]
    high = side[pl.ds(first + 7 - step, 6, stride=8), :]
    return jnp.where(top == 0, low, high)


def share_kernel(side, turn, diagonal, out):
    top = lax.axis_index("row")
    half = pl.multiple_of((1 - top) * (8 * tiles), 8)
    out[pl.ds(0, 8 * tiles), :] = side[pl.ds(half, 8 * tiles), :]
    for place, (first, step) in enumerate(((0, 0), (48, 0), (0, 1))):
        low = side[pl.ds(first + 7 - step, 6, stride=8), :]
        high = side[pl.ds(8 * tiles + first + step, 6, stride=8), :]
        out[pl.ds(share_corner + 8 * place, 6), :] = jnp.where(top == 0, low, high)
    out[pl.ds(share_rest, side_length - side_wall), :] = side[
        pl.ds(side_wall, side_length - side_wall), :
    ]
    out[pl.ds(share_turn, 8 * tiles), :] = turn[...]
    out[pl.ds(share_diagonal, diagonal_length), :] = diagonal[...]


def compact_kernel(
    field, velocity, far_field, far_flow, reflect, strip, side, turn, diagonal, opposite, shared,
    basis, gram, message, advanced, cells, walls, line, first, second, edge, edge_flow, table,
):
    top = lax.axis_index("row")
    low_half = top == 0
    upper = faces_up()
    mine_low = lax.axis_index("gz") == 0

    def both(own, other):
        return jnp.where(upper, other, own), jnp.where(upper, own, other)

    own_half = pl.multiple_of(top * (8 * tiles), 8)

    def tile_pair(tile):
        return both(
            side[pl.ds(pl.multiple_of(own_half + 8 * tile, 8), 8), :], shared[pl.ds(8 * tile, 8), :]
        )

    def rest_pair(start, count):
        return both(
            side[pl.ds(start, count), :], shared[pl.ds(share_rest + start - side_wall, count), :]
        )

    def diagonal_pair(start, count):
        return both(
            diagonal[pl.ds(start, count), :], shared[pl.ds(share_diagonal + start, count), :]
        )

    behind = [shared[pl.ds(share_turn + 8 * tile, 8), :] for tile in range(tiles)]
    nothing = jnp.zeros((8, 128), jnp.float32)
    for c in range(6):
        source, far = (field, far_field) if c < 3 else (velocity, far_flow)
        sign = signs[c % 3]
        for r in range(8):
            cells[pl.ds(row_of(c, r + 3), 8), :] = layer(source, c % 3, r)
        for w in range(window):
            cells[pl.ds(row_of(c, w) + 8, 8), :] = nothing
        for w in range(3):
            ghost = sign * behind[6 * (2 - w) + c] if w > 0 else 0.0
            cells[pl.ds(row_of(c, w), 8), :] = jnp.where(low_half, ghost, layer(far, c % 3, 5 + w))
            cells[pl.ds(row_of(c, 11 + w), 8), :] = jnp.where(low_half, layer(far, c % 3, w), 0.0)
        for depth in range(2):
            below, above = tile_pair(6 * depth + c)
            cells[pl.ds(row_of(c, 3) + 15 - depth, 8, stride=sub), :] = below
            cells[pl.ds(row_of(c, 3) + 8 + depth, 8, stride=sub), :] = above
    flip = lax.broadcasted_iota(jnp.int32, (6, 128), 0)
    flip = jnp.where((flip == 2) | (flip == 5), 1.0, -1.0)
    for place, (w, first_row, step, depth) in enumerate(((2, 0, 0, 0), (2, 48, 0, 1), (1, 0, 1, 0))):
        axis_high, axis_low = rest_pair(side_axis + 8 * place, 6)
        below, above = both(
            other_corner(side, first_row, step), shared[pl.ds(share_corner + 8 * place, 6), :]
        )
        for axis_part, other, q in ((axis_low, below, 15 - depth), (axis_high, above, 8 + depth)):
            low = pl.ds(row_of(0, w) + q, 6, stride=window * sub)
            high = pl.ds(row_of(0, 13 - w) + q, 6, stride=window * sub)
            cells[low, :] = jnp.where(low_half, flip * axis_part, other)
            cells[high, :] = jnp.where(low_half, other, 0.0)

    slot, inside = lanes(sub) // 8, lanes(sub) % 8
    axial_turn = [
        jnp.where(
            low_half, turn[pl.ds(8 * tile, 8), :], shared[pl.ds(share_turn + 8 * tile, 8), :]
        )
        for tile in range(7)
    ]
    own_side = (inside < 4) == mine_low

    def merge(own, other):
        return jnp.where(own_side[: own.shape[0]], own, other)

    for part, (tile, pair) in enumerate(
        ((reflect[...], rest_pair(side_wall, 2)), (axial_turn[6], diagonal_pair(diagonal_wall, 2)))
    ):
        below, above = pair
        base = sub * part
        walls[pl.ds(base, 8), :] = tile
        walls[pl.ds(base + 8, 8), :] = nothing
        walls[pl.ds(base + 8, 2), :] = above
        walls[pl.ds(base + 15, 1), :] = below[0:1]
        walls[pl.ds(base + 14, 1), :] = below[1:2]
    factor = merge(
        pltpu.roll(walls[pl.ds(0, sub), :], 84, 1), pltpu.roll(walls[pl.ds(sub, sub), :], 84, 1)
    )

    for c in range(6):
        own = strip[pl.ds(8 * c, 8), :]
        line[pl.ds(sub * c, 8), :] = merge(own, axial_turn[c])
        line[pl.ds(sub * c + 8, 8), :] = nothing
    for depth in (1, 2):
        below, above = rest_pair(side_strip + 8 * (depth - 1), 6)
        beyond_below, beyond_above = diagonal_pair(8 * (depth - 1), 6)
        line[pl.ds(16 - depth, 6, stride=sub), :] = merge(below, beyond_below)
        line[pl.ds(7 + depth, 6, stride=sub), :] = merge(above, beyond_above)
    axis_high, axis_low = diagonal_pair(16, 6)
    combined = []
    for c in range(6):
        value = line[pl.ds(sub * c, sub), :]
        combined.append(jnp.where(low_half, pltpu.roll(value, 16, 1), pltpu.roll(value, 80, 1)))
    for c in range(6):
        sign = signs[c % 3]
        across = opposite[pl.ds(8 * c, 8), :]
        own = jnp.where(
            slot[:8] == 1,
            pltpu.roll(behind[c], 12, 1),
            pltpu.roll(behind[6 + c], 4, 1),
        )
        other = jnp.where(slot[:8] == 1, pltpu.roll(across, 8, 1), pltpu.roll(across, 120, 1))
        line[pl.ds(sub * c, 8), :] = sign * merge(own, other)
        line[pl.ds(sub * c + 8, 8), :] = nothing
        line[pl.ds(sub * c + 8, 1), :] = sign * pltpu.roll(axis_high, 8, 1)[c : c + 1]
        line[pl.ds(sub * c + 15, 1), :] = sign * pltpu.roll(axis_low, 8, 1)[c : c + 1]
        ghost = line[pl.ds(sub * c, sub), :]
        combined[c] = jnp.where(jnp.logical_and(slot < 2, low_half), ghost, combined[c])
    combined.append(factor)
    ghosts = [jnp.where(low_half, signs[c] * behind[12 + c], 0.0) for c in range(3)]
    lows, highs = zip(*[tile_pair(12 + c) for c in range(3)])
    march(
        [combined], ghosts, lows, highs, walls.at[pl.ds(0, sub), :], cells, basis, gram, message,
        advanced, first, second, edge, edge_flow, table,
    )


def gram_place(m, n):
    return 16 + m * (m + 1) // 2 + n


def gram_kernel(basis, out):
    count = basis.shape[0] // 192
    spot = lanes(1)
    line = jnp.zeros((1, 128), jnp.float32)
    for m in range(count):
        sums = [jnp.zeros((8, 128), jnp.float32) for _ in range(m + 1)]
        for tile in range(24):
            value = basis[pl.ds(192 * m + 8 * tile, 8), :]
            for n in range(m + 1):
                sums[n] += value * basis[pl.ds(192 * n + 8 * tile, 8), :]
        for n in range(m + 1):
            total = jnp.sum(jnp.sum(sums[n], axis=0, keepdims=True), axis=1, keepdims=True)
            line = jnp.where(spot == gram_place(m, n), total, line)
    out[...] = line


def finish_kernel(cell_count, messages, advanced, basis, out, hessenberg):
    count = basis.shape[0] // 192
    total = messages[0]
    for device in range(1, messages.shape[0]):
        total = total + messages[device]

    def entry(index):
        return jnp.broadcast_to(total[:, index : index + 1], (8, 128))

    pending = [entry(m) for m in range(count)]
    energy = entry(count)
    weights = []
    for m in range(count):
        diagonal = entry(gram_place(m, m))
        weight = pending[m] / diagonal
        weights.append(weight)
        energy = energy - weight * (2.0 * pending[m] - weight * diagonal)
        for n in range(m + 1, count):
            pending[n] = pending[n] - weight * entry(gram_place(n, m))
    spread = jnp.sqrt(jnp.maximum(energy, 0.0) / cell_count + epsilon)
    scale = 1.0 / spread
    for tile in range(24):
        rows = pl.ds(8 * tile, 8)
        value = advanced[rows, :]
        for m in range(count):
            value = value - weights[m] * basis[pl.ds(192 * m + 8 * tile, 8), :]
        out[rows, :] = value * scale
    for m in range(count):
        hessenberg[m] = weights[m][0, 0]
    hessenberg[count] = spread[0, 0]


def shift(value, axis, step):
    count = lax.axis_size(axis)
    return lax.ppermute(value, axis, [(i, (i + step) % count) for i in range(count)])


def march_scratch():
    return [
        shape(3 * window * sub, 128),
        shape(3 * window * sub, 128),
        shape(3 * sub, 128),
        shape(3 * sub, 128),
        shape(kinds_of_coefficient * 12 * sub, 128),
    ]


def general_plan(field, velocity, basis, wall_region, wall_conductance):
    loop = lax.axis_size("phi")
    ends = lax.axis_size("gz")
    halves = lax.axis_size("row")
    fold = loop == 4
    many = ends > 2
    vectors = basis.shape[0]
    field_rows = field.reshape(192, 128)
    flow_rows = velocity.reshape(192, 128)
    swap = [(0, 1), (1, 0)]
    far_field = lax.ppermute(field_rows, "row", swap)
    far_flow = lax.ppermute(flow_rows, "row", swap)
    field_rows, flow_rows, basis_rows = near(
        field_rows, flow_rows, basis.reshape(vectors * 192, 128)
    )
    inner = pl.pallas_call(
        inner_kernel, in_specs=vmem(2), out_specs=vmem(1)[0], out_shape=shape(8 * tiles, 128)
    )(field_rows, flow_rows)
    half = loop // 2
    turned = []
    for p in range(loop):
        for r in range(halves):
            turned.append((p * halves + r, ((p + half) % loop if r == 0 else p) * halves + r))
    behind = lax.ppermute(inner, ("phi", "row"), turned)
    far_field, far_flow = near(far_field, far_flow)
    side = side_rows if fold else axis_row
    packed = pl.pallas_call(
        functools.partial(sides_kernel, fold),
        in_specs=[pl.BlockSpec(memory_space=pltpu.SMEM)] + vmem(5),
        out_specs=vmem(3 if fold else 5),
        out_shape=[shape(side, 128), shape(side, 128), shape(8, 128)]
        + ([] if fold else [shape(24, 128)] * 2),
    )(wall_conductance, wall_region, field_rows, flow_rows, far_field, far_flow)
    up, down, reflect = packed[:3]
    below = shift(up, "phi", 1)
    above = shift(down, "phi", -1)
    corners = []
    if not fold:
        corners = [shift(packed[3], "phi", half + 1), shift(packed[4], "phi", half - 1)]
    gram = pl.pallas_call(
        gram_kernel, in_specs=vmem(1), out_specs=vmem(1)[0], out_shape=shape(1, 128)
    )(basis_rows)
    below, above, behind, gram, *corners = lax.optimization_barrier(
        (below, above, behind, gram, *corners)
    )
    below, above, behind, gram, *corners = near(below, above, behind, gram, *corners)
    walls, strip, cells = pl.pallas_call(
        functools.partial(window_kernel, fold),
        in_specs=vmem(8 + len(corners)),
        out_specs=vmem(3),
        out_shape=[shape(sub, 128), shape(6 * sub, 128), shape(6 * window * sub, 128)],
    )(field_rows, flow_rows, far_field, far_flow, below, above, behind, reflect, *corners)
    if many:
        up_pairs = [(i, i + 1) for i in range(ends - 1)]
        others = [
            lax.ppermute(strip, "gz", up_pairs),
            lax.ppermute(strip, "gz", [(b, a) for a, b in up_pairs]),
        ]
    else:
        others = [lax.ppermute(strip, "gz", swap)]
    walls, strip, cells, *others = near(walls, strip, cells, *others)
    devices = lax.axis_size(("phi", "gz", "row"))
    return pl.pallas_call(
        functools.partial(stage_kernel, many),
        in_specs=vmem(8 + len(others)),
        out_specs=vmem(2),
        out_shape=[shape(devices, 1, 128), shape(192, 128)],
        scratch_shapes=march_scratch(),
    )(below, above, behind, walls, strip, *others, cells, basis_rows, gram)


def compact_plan(field, velocity, basis, wall_region, wall_conductance):
    vectors = basis.shape[0]
    field_rows = field.reshape(192, 128)
    flow_rows = velocity.reshape(192, 128)
    axes = ("phi", "gz", "row")
    devices = lax.axis_size(axes)

    def exchange(value, partner):
        pairs = []
        for p in range(4):
            for g in range(2):
                for r in range(2):
                    q, h = partner(p, g, r)
                    pairs.append(((p * 2 + g) * 2 + r, (q % 4 * 2 + h) * 2 + r))
        return lax.ppermute(value, axes, pairs)

    def beside(p, r):
        return p + 1 if (p + r) % 2 == 0 else p - 1

    swap = [(0, 1), (1, 0)]
    far_field = lax.ppermute(field_rows, "row", swap)
    far_flow = lax.ppermute(flow_rows, "row", swap)
    reflect, field_rows, flow_rows = pl.pallas_call(
        load_kernel,
        in_specs=[pl.BlockSpec(memory_space=pltpu.SMEM)] + vmem(3),
        out_specs=vmem(3),
        out_shape=[shape(8, 128), shape(192, 128), shape(192, 128)],
    )(wall_conductance, wall_region, field_rows, flow_rows)
    blocks = near(field_rows, flow_rows, far_field, far_flow, reflect)
    side, turn, diagonal, strip = pl.pallas_call(
        send_kernel,
        in_specs=vmem(5),
        out_specs=vmem(4),
        out_shape=[
            shape(side_length, 128),
            shape(8 * tiles, 128),
            shape(diagonal_length, 128),
            shape(48, 128),
        ],
    )(*blocks)
    opposite = exchange(strip, lambda p, g, r: (p + 2, 1 - g))
    turn = exchange(turn, lambda p, g, r: (p, 1 - g) if r == 0 else (p + 2, g))
    diagonal = exchange(diagonal, lambda p, g, r: (beside(p, r), 1 - g))
    side = exchange(side, lambda p, g, r: (beside(p, r), g))
    (basis_rows,) = near(basis.reshape(vectors * 192, 128))
    gram = pl.pallas_call(
        gram_kernel, in_specs=vmem(1), out_specs=vmem(1)[0], out_shape=shape(1, 128)
    )(basis_rows)
    side, turn, diagonal, opposite, gram = near(
        *lax.optimization_barrier((side, turn, diagonal, opposite, gram))
    )
    share = pl.pallas_call(
        share_kernel, in_specs=vmem(3), out_specs=vmem(1)[0], out_shape=shape(share_length, 128)
    )(side, turn, diagonal)
    shared = lax.ppermute(share, "row", swap)
    strip, shared = near(strip, shared)
    return pl.pallas_call(
        compact_kernel,
        in_specs=vmem(13),
        out_specs=vmem(2),
        out_shape=[shape(devices, 1, 128), shape(192, 128)],
        scratch_shapes=[
            shape(6 * window * sub, 128),
            shape(2 * sub, 128),
            shape(6 * sub, 128),
        ]
        + march_scratch(),
    )(*blocks, strip, side, turn, diagonal, opposite, shared, basis_rows, gram)


def local(field, velocity, basis, wall_region, wall_conductance):
    axes = ("phi", "gz", "row")
    vectors = basis.shape[0]
    devices = lax.axis_size(axes)
    compact = tuple(lax.axis_size(axis) for axis in axes) == (4, 2, 2)
    plan = compact_plan if compact else general_plan
    message, advanced = plan(field, velocity, basis, wall_region, wall_conductance)
    (basis_rows,) = near(basis.reshape(vectors * 192, 128))
    messages = lax.all_to_all(message, axes, 0, 0, tiled=True)
    messages, advanced = near(messages, advanced)
    out, hessenberg = pl.pallas_call(
        functools.partial(finish_kernel, float(field.size * devices)),
        in_specs=vmem(3),
        out_specs=vmem(1) + [pl.BlockSpec(memory_space=pltpu.SMEM)],
        out_shape=[
            jax.ShapeDtypeStruct((192, 128), jnp.float32),
            jax.ShapeDtypeStruct((vectors + 1,), jnp.float32),
        ],
    )(messages, advanced, basis_rows)
    return out.reshape(field.shape), hessenberg


def solution(mesh):
    return jax.shard_map(
        local,
        mesh=mesh,
        in_specs=(
            P("groups", "row", "phi", "gz"),
            P("groups", "row", "phi", "gz"),
            P("groups", None, "row", "phi", "gz"),
            P(("groups", "phi"), "gz"),
            P("groups"),
        ),
        out_specs=(P("groups", "row", "phi", "gz"), P("groups")),
        check_vma=False,
    )
```

```python
import functools

import jax
import jax.numpy as jnp
import numpy as np
from jax import lax
from jax.experimental import pallas as pl
from jax.experimental.pallas import tpu as pltpu
from jax.sharding import PartitionSpec as P

advect = 0.2
diffuse = 0.1
epsilon = 1e-06
signs = (-1.0, -1.0, 1.0)
wall_signs = (-1.0, 1.0, 1.0)

tiles = 15
wall_row = 8 * tiles
corner_row = wall_row + 8
axis_row = corner_row + 24
side_rows = axis_row + 24
window = 14
sub = 16
kinds_of_coefficient = 15


def row_of(component, w):
    return (component * window + w) * sub


def vmem(count):
    return [pl.BlockSpec(memory_space=pltpu.VMEM)] * count


def shape(*dims):
    return pltpu.VMEM(dims, jnp.float32)


def near(*values):
    return [pltpu.with_memory_space_constraint(value, pltpu.VMEM) for value in values]


def lanes(rows):
    return lax.broadcasted_iota(jnp.int32, (rows, 128), 1)


def layer(source, c, r):
    return source[pl.ds(c * 64 + r * 8, 8), :]


def inner_kernel(field, velocity, inner):
    middle = lax.axis_index("row").astype(jnp.float32) * 8.0 + 1.5
    pull = diffuse * (middle + 0.5) / jnp.full((8, 128), middle)
    carry = pull - advect * jnp.minimum(layer(velocity, 0, 1), 0.0)
    stretch = (0.5 * advect) * layer(field, 0, 1)
    for c in range(3):
        inner[pl.ds(8 * c, 8), :] = layer(field, c, 0)
        inner[pl.ds(8 * (3 + c), 8), :] = layer(velocity, c, 0)
        inner[pl.ds(8 * (6 + c), 8), :] = layer(field, c, 1)
        inner[pl.ds(8 * (9 + c), 8), :] = layer(velocity, c, 1)
        inner[pl.ds(8 * (12 + c), 8), :] = carry * layer(field, c, 2) + stretch * layer(
            velocity, c, 2
        )


def sides_kernel(
    fold, conductance, region, field, velocity, far_field, far_flow, up, down, reflect, *corners
):
    top = lax.axis_index("row")
    kinds = region[...]
    value = jnp.zeros(kinds.shape, jnp.float32)
    for kind in range(conductance.shape[0]):
        value = jnp.where(kinds == kind, conductance[kind], value)
    reflect[...] = 1.0 - 2.0 * value / (1.0 + value)

    def column(source, c, q):
        return source[pl.ds(c * 64 + q, 8, stride=8), :]

    def cell(source, r, q):
        return source[pl.ds(r * 8 + q, 3, stride=64), :]

    radius = lax.broadcasted_iota(jnp.int32, (8, 128), 0).astype(jnp.float32)
    turn = diffuse / (radius + (top.astype(jnp.float32) * 8.0 + 0.5))
    for out, (one, two, three), direction in ((up, (7, 6, 5), -1.0), (down, (0, 1, 2), 1.0)):
        for c in range(3):
            out[pl.ds(8 * c, 8), :] = column(field, c, one)
            out[pl.ds(8 * (3 + c), 8), :] = column(velocity, c, one)
            out[pl.ds(8 * (6 + c), 8), :] = column(field, c, two)
            out[pl.ds(8 * (9 + c), 8), :] = column(velocity, c, two)
        speed = column(velocity, 1, two)
        carry = diffuse + advect * jnp.maximum(-direction * speed, 0.0)
        stretch = (0.5 * advect * direction) * column(field, 1, two)
        far = [column(field, c, three) for c in range(3)]
        term = [carry * far[c] + stretch * column(velocity, c, three) for c in range(3)]
        term[0] = term[0] - (direction * turn) * far[1]
        term[1] = term[1] + (direction * turn) * far[0]
        for c in range(3):
            out[pl.ds(8 * (12 + c), 8), :] = term[c]
        out[pl.ds(wall_row, 1), :] = reflect[pl.ds(one, 1), :]
        out[pl.ds(wall_row + 1, 1), :] = reflect[pl.ds(two, 1), :]
        for place, (r, q) in enumerate(((0, one), (0, two), (1, one))):
            for part, source in enumerate((far_field, far_flow)):
                out[pl.ds(corner_row + 8 * place + 3 * part, 3), :] = jnp.where(
                    top == 0, cell(source, r, q), cell(source, 7 - r, q)
                )
    for side, (one, two) in ((0, (7, 6)), (1, (0, 1))):
        if fold:
            out, base = (down, up)[side], axis_row
        else:
            out, base = corners[side], 0
        for place, (r, q) in enumerate(((0, one), (0, two), (1, one))):
            out[pl.ds(base + 8 * place, 3), :] = cell(field, r, q)
            out[pl.ds(base + 8 * place + 3, 3), :] = cell(velocity, r, q)


def window_kernel(
    fold, field, velocity, far_field, far_flow, below, above, behind, reflect, *rest
):
    if fold:
        axis_low, axis_high, axis_base = above, below, axis_row
    else:
        axis_low, axis_high, axis_base = rest[0], rest[1], 0
    walls, strip, cells = rest[-3:]
    low_half = lax.axis_index("row") == 0
    nothing = jnp.zeros((8, 128), jnp.float32)
    for c in range(6):
        source, far = (field, far_field) if c < 3 else (velocity, far_flow)
        sign = signs[c % 3]
        for r in range(8):
            cells[pl.ds(row_of(c, r + 3), 8), :] = layer(source, c % 3, r)
        for w in range(window):
            cells[pl.ds(row_of(c, w) + 8, 8), :] = nothing
        for w in range(3):
            ghost = sign * behind[pl.ds(48 * (2 - w) + 8 * c, 8), :] if w > 0 else 0.0
            cells[pl.ds(row_of(c, w), 8), :] = jnp.where(low_half, ghost, layer(far, c % 3, 5 + w))
            cells[pl.ds(row_of(c, 11 + w), 8), :] = jnp.where(low_half, layer(far, c % 3, w), 0.0)
        for depth in range(2):
            place = pl.ds(48 * depth + 8 * c, 8)
            cells[pl.ds(row_of(c, 3) + 15 - depth, 8, stride=sub), :] = below[place, :]
            cells[pl.ds(row_of(c, 3) + 8 + depth, 8, stride=sub), :] = above[place, :]
    flip = lax.broadcasted_iota(jnp.int32, (6, 128), 0)
    flip = jnp.where((flip == 2) | (flip == 5), 1.0, -1.0)
    for place, (w, step) in enumerate(((2, 0), (2, 1), (1, 0))):
        for axis_source, source, q in ((axis_low, below, 15 - step), (axis_high, above, 8 + step)):
            ghost = flip * axis_source[pl.ds(axis_base + 8 * place, 6), :]
            other = source[pl.ds(corner_row + 8 * place, 6), :]
            low = jnp.where(low_half, ghost, other)
            high = jnp.where(low_half, other, 0.0)
            for c in range(6):
                cells[pl.ds(row_of(c, w) + q, 1), :] = low[c : c + 1]
                cells[pl.ds(row_of(c, 13 - w) + q, 1), :] = high[c : c + 1]
    walls[pl.ds(0, 8), :] = reflect[...]
    walls[pl.ds(8, 8), :] = nothing
    walls[pl.ds(8, 2), :] = above[pl.ds(wall_row, 2), :]
    walls[pl.ds(15, 1), :] = below[pl.ds(wall_row, 1), :]
    walls[pl.ds(14, 1), :] = below[pl.ds(wall_row + 1, 1), :]
    slot = lanes(sub) // 8
    for c in range(6):
        packed = jnp.where(slot == 12, pltpu.roll(walls[...], 100, 1), 0.0)
        for w in range(1, window - 1):
            row = cells[pl.ds(row_of(c, w), sub), :]
            packed = jnp.where(slot == w - 1, pltpu.roll(row, (8 * (w - 1) + 4) % 128, 1), packed)
        strip[pl.ds(sub * c, sub), :] = packed


def back(value, axis, step=1):
    return pltpu.roll(value, step, axis)


def ahead(value, axis, step=1):
    return pltpu.roll(value, value.shape[axis] - step, axis)


def rate(center, sides, coefficients):
    inward, outward, before, after, under, over = sides
    pull_in, pull_out, pull_before, pull_after, pull_under, pull_over, mix, turn = coefficients
    result = []
    for c in range(3):
        value = (
            (pull_in * inward[c] + pull_out * outward[c])
            + (pull_before * before[c] + pull_after * after[c])
            + (pull_under * under[c] + pull_over * over[c])
        )
        for d in range(3):
            value = value + mix[c][d] * center[d]
        result.append(value)
    result[0] = result[0] - turn * (after[1] - before[1])
    result[1] = result[1] + turn * (after[0] - before[0])
    return result


def coefficients_of(speed, sides, sense, inner_pull, outer_pull, bend, inverse_square, turn):
    inward, outward, before, after, under, over = sides
    radial, around, axial = speed
    around_here = sense * around
    pulls = (
        inner_pull + advect * jnp.maximum(radial, 0.0),
        outer_pull - advect * jnp.minimum(radial, 0.0),
        diffuse + advect * jnp.maximum(around_here, 0.0),
        diffuse - advect * jnp.minimum(around_here, 0.0),
        diffuse + advect * jnp.maximum(axial, 0.0),
        diffuse - advect * jnp.minimum(axial, 0.0),
    )
    keep = -6.0 * diffuse - advect * (jnp.abs(radial) + jnp.abs(around) + jnp.abs(axial))
    half = 0.5 * advect
    mix = []
    for c in range(3):
        mix.append(
            [
                half * (outward[c] - inward[c]),
                (half * sense) * (after[c] - before[c]),
                half * (over[c] - under[c]),
            ]
        )
    mix[0][0] = mix[0][0] + (keep - diffuse * inverse_square)
    mix[1][1] = mix[1][1] + (keep - diffuse * inverse_square) + bend * radial
    mix[1][0] = mix[1][0] - bend * around
    mix[2][2] = mix[2][2] + keep
    return pulls + (mix, turn)


def stage_kernel(many, below, above, behind, walls, strip, *rest):
    others = rest[: 2 if many else 1]
    cells, basis, gram, message, advanced, first, second, edge, edge_flow, table = rest[len(others) :]
    has_high = lax.axis_index("gz") < lax.axis_size("gz") - 1
    inside = lanes(sub) % 8
    mine = [strip[pl.ds(sub * c, sub), :] for c in range(6)]
    if many:
        from_low = [others[0][pl.ds(sub * c, sub), :] for c in range(6)]
        from_high = [others[1][pl.ds(sub * c, sub), :] for c in range(6)]
        strips = [
            [jnp.where(inside < 4, b, a) for a, b in zip(mine, from_low)],
            [jnp.where(inside < 4, a, b) for a, b in zip(mine, from_high)],
        ]
    else:
        other = [others[0][pl.ds(sub * c, sub), :] for c in range(6)]
        strips = [[jnp.where((inside < 4) == has_high, a, b) for a, b in zip(mine, other)]]
    strips = [line + [ahead(line[0], 1, 16)] for line in strips]
    low_half = lax.axis_index("row") == 0
    ghosts = [jnp.where(low_half, signs[c] * layer(behind, 0, 12 + c), 0.0) for c in range(3)]
    lows = [layer(below, 0, 12 + c) for c in range(3)]
    highs = [layer(above, 0, 12 + c) for c in range(3)]
    march(
        strips, ghosts, lows, highs, walls, cells, basis, gram, message, advanced,
        first, second, edge, edge_flow, table,
    )


def march(
    strips, ghosts, lows, highs, walls, cells, basis, gram, message, advanced,
    first, second, edge, edge_flow, table,
):
    top = lax.axis_index("row")
    low_half = top == 0
    place = lax.axis_index("gz")
    has_low = place > 0
    has_high = place < lax.axis_size("gz") - 1
    lane = lanes(sub)
    slot = lane // 8

    number = (slot - 2).astype(jnp.float32) + top.astype(jnp.float32) * 8.0 + 0.5
    inverse = 1.0 / number
    strip_scalars = (
        jnp.where(number < 0.0, -1.0, 1.0),
        diffuse * (number - 0.5) * inverse,
        diffuse * (number + 0.5) * inverse,
        advect * inverse,
        inverse * inverse,
        diffuse * jnp.abs(inverse),
    )
    strip_wall = jnp.logical_and(slot == 10, top == 1)

    def strip_sides(values):
        return (
            [back(v, 1, 8) for v in values],
            [ahead(v, 1, 8) for v in values],
            [back(v, 0) for v in values],
            [ahead(v, 0) for v in values],
            [back(v, 1) for v in values],
            [ahead(v, 1) for v in values],
        )

    def walled(values, factors):
        return [jnp.where(strip_wall, f * back(v, 1, 8), v) for v, f in zip(values, factors)]

    levels = []
    flows = []
    for line in strips:
        factor = line[6]
        flow = walled(line[3:6], wall_signs)
        flows.append(flow)
        weights = coefficients_of(flow, strip_sides(flow), *strip_scalars)
        start = walled(line[:3], [factor] * 3)
        one = rate(start, strip_sides(start), weights)
        one = walled([a + b for a, b in zip(start, one)], [factor] * 3)
        two = rate(one, strip_sides(one), weights)
        two = [0.75 * s + 0.25 * (a + b) for s, a, b in zip(start, one, two)]
        levels.append((start, one, two))

    inner_side = lane % 8 < 4

    def store_edges(target, low_values, high_values):
        for c in range(3):
            low = jnp.where(has_low, back(low_values[c], 1), 0.0)
            high = jnp.where(has_high, ahead(high_values[c], 1), 0.0)
            target[pl.ds(sub * c, sub), :] = jnp.where(inner_side, high, low)

    def axial(value, source, c, w, start, size):
        ghost = source[pl.ds(sub * c + start, size), :]
        ghost = pltpu.roll(ghost, 128 - (8 * (w - 1) + 4), 1)
        at = lane[:size]
        return (
            jnp.where(at == 0, ghost, back(value, 1)),
            jnp.where(at == 127, ghost, ahead(value, 1)),
        )

    def pick(low, high):
        return jnp.where(low_half, np.float32(low), np.float32(high))

    def scalars(w):
        options = []
        for half in range(2):
            r = half * 8 + (w - 3) + 0.5
            options.append(
                (
                    -1.0 if r < 0 else 1.0,
                    diffuse * (r - 0.5) / r,
                    diffuse * (r + 0.5) / r,
                    advect / r,
                    1.0 / (r * r),
                    diffuse / abs(r),
                )
            )
        return [pick(a, b) for a, b in zip(*options)]

    def read(source, c, w, start=0, size=sub):
        return source[pl.ds(row_of(c, w) + start, size), :]

    for c in range(6):
        last = read(cells, c, 10)
        factor = walls[...] if c < 3 else wall_signs[c - 3]
        cells[pl.ds(row_of(c, 11), sub), :] = jnp.where(low_half, read(cells, c, 11), factor * last)

    def surroundings(source, first_component, ends, w, start, size):
        center, sides = [], [[], [], [], [], [], []]
        for c in range(3):
            at = first_component + c
            whole = read(source, at, w)
            value = whole[:size]
            under, over = axial(value, ends, c, w, start, size)
            for side, part in zip(
                sides,
                (
                    read(source, at, w - 1, start, size),
                    read(source, at, w + 1, start, size),
                    back(whole, 0)[:size],
                    ahead(whole, 0)[:size],
                    under,
                    over,
                ),
            ):
                side.append(part)
            center.append(value)
        return center, sides

    def table_rows(kind, w, start, size):
        return pl.ds((kind * 12 + w - 1) * sub + start, size)

    def make_table(w):
        weights = coefficients_of(*surroundings(cells, 3, edge_flow, w, 0, sub), *scalars(w))
        flat = list(weights[:6]) + [value for row in weights[6] for value in row]
        if w not in (1, 12):
            for kind, value in enumerate(flat):
                table[table_rows(kind, w, 0, sub), :] = value
        return weights

    def stored_table(w, start, size):
        flat = [table[table_rows(kind, w, start, size), :] for kind in range(kinds_of_coefficient)]
        mix = [flat[6:9], flat[9:12], flat[12:15]]
        return tuple(flat[:6]) + (mix, scalars(w)[-1])

    def field_rate(source, w, start=0, size=sub, weights=None):
        center, sides = surroundings(source, 0, edge, w, start, size)
        return center, rate(center, sides, weights or stored_table(w, start, size))

    store_edges(edge_flow, flows[0], flows[-1])
    store_edges(edge, levels[0][0], levels[-1][0])
    for w in range(1, 13):
        center, change = field_rate(cells, w, weights=make_table(w))
        for c in range(3):
            first[pl.ds(row_of(c, w), sub), :] = center[c] + change[c]
    for c in range(3):
        low = pl.ds(row_of(c, 1), 8)
        first[low, :] = first[low, :] + ghosts[c]
        before = pl.ds(row_of(c, 3) + 14, 8, stride=sub)
        after = pl.ds(row_of(c, 3) + 9, 8, stride=sub)
        first[before, :] = first[before, :] + lows[c]
        first[after, :] = first[after, :] + highs[c]

    def close_wall(source):
        for c in range(3):
            source[pl.ds(row_of(c, 11), sub), :] = jnp.where(
                low_half, read(source, c, 11), walls[...] * read(source, c, 10)
            )

    close_wall(first)
    store_edges(edge, levels[0][1], levels[-1][1])
    for w in range(2, 12):
        center, change = field_rate(first, w)
        for c in range(3):
            second[pl.ds(row_of(c, w), sub), :] = 0.75 * read(cells, c, w) + 0.25 * (
                center[c] + change[c]
            )
    close_wall(second)
    store_edges(edge, levels[0][2], levels[-1][2])
    count = basis.shape[0] // 192
    sums = [jnp.zeros((8, 128), jnp.float32) for _ in range(count + 1)]
    for w in range(3, 11):
        center, change = field_rate(second, w, 0, 8)
        for c in range(3):
            rows = pl.ds(64 * c + 8 * (w - 3), 8)
            value = read(cells, c, w, 0, 8) / 3.0 + (2.0 / 3.0) * (center[c] + change[c])
            advanced[rows, :] = value
            for m in range(count):
                sums[m] += basis[pl.ds(192 * m + 64 * c + 8 * (w - 3), 8), :] * value
            sums[count] += value * value
    spot = lanes(1)
    line = gram[...]
    for m in range(count + 1):
        total = jnp.sum(jnp.sum(sums[m], axis=0, keepdims=True), axis=1, keepdims=True)
        line = jnp.where(spot == m, total, line)
    for device in range(message.shape[0]):
        message[device] = line


side_wall = 16 * tiles
side_strip = side_wall + 8
side_axis = side_strip + 16
side_length = side_axis + 24
diagonal_wall = 24
diagonal_length = 32
strip_length = 56
share_corner = 8 * tiles
share_rest = share_corner + 24
share_turn = share_rest + side_length - side_wall
share_strip = share_turn + 8 * tiles
share_diagonal = share_strip + strip_length
share_length = share_diagonal + diagonal_length


def faces_up():
    return (lax.axis_index("phi") + lax.axis_index("row")) % 2 == 0


def load_kernel(conductance, region, field, velocity, reflect, field_copy, flow_copy):
    kinds = region[...]
    value = jnp.zeros(kinds.shape, jnp.float32)
    for kind in range(conductance.shape[0]):
        value = jnp.where(kinds == kind, conductance[kind], value)
    reflect[...] = 1.0 - 2.0 * value / (1.0 + value)
    field_copy[...] = field[...]
    flow_copy[...] = velocity[...]


def send_kernel(field, velocity, far_field, far_flow, reflect, side, turn, diagonal, strip):
    top = lax.axis_index("row")
    upper = faces_up()
    slot = lanes(8) // 8

    def facing(load, depth):
        return jnp.where(upper, load(8 - depth), load(depth - 1))

    def column(source, c, depth):
        return facing(lambda q: source[pl.ds(c * 64 + q, 8, stride=8), :], depth)

    direction = jnp.where(upper, -1.0, 1.0)
    index = lax.broadcasted_iota(jnp.int32, (8, 128), 0).astype(jnp.float32)
    for source, flow, half in ((field, velocity, top), (far_field, far_flow, 1 - top)):
        base = half * (8 * tiles)

        def put(tile, value):
            side[pl.ds(pl.multiple_of(base + 8 * tile, 8), 8), :] = value

        bend = (diffuse * direction) / (index + (half.astype(jnp.float32) * 8.0 + 0.5))
        near_two = [column(source, c, 2) for c in range(3)]
        flow_two = [column(flow, c, 2) for c in range(3)]
        distant = [column(source, c, 3) for c in range(3)]
        carry = diffuse + advect * jnp.maximum(-direction * flow_two[1], 0.0)
        stretch = (0.5 * advect * direction) * near_two[1]
        term = [carry * distant[c] + stretch * column(flow, c, 3) for c in range(3)]
        term[0] = term[0] - bend * distant[1]
        term[1] = term[1] + bend * distant[0]
        for c in range(3):
            put(c, column(source, c, 1))
            put(3 + c, column(flow, c, 1))
            put(6 + c, near_two[c])
            put(9 + c, flow_two[c])
            put(12 + c, term[c])
    for depth in (1, 2):
        wall = facing(lambda q: reflect[pl.ds(q, 1), :], depth)
        side[pl.ds(side_wall + depth - 1, 1), :] = wall
        diagonal[pl.ds(diagonal_wall + depth - 1, 1), :] = wall

    for c in range(6):
        own, far = (field, far_field) if c < 3 else (velocity, far_flow)
        parts = []
        for source in (own, far):
            part = jnp.zeros((8, 128), jnp.float32)
            for r in range(8):
                part = jnp.where(
                    slot == r, pltpu.roll(layer(source, c % 3, r), (8 * r + 4) % 128, 1), part
                )
            parts.append(part)
        low = jnp.where(top == 0, parts[0], parts[1])
        high = jnp.where(top == 0, parts[1], parts[0])
        strip[pl.ds(8 * c, 8), :] = jnp.where(slot < 8, low, pltpu.roll(high, 64, 1))
    for depth in (1, 2):
        edge = facing(lambda q: strip[pl.ds(q, 6, stride=8), :], depth)
        side[pl.ds(side_strip + 8 * (depth - 1), 6), :] = edge
        diagonal[pl.ds(8 * (depth - 1), 6), :] = edge
    diagonal[pl.ds(16, 6), :] = jnp.where(
        upper, strip[pl.ds(0, 6, stride=8), :], strip[pl.ds(7, 6, stride=8), :]
    )

    def inner_cell(own, far, start, count, step):
        rows = pl.ds(start, count, stride=step)
        return jnp.where(top == 0, own[rows, :], far[rows, :])

    for place, (r, depth) in enumerate(((0, 1), (0, 2), (1, 1))):
        for part, (own, far) in enumerate(((field, far_field), (velocity, far_flow))):
            side[pl.ds(side_axis + 8 * place + 3 * part, 3), :] = jnp.where(
                upper,
                inner_cell(own, far, r * 8 + depth - 1, 3, 64),
                inner_cell(own, far, r * 8 + 8 - depth, 3, 64),
            )
    carry = (diffuse * 2.0 / 1.5) - advect * jnp.minimum(layer(velocity, 0, 1), 0.0)
    stretch = (0.5 * advect) * layer(field, 0, 1)
    for c in range(3):
        for r in range(2):
            turn[pl.ds(8 * (6 * r + c), 8), :] = layer(field, c, r)
            turn[pl.ds(8 * (6 * r + 3 + c), 8), :] = layer(velocity, c, r)
        turn[pl.ds(8 * (12 + c), 8), :] = carry * layer(field, c, 2) + stretch * layer(
            velocity, c, 2
        )
    strip[pl.ds(48, 8), :] = reflect[...]


def other_corner(side, first, step):
    top = lax.axis_index("row")
    low = side[pl.ds(8 * tiles + first + step, 6, stride=8), :]
    high = side[pl.ds(first + 7 - step, 6, stride=8), :]
    return jnp.where(top == 0, low, high)


def share_kernel(side, turn, opposite, diagonal, out):
    top = lax.axis_index("row")
    half = pl.multiple_of((1 - top) * (8 * tiles), 8)
    out[pl.ds(0, 8 * tiles), :] = side[pl.ds(half, 8 * tiles), :]
    for place, (first, step) in enumerate(((0, 0), (48, 0), (0, 1))):
        low = side[pl.ds(first + 7 - step, 6, stride=8), :]
        high = side[pl.ds(8 * tiles + first + step, 6, stride=8), :]
        out[pl.ds(share_corner + 8 * place, 6), :] = jnp.where(top == 0, low, high)
    out[pl.ds(share_rest, side_length - side_wall), :] = side[
        pl.ds(side_wall, side_length - side_wall), :
    ]
    out[pl.ds(share_turn, 8 * tiles), :] = turn[...]
    out[pl.ds(share_strip, strip_length), :] = opposite[...]
    out[pl.ds(share_diagonal, diagonal_length), :] = diagonal[...]


def compact_kernel(
    field, velocity, far_field, far_flow, reflect, strip, side, diagonal, opposite, shared,
    basis, gram, message, advanced, cells, walls, line, first, second, edge, edge_flow, table,
):
    top = lax.axis_index("row")
    low_half = top == 0
    upper = faces_up()
    mine_low = lax.axis_index("gz") == 0

    def both(own, other):
        return jnp.where(upper, other, own), jnp.where(upper, own, other)

    own_half = pl.multiple_of(top * (8 * tiles), 8)

    def tile_pair(tile):
        return both(
            side[pl.ds(pl.multiple_of(own_half + 8 * tile, 8), 8), :], shared[pl.ds(8 * tile, 8), :]
        )

    def rest_pair(start, count):
        return both(
            side[pl.ds(start, count), :], shared[pl.ds(share_rest + start - side_wall, count), :]
        )

    def diagonal_pair(start, count):
        return both(
            diagonal[pl.ds(start, count), :], shared[pl.ds(share_diagonal + start, count), :]
        )

    behind = [shared[pl.ds(share_turn + 8 * tile, 8), :] for tile in range(tiles)]
    nothing = jnp.zeros((8, 128), jnp.float32)
    for c in range(6):
        source, far = (field, far_field) if c < 3 else (velocity, far_flow)
        sign = signs[c % 3]
        for r in range(8):
            cells[pl.ds(row_of(c, r + 3), 8), :] = layer(source, c % 3, r)
        for w in range(window):
            cells[pl.ds(row_of(c, w) + 8, 8), :] = nothing
        for w in range(3):
            ghost = sign * behind[6 * (2 - w) + c] if w > 0 else 0.0
            cells[pl.ds(row_of(c, w), 8), :] = jnp.where(low_half, ghost, layer(far, c % 3, 5 + w))
            cells[pl.ds(row_of(c, 11 + w), 8), :] = jnp.where(low_half, layer(far, c % 3, w), 0.0)
        for depth in range(2):
            below, above = tile_pair(6 * depth + c)
            cells[pl.ds(row_of(c, 3) + 15 - depth, 8, stride=sub), :] = below
            cells[pl.ds(row_of(c, 3) + 8 + depth, 8, stride=sub), :] = above
    flip = lax.broadcasted_iota(jnp.int32, (6, 128), 0)
    flip = jnp.where((flip == 2) | (flip == 5), 1.0, -1.0)
    for place, (w, first_row, step, depth) in enumerate(((2, 0, 0, 0), (2, 48, 0, 1), (1, 0, 1, 0))):
        axis_high, axis_low = rest_pair(side_axis + 8 * place, 6)
        below, above = both(
            other_corner(side, first_row, step), shared[pl.ds(share_corner + 8 * place, 6), :]
        )
        for axis_part, other, q in ((axis_low, below, 15 - depth), (axis_high, above, 8 + depth)):
            low = pl.ds(row_of(0, w) + q, 6, stride=window * sub)
            high = pl.ds(row_of(0, 13 - w) + q, 6, stride=window * sub)
            cells[low, :] = jnp.where(low_half, flip * axis_part, other)
            cells[high, :] = jnp.where(low_half, other, 0.0)

    slot, inside = lanes(sub) // 8, lanes(sub) % 8
    axial_strip = [
        jnp.where(
            low_half, opposite[pl.ds(8 * tile, 8), :], shared[pl.ds(share_strip + 8 * tile, 8), :]
        )
        for tile in range(7)
    ]
    own_side = (inside < 4) == mine_low

    def merge(own, other):
        return jnp.where(own_side[: own.shape[0]], own, other)

    for part, (tile, pair) in enumerate(
        ((reflect[...], rest_pair(side_wall, 2)), (axial_strip[6], diagonal_pair(diagonal_wall, 2)))
    ):
        below, above = pair
        base = sub * part
        walls[pl.ds(base, 8), :] = tile
        walls[pl.ds(base + 8, 8), :] = nothing
        walls[pl.ds(base + 8, 2), :] = above
        walls[pl.ds(base + 15, 1), :] = below[0:1]
        walls[pl.ds(base + 14, 1), :] = below[1:2]
    factor = merge(
        pltpu.roll(walls[pl.ds(0, sub), :], 84, 1), pltpu.roll(walls[pl.ds(sub, sub), :], 84, 1)
    )

    for c in range(6):
        own = strip[pl.ds(8 * c, 8), :]
        line[pl.ds(sub * c, 8), :] = merge(own, axial_strip[c])
        line[pl.ds(sub * c + 8, 8), :] = nothing
    for depth in (1, 2):
        below, above = rest_pair(side_strip + 8 * (depth - 1), 6)
        beyond_below, beyond_above = diagonal_pair(8 * (depth - 1), 6)
        line[pl.ds(16 - depth, 6, stride=sub), :] = merge(below, beyond_below)
        line[pl.ds(7 + depth, 6, stride=sub), :] = merge(above, beyond_above)
    axis_high, axis_low = diagonal_pair(16, 6)
    combined = []
    for c in range(6):
        value = line[pl.ds(sub * c, sub), :]
        combined.append(jnp.where(low_half, pltpu.roll(value, 16, 1), pltpu.roll(value, 80, 1)))
    for c in range(6):
        sign = signs[c % 3]
        across = shared[pl.ds(share_strip + 8 * c, 8), :]
        own = jnp.where(
            slot[:8] == 1,
            pltpu.roll(behind[c], 12, 1),
            pltpu.roll(behind[6 + c], 4, 1),
        )
        other = jnp.where(slot[:8] == 1, pltpu.roll(across, 8, 1), pltpu.roll(across, 120, 1))
        line[pl.ds(sub * c, 8), :] = sign * merge(own, other)
        line[pl.ds(sub * c + 8, 8), :] = nothing
        line[pl.ds(sub * c + 8, 1), :] = sign * pltpu.roll(axis_high, 8, 1)[c : c + 1]
        line[pl.ds(sub * c + 15, 1), :] = sign * pltpu.roll(axis_low, 8, 1)[c : c + 1]
        ghost = line[pl.ds(sub * c, sub), :]
        combined[c] = jnp.where(jnp.logical_and(slot < 2, low_half), ghost, combined[c])
    combined.append(factor)
    ghosts = [jnp.where(low_half, signs[c] * behind[12 + c], 0.0) for c in range(3)]
    lows, highs = zip(*[tile_pair(12 + c) for c in range(3)])
    march(
        [combined], ghosts, lows, highs, walls.at[pl.ds(0, sub), :], cells, basis, gram, message,
        advanced, first, second, edge, edge_flow, table,
    )


def gram_place(m, n):
    return 16 + m * (m + 1) // 2 + n


def gram_kernel(basis, out):
    count = basis.shape[0] // 192
    spot = lanes(1)
    line = jnp.zeros((1, 128), jnp.float32)
    for m in range(count):
        sums = [jnp.zeros((8, 128), jnp.float32) for _ in range(m + 1)]
        for tile in range(24):
            value = basis[pl.ds(192 * m + 8 * tile, 8), :]
            for n in range(m + 1):
                sums[n] += value * basis[pl.ds(192 * n + 8 * tile, 8), :]
        for n in range(m + 1):
            total = jnp.sum(jnp.sum(sums[n], axis=0, keepdims=True), axis=1, keepdims=True)
            line = jnp.where(spot == gram_place(m, n), total, line)
    out[...] = line


def finish_kernel(cell_count, messages, advanced, basis, out, hessenberg):
    count = basis.shape[0] // 192
    total = messages[0]
    for device in range(1, messages.shape[0]):
        total = total + messages[device]

    def entry(index):
        return jnp.broadcast_to(total[:, index : index + 1], (8, 128))

    pending = [entry(m) for m in range(count)]
    energy = entry(count)
    weights = []
    for m in range(count):
        diagonal = entry(gram_place(m, m))
        weight = pending[m] / diagonal
        weights.append(weight)
        energy = energy - weight * (2.0 * pending[m] - weight * diagonal)
        for n in range(m + 1, count):
            pending[n] = pending[n] - weight * entry(gram_place(n, m))
    spread = jnp.sqrt(jnp.maximum(energy, 0.0) / cell_count + epsilon)
    scale = 1.0 / spread
    for tile in range(24):
        rows = pl.ds(8 * tile, 8)
        value = advanced[rows, :]
        for m in range(count):
            value = value - weights[m] * basis[pl.ds(192 * m + 8 * tile, 8), :]
        out[rows, :] = value * scale
    for m in range(count):
        hessenberg[m] = weights[m][0, 0]
    hessenberg[count] = spread[0, 0]


def shift(value, axis, step):
    count = lax.axis_size(axis)
    return lax.ppermute(value, axis, [(i, (i + step) % count) for i in range(count)])


def march_scratch():
    return [
        shape(3 * window * sub, 128),
        shape(3 * window * sub, 128),
        shape(3 * sub, 128),
        shape(3 * sub, 128),
        shape(kinds_of_coefficient * 12 * sub, 128),
    ]


def general_plan(field, velocity, basis, wall_region, wall_conductance):
    loop = lax.axis_size("phi")
    ends = lax.axis_size("gz")
    halves = lax.axis_size("row")
    fold = loop == 4
    many = ends > 2
    vectors = basis.shape[0]
    field_rows = field.reshape(192, 128)
    flow_rows = velocity.reshape(192, 128)
    swap = [(0, 1), (1, 0)]
    far_field = lax.ppermute(field_rows, "row", swap)
    far_flow = lax.ppermute(flow_rows, "row", swap)
    field_rows, flow_rows, basis_rows = near(
        field_rows, flow_rows, basis.reshape(vectors * 192, 128)
    )
    inner = pl.pallas_call(
        inner_kernel, in_specs=vmem(2), out_specs=vmem(1)[0], out_shape=shape(8 * tiles, 128)
    )(field_rows, flow_rows)
    half = loop // 2
    turned = []
    for p in range(loop):
        for r in range(halves):
            turned.append((p * halves + r, ((p + half) % loop if r == 0 else p) * halves + r))
    behind = lax.ppermute(inner, ("phi", "row"), turned)
    far_field, far_flow = near(far_field, far_flow)
    side = side_rows if fold else axis_row
    packed = pl.pallas_call(
        functools.partial(sides_kernel, fold),
        in_specs=[pl.BlockSpec(memory_space=pltpu.SMEM)] + vmem(5),
        out_specs=vmem(3 if fold else 5),
        out_shape=[shape(side, 128), shape(side, 128), shape(8, 128)]
        + ([] if fold else [shape(24, 128)] * 2),
    )(wall_conductance, wall_region, field_rows, flow_rows, far_field, far_flow)
    up, down, reflect = packed[:3]
    below = shift(up, "phi", 1)
    above = shift(down, "phi", -1)
    corners = []
    if not fold:
        corners = [shift(packed[3], "phi", half + 1), shift(packed[4], "phi", half - 1)]
    gram = pl.pallas_call(
        gram_kernel, in_specs=vmem(1), out_specs=vmem(1)[0], out_shape=shape(1, 128)
    )(basis_rows)
    below, above, behind, gram, *corners = lax.optimization_barrier(
        (below, above, behind, gram, *corners)
    )
    below, above, behind, gram, *corners = near(below, above, behind, gram, *corners)
    walls, strip, cells = pl.pallas_call(
        functools.partial(window_kernel, fold),
        in_specs=vmem(8 + len(corners)),
        out_specs=vmem(3),
        out_shape=[shape(sub, 128), shape(6 * sub, 128), shape(6 * window * sub, 128)],
    )(field_rows, flow_rows, far_field, far_flow, below, above, behind, reflect, *corners)
    if many:
        up_pairs = [(i, i + 1) for i in range(ends - 1)]
        others = [
            lax.ppermute(strip, "gz", up_pairs),
            lax.ppermute(strip, "gz", [(b, a) for a, b in up_pairs]),
        ]
    else:
        others = [lax.ppermute(strip, "gz", swap)]
    walls, strip, cells, *others = near(walls, strip, cells, *others)
    devices = lax.axis_size(("phi", "gz", "row"))
    return pl.pallas_call(
        functools.partial(stage_kernel, many),
        in_specs=vmem(8 + len(others)),
        out_specs=vmem(2),
        out_shape=[shape(devices, 1, 128), shape(192, 128)],
        scratch_shapes=march_scratch(),
    )(below, above, behind, walls, strip, *others, cells, basis_rows, gram)


def compact_plan(field, velocity, basis, wall_region, wall_conductance):
    vectors = basis.shape[0]
    field_rows = field.reshape(192, 128)
    flow_rows = velocity.reshape(192, 128)
    axes = ("phi", "gz", "row")
    devices = lax.axis_size(axes)

    def exchange(value, partner):
        pairs = []
        for p in range(4):
            for g in range(2):
                for r in range(2):
                    q, h, t = partner(p, g, r)
                    pairs.append(((p * 2 + g) * 2 + r, (q % 4 * 2 + h) * 2 + t))
        return lax.ppermute(value, axes, pairs)

    def beside(p, r):
        return p + 1 if (p + r) % 2 == 0 else p - 1

    swap = [(0, 1), (1, 0)]
    far_field = lax.ppermute(field_rows, "row", swap)
    far_flow = lax.ppermute(flow_rows, "row", swap)
    reflect, field_rows, flow_rows = pl.pallas_call(
        load_kernel,
        in_specs=[pl.BlockSpec(memory_space=pltpu.SMEM)] + vmem(3),
        out_specs=vmem(3),
        out_shape=[shape(8, 128), shape(192, 128), shape(192, 128)],
    )(wall_conductance, wall_region, field_rows, flow_rows)
    blocks = near(field_rows, flow_rows, far_field, far_flow, reflect)
    side, turn, diagonal, strip = pl.pallas_call(
        send_kernel,
        in_specs=vmem(5),
        out_specs=vmem(4),
        out_shape=[
            shape(side_length, 128),
            shape(8 * tiles, 128),
            shape(diagonal_length, 128),
            shape(strip_length, 128),
        ],
    )(*blocks)
    opposite = exchange(strip, lambda p, g, r: (p + 2, 1 - g, 1) if r == 0 else (p, 1 - g, 0))
    turn = exchange(turn, lambda p, g, r: (p + 2, g, 1) if r == 0 else (p, g, 0))
    diagonal = exchange(diagonal, lambda p, g, r: (beside(p, r), 1 - g, r))
    side = exchange(side, lambda p, g, r: (beside(p, r), g, r))
    (basis_rows,) = near(basis.reshape(vectors * 192, 128))
    gram = pl.pallas_call(
        gram_kernel, in_specs=vmem(1), out_specs=vmem(1)[0], out_shape=shape(1, 128)
    )(basis_rows)
    side, turn, diagonal, opposite, gram = near(
        *lax.optimization_barrier((side, turn, diagonal, opposite, gram))
    )
    share = pl.pallas_call(
        share_kernel, in_specs=vmem(4), out_specs=vmem(1)[0], out_shape=shape(share_length, 128)
    )(side, turn, opposite, diagonal)
    shared = lax.ppermute(share, "row", swap)
    strip, shared = near(strip, shared)
    return pl.pallas_call(
        compact_kernel,
        in_specs=vmem(12),
        out_specs=vmem(2),
        out_shape=[shape(devices, 1, 128), shape(192, 128)],
        scratch_shapes=[
            shape(6 * window * sub, 128),
            shape(2 * sub, 128),
            shape(6 * sub, 128),
        ]
        + march_scratch(),
    )(*blocks, strip, side, diagonal, opposite, shared, basis_rows, gram)


def local(field, velocity, basis, wall_region, wall_conductance):
    axes = ("phi", "gz", "row")
    vectors = basis.shape[0]
    devices = lax.axis_size(axes)
    compact = tuple(lax.axis_size(axis) for axis in axes) == (4, 2, 2)
    plan = compact_plan if compact else general_plan
    message, advanced = plan(field, velocity, basis, wall_region, wall_conductance)
    (basis_rows,) = near(basis.reshape(vectors * 192, 128))
    messages = lax.all_to_all(message, axes, 0, 0, tiled=True)
    messages, advanced = near(messages, advanced)
    out, hessenberg = pl.pallas_call(
        functools.partial(finish_kernel, float(field.size * devices)),
        in_specs=vmem(3),
        out_specs=vmem(1) + [pl.BlockSpec(memory_space=pltpu.SMEM)],
        out_shape=[
            jax.ShapeDtypeStruct((192, 128), jnp.float32),
            jax.ShapeDtypeStruct((vectors + 1,), jnp.float32),
        ],
    )(messages, advanced, basis_rows)
    return out.reshape(field.shape), hessenberg


def solution(mesh):
    return jax.shard_map(
        local,
        mesh=mesh,
        in_specs=(
            P("groups", "row", "phi", "gz"),
            P("groups", "row", "phi", "gz"),
            P("groups", None, "row", "phi", "gz"),
            P(("groups", "phi"), "gz"),
            P("groups"),
        ),
        out_specs=(P("groups", "row", "phi", "gz"), P("groups")),
        check_vma=False,
    )
```

```python
import functools

import jax
import jax.numpy as jnp
import numpy as np
from jax import lax
from jax.experimental import pallas as pl
from jax.experimental.pallas import tpu as pltpu
from jax.sharding import PartitionSpec as P

advect = 0.2
diffuse = 0.1
epsilon = 1e-06
signs = (-1.0, -1.0, 1.0)
wall_signs = (-1.0, 1.0, 1.0)

tiles = 15
wall_row = 8 * tiles
corner_row = wall_row + 8
axis_row = corner_row + 24
side_rows = axis_row + 24
window = 14
sub = 16
kinds_of_coefficient = 15


def row_of(component, w):
    return (component * window + w) * sub


def vmem(count):
    return [pl.BlockSpec(memory_space=pltpu.VMEM)] * count


def shape(*dims):
    return pltpu.VMEM(dims, jnp.float32)


def near(*values):
    return [pltpu.with_memory_space_constraint(value, pltpu.VMEM) for value in values]


def lanes(rows):
    return lax.broadcasted_iota(jnp.int32, (rows, 128), 1)


def layer(source, c, r):
    return source[pl.ds(c * 64 + r * 8, 8), :]


def inner_kernel(field, velocity, inner):
    middle = lax.axis_index("row").astype(jnp.float32) * 8.0 + 1.5
    pull = diffuse * (middle + 0.5) / jnp.full((8, 128), middle)
    carry = pull - advect * jnp.minimum(layer(velocity, 0, 1), 0.0)
    stretch = (0.5 * advect) * layer(field, 0, 1)
    for c in range(3):
        inner[pl.ds(8 * c, 8), :] = layer(field, c, 0)
        inner[pl.ds(8 * (3 + c), 8), :] = layer(velocity, c, 0)
        inner[pl.ds(8 * (6 + c), 8), :] = layer(field, c, 1)
        inner[pl.ds(8 * (9 + c), 8), :] = layer(velocity, c, 1)
        inner[pl.ds(8 * (12 + c), 8), :] = carry * layer(field, c, 2) + stretch * layer(
            velocity, c, 2
        )


def sides_kernel(
    fold, conductance, region, field, velocity, far_field, far_flow, up, down, reflect, *corners
):
    top = lax.axis_index("row")
    kinds = region[...]
    value = jnp.zeros(kinds.shape, jnp.float32)
    for kind in range(conductance.shape[0]):
        value = jnp.where(kinds == kind, conductance[kind], value)
    reflect[...] = 1.0 - 2.0 * value / (1.0 + value)

    def column(source, c, q):
        return source[pl.ds(c * 64 + q, 8, stride=8), :]

    def cell(source, r, q):
        return source[pl.ds(r * 8 + q, 3, stride=64), :]

    radius = lax.broadcasted_iota(jnp.int32, (8, 128), 0).astype(jnp.float32)
    turn = diffuse / (radius + (top.astype(jnp.float32) * 8.0 + 0.5))
    for out, (one, two, three), direction in ((up, (7, 6, 5), -1.0), (down, (0, 1, 2), 1.0)):
        for c in range(3):
            out[pl.ds(8 * c, 8), :] = column(field, c, one)
            out[pl.ds(8 * (3 + c), 8), :] = column(velocity, c, one)
            out[pl.ds(8 * (6 + c), 8), :] = column(field, c, two)
            out[pl.ds(8 * (9 + c), 8), :] = column(velocity, c, two)
        speed = column(velocity, 1, two)
        carry = diffuse + advect * jnp.maximum(-direction * speed, 0.0)
        stretch = (0.5 * advect * direction) * column(field, 1, two)
        far = [column(field, c, three) for c in range(3)]
        term = [carry * far[c] + stretch * column(velocity, c, three) for c in range(3)]
        term[0] = term[0] - (direction * turn) * far[1]
        term[1] = term[1] + (direction * turn) * far[0]
        for c in range(3):
            out[pl.ds(8 * (12 + c), 8), :] = term[c]
        out[pl.ds(wall_row, 1), :] = reflect[pl.ds(one, 1), :]
        out[pl.ds(wall_row + 1, 1), :] = reflect[pl.ds(two, 1), :]
        for place, (r, q) in enumerate(((0, one), (0, two), (1, one))):
            for part, source in enumerate((far_field, far_flow)):
                out[pl.ds(corner_row + 8 * place + 3 * part, 3), :] = jnp.where(
                    top == 0, cell(source, r, q), cell(source, 7 - r, q)
                )
    for side, (one, two) in ((0, (7, 6)), (1, (0, 1))):
        if fold:
            out, base = (down, up)[side], axis_row
        else:
            out, base = corners[side], 0
        for place, (r, q) in enumerate(((0, one), (0, two), (1, one))):
            out[pl.ds(base + 8 * place, 3), :] = cell(field, r, q)
            out[pl.ds(base + 8 * place + 3, 3), :] = cell(velocity, r, q)


def window_kernel(
    fold, field, velocity, far_field, far_flow, below, above, behind, reflect, *rest
):
    if fold:
        axis_low, axis_high, axis_base = above, below, axis_row
    else:
        axis_low, axis_high, axis_base = rest[0], rest[1], 0
    walls, strip, cells = rest[-3:]
    low_half = lax.axis_index("row") == 0
    nothing = jnp.zeros((8, 128), jnp.float32)
    for c in range(6):
        source, far = (field, far_field) if c < 3 else (velocity, far_flow)
        sign = signs[c % 3]
        for r in range(8):
            cells[pl.ds(row_of(c, r + 3), 8), :] = layer(source, c % 3, r)
        for w in range(window):
            cells[pl.ds(row_of(c, w) + 8, 8), :] = nothing
        for w in range(3):
            ghost = sign * behind[pl.ds(48 * (2 - w) + 8 * c, 8), :] if w > 0 else 0.0
            cells[pl.ds(row_of(c, w), 8), :] = jnp.where(low_half, ghost, layer(far, c % 3, 5 + w))
            cells[pl.ds(row_of(c, 11 + w), 8), :] = jnp.where(low_half, layer(far, c % 3, w), 0.0)
        for depth in range(2):
            place = pl.ds(48 * depth + 8 * c, 8)
            cells[pl.ds(row_of(c, 3) + 15 - depth, 8, stride=sub), :] = below[place, :]
            cells[pl.ds(row_of(c, 3) + 8 + depth, 8, stride=sub), :] = above[place, :]
    flip = lax.broadcasted_iota(jnp.int32, (6, 128), 0)
    flip = jnp.where((flip == 2) | (flip == 5), 1.0, -1.0)
    for place, (w, step) in enumerate(((2, 0), (2, 1), (1, 0))):
        for axis_source, source, q in ((axis_low, below, 15 - step), (axis_high, above, 8 + step)):
            ghost = flip * axis_source[pl.ds(axis_base + 8 * place, 6), :]
            other = source[pl.ds(corner_row + 8 * place, 6), :]
            low = jnp.where(low_half, ghost, other)
            high = jnp.where(low_half, other, 0.0)
            for c in range(6):
                cells[pl.ds(row_of(c, w) + q, 1), :] = low[c : c + 1]
                cells[pl.ds(row_of(c, 13 - w) + q, 1), :] = high[c : c + 1]
    walls[pl.ds(0, 8), :] = reflect[...]
    walls[pl.ds(8, 8), :] = nothing
    walls[pl.ds(8, 2), :] = above[pl.ds(wall_row, 2), :]
    walls[pl.ds(15, 1), :] = below[pl.ds(wall_row, 1), :]
    walls[pl.ds(14, 1), :] = below[pl.ds(wall_row + 1, 1), :]
    slot = lanes(sub) // 8
    for c in range(6):
        packed = jnp.where(slot == 12, pltpu.roll(walls[...], 100, 1), 0.0)
        for w in range(1, window - 1):
            row = cells[pl.ds(row_of(c, w), sub), :]
            packed = jnp.where(slot == w - 1, pltpu.roll(row, (8 * (w - 1) + 4) % 128, 1), packed)
        strip[pl.ds(sub * c, sub), :] = packed


def back(value, axis, step=1):
    return pltpu.roll(value, step, axis)


def ahead(value, axis, step=1):
    return pltpu.roll(value, value.shape[axis] - step, axis)


def rate(center, sides, coefficients):
    inward, outward, before, after, under, over = sides
    pull_in, pull_out, pull_before, pull_after, pull_under, pull_over, mix, turn = coefficients
    result = []
    for c in range(3):
        value = (
            (pull_in * inward[c] + pull_out * outward[c])
            + (pull_before * before[c] + pull_after * after[c])
            + (pull_under * under[c] + pull_over * over[c])
        )
        for d in range(3):
            value = value + mix[c][d] * center[d]
        result.append(value)
    result[0] = result[0] - turn * (after[1] - before[1])
    result[1] = result[1] + turn * (after[0] - before[0])
    return result


def coefficients_of(speed, sides, sense, inner_pull, outer_pull, bend, inverse_square, turn):
    inward, outward, before, after, under, over = sides
    radial, around, axial = speed
    around_here = sense * around
    pulls = (
        inner_pull + advect * jnp.maximum(radial, 0.0),
        outer_pull - advect * jnp.minimum(radial, 0.0),
        diffuse + advect * jnp.maximum(around_here, 0.0),
        diffuse - advect * jnp.minimum(around_here, 0.0),
        diffuse + advect * jnp.maximum(axial, 0.0),
        diffuse - advect * jnp.minimum(axial, 0.0),
    )
    keep = -6.0 * diffuse - advect * (jnp.abs(radial) + jnp.abs(around) + jnp.abs(axial))
    half = 0.5 * advect
    mix = []
    for c in range(3):
        mix.append(
            [
                half * (outward[c] - inward[c]),
                (half * sense) * (after[c] - before[c]),
                half * (over[c] - under[c]),
            ]
        )
    mix[0][0] = mix[0][0] + (keep - diffuse * inverse_square)
    mix[1][1] = mix[1][1] + (keep - diffuse * inverse_square) + bend * radial
    mix[1][0] = mix[1][0] - bend * around
    mix[2][2] = mix[2][2] + keep
    return pulls + (mix, turn)


def stage_kernel(many, below, above, behind, walls, strip, *rest):
    others = rest[: 2 if many else 1]
    cells, basis, gram, message, advanced, first, second, edge, edge_flow, table = rest[len(others) :]
    has_high = lax.axis_index("gz") < lax.axis_size("gz") - 1
    inside = lanes(sub) % 8
    mine = [strip[pl.ds(sub * c, sub), :] for c in range(6)]
    if many:
        from_low = [others[0][pl.ds(sub * c, sub), :] for c in range(6)]
        from_high = [others[1][pl.ds(sub * c, sub), :] for c in range(6)]
        strips = [
            [jnp.where(inside < 4, b, a) for a, b in zip(mine, from_low)],
            [jnp.where(inside < 4, a, b) for a, b in zip(mine, from_high)],
        ]
    else:
        other = [others[0][pl.ds(sub * c, sub), :] for c in range(6)]
        strips = [[jnp.where((inside < 4) == has_high, a, b) for a, b in zip(mine, other)]]
    strips = [line + [ahead(line[0], 1, 16)] for line in strips]
    low_half = lax.axis_index("row") == 0
    ghosts = [jnp.where(low_half, signs[c] * layer(behind, 0, 12 + c), 0.0) for c in range(3)]
    lows = [layer(below, 0, 12 + c) for c in range(3)]
    highs = [layer(above, 0, 12 + c) for c in range(3)]
    march(
        strips, ghosts, lows, highs, walls, cells, basis, gram, message, advanced,
        first, second, edge, edge_flow, table,
    )


def march(
    strips, ghosts, lows, highs, walls, cells, basis, gram, message, advanced,
    first, second, edge, edge_flow, table,
):
    top = lax.axis_index("row")
    low_half = top == 0
    place = lax.axis_index("gz")
    has_low = place > 0
    has_high = place < lax.axis_size("gz") - 1
    lane = lanes(sub)
    slot = lane // 8

    number = (slot - 2).astype(jnp.float32) + top.astype(jnp.float32) * 8.0 + 0.5
    inverse = 1.0 / number
    strip_scalars = (
        jnp.where(number < 0.0, -1.0, 1.0),
        diffuse * (number - 0.5) * inverse,
        diffuse * (number + 0.5) * inverse,
        advect * inverse,
        inverse * inverse,
        diffuse * jnp.abs(inverse),
    )
    strip_wall = jnp.logical_and(slot == 10, top == 1)

    def strip_sides(values):
        return (
            [back(v, 1, 8) for v in values],
            [ahead(v, 1, 8) for v in values],
            [back(v, 0) for v in values],
            [ahead(v, 0) for v in values],
            [back(v, 1) for v in values],
            [ahead(v, 1) for v in values],
        )

    def walled(values, factors):
        return [jnp.where(strip_wall, f * back(v, 1, 8), v) for v, f in zip(values, factors)]

    levels = []
    flows = []
    for line in strips:
        factor = line[6]
        flow = walled(line[3:6], wall_signs)
        flows.append(flow)
        weights = coefficients_of(flow, strip_sides(flow), *strip_scalars)
        start = walled(line[:3], [factor] * 3)
        one = rate(start, strip_sides(start), weights)
        one = walled([a + b for a, b in zip(start, one)], [factor] * 3)
        two = rate(one, strip_sides(one), weights)
        two = [0.75 * s + 0.25 * (a + b) for s, a, b in zip(start, one, two)]
        levels.append((start, one, two))

    inner_side = lane % 8 < 4

    def store_edges(target, low_values, high_values):
        for c in range(3):
            low = jnp.where(has_low, back(low_values[c], 1), 0.0)
            high = jnp.where(has_high, ahead(high_values[c], 1), 0.0)
            target[pl.ds(sub * c, sub), :] = jnp.where(inner_side, high, low)

    def axial(value, source, c, w, start, size):
        ghost = source[pl.ds(sub * c + start, size), :]
        ghost = pltpu.roll(ghost, 128 - (8 * (w - 1) + 4), 1)
        at = lane[:size]
        return (
            jnp.where(at == 0, ghost, back(value, 1)),
            jnp.where(at == 127, ghost, ahead(value, 1)),
        )

    def pick(low, high):
        return jnp.where(low_half, np.float32(low), np.float32(high))

    def scalars(w):
        options = []
        for half in range(2):
            r = half * 8 + (w - 3) + 0.5
            options.append(
                (
                    -1.0 if r < 0 else 1.0,
                    diffuse * (r - 0.5) / r,
                    diffuse * (r + 0.5) / r,
                    advect / r,
                    1.0 / (r * r),
                    diffuse / abs(r),
                )
            )
        return [pick(a, b) for a, b in zip(*options)]

    def read(source, c, w, start=0, size=sub):
        return source[pl.ds(row_of(c, w) + start, size), :]

    for c in range(6):
        last = read(cells, c, 10)
        factor = walls[...] if c < 3 else wall_signs[c - 3]
        cells[pl.ds(row_of(c, 11), sub), :] = jnp.where(low_half, read(cells, c, 11), factor * last)

    def surroundings(source, first_component, ends, w, start, size):
        center, sides = [], [[], [], [], [], [], []]
        for c in range(3):
            at = first_component + c
            whole = read(source, at, w)
            value = whole[:size]
            under, over = axial(value, ends, c, w, start, size)
            for side, part in zip(
                sides,
                (
                    read(source, at, w - 1, start, size),
                    read(source, at, w + 1, start, size),
                    back(whole, 0)[:size],
                    ahead(whole, 0)[:size],
                    under,
                    over,
                ),
            ):
                side.append(part)
            center.append(value)
        return center, sides

    def table_rows(kind, w, start, size):
        return pl.ds((kind * 12 + w - 1) * sub + start, size)

    def make_table(w):
        weights = coefficients_of(*surroundings(cells, 3, edge_flow, w, 0, sub), *scalars(w))
        flat = list(weights[:6]) + [value for row in weights[6] for value in row]
        if w not in (1, 12):
            for kind, value in enumerate(flat):
                table[table_rows(kind, w, 0, sub), :] = value
        return weights

    def stored_table(w, start, size):
        flat = [table[table_rows(kind, w, start, size), :] for kind in range(kinds_of_coefficient)]
        mix = [flat[6:9], flat[9:12], flat[12:15]]
        return tuple(flat[:6]) + (mix, scalars(w)[-1])

    def field_rate(source, w, start=0, size=sub, weights=None):
        center, sides = surroundings(source, 0, edge, w, start, size)
        return center, rate(center, sides, weights or stored_table(w, start, size))

    store_edges(edge_flow, flows[0], flows[-1])
    store_edges(edge, levels[0][0], levels[-1][0])
    for w in range(1, 13):
        center, change = field_rate(cells, w, weights=make_table(w))
        for c in range(3):
            first[pl.ds(row_of(c, w), sub), :] = center[c] + change[c]
    for c in range(3):
        low = pl.ds(row_of(c, 1), 8)
        first[low, :] = first[low, :] + ghosts[c]
        before = pl.ds(row_of(c, 3) + 14, 8, stride=sub)
        after = pl.ds(row_of(c, 3) + 9, 8, stride=sub)
        first[before, :] = first[before, :] + lows[c]
        first[after, :] = first[after, :] + highs[c]

    def close_wall(source):
        for c in range(3):
            source[pl.ds(row_of(c, 11), sub), :] = jnp.where(
                low_half, read(source, c, 11), walls[...] * read(source, c, 10)
            )

    close_wall(first)
    store_edges(edge, levels[0][1], levels[-1][1])
    for w in range(2, 12):
        center, change = field_rate(first, w)
        for c in range(3):
            second[pl.ds(row_of(c, w), sub), :] = 0.75 * read(cells, c, w) + 0.25 * (
                center[c] + change[c]
            )
    close_wall(second)
    store_edges(edge, levels[0][2], levels[-1][2])
    count = basis.shape[0] // 192
    sums = [jnp.zeros((8, 128), jnp.float32) for _ in range(count + 1)]
    for w in range(3, 11):
        center, change = field_rate(second, w, 0, 8)
        for c in range(3):
            rows = pl.ds(64 * c + 8 * (w - 3), 8)
            value = read(cells, c, w, 0, 8) / 3.0 + (2.0 / 3.0) * (center[c] + change[c])
            advanced[rows, :] = value
            for m in range(count):
                sums[m] += basis[pl.ds(192 * m + 64 * c + 8 * (w - 3), 8), :] * value
            sums[count] += value * value
    line = write_sums(jnp.broadcast_to(gram[...], (8, 128)), sums, range(count + 1))[:1]
    for device in range(message.shape[0]):
        message[device] = line


side_wall = 16 * tiles
side_strip = side_wall + 8
side_axis = side_strip + 16
side_length = side_axis + 24
diagonal_wall = 24
diagonal_length = 32
strip_length = 56
share_corner = 8 * tiles
share_rest = share_corner + 24
share_turn = share_rest + side_length - side_wall
share_strip = share_turn + 8 * tiles
share_diagonal = share_strip + strip_length
share_length = share_diagonal + diagonal_length


def faces_up():
    return (lax.axis_index("phi") + lax.axis_index("row")) % 2 == 0


def load_kernel(conductance, region, field, velocity, reflect, field_copy, flow_copy):
    kinds = region[...]
    value = jnp.zeros(kinds.shape, jnp.float32)
    for kind in range(conductance.shape[0]):
        value = jnp.where(kinds == kind, conductance[kind], value)
    reflect[...] = 1.0 - 2.0 * value / (1.0 + value)
    field_copy[...] = field[...]
    flow_copy[...] = velocity[...]


def send_kernel(field, velocity, far_field, far_flow, reflect, side, turn, diagonal, strip):
    top = lax.axis_index("row")
    upper = faces_up()
    slot = lanes(8) // 8

    def facing(load, depth):
        return jnp.where(upper, load(8 - depth), load(depth - 1))

    def column(source, c, depth):
        return facing(lambda q: source[pl.ds(c * 64 + q, 8, stride=8), :], depth)

    direction = jnp.where(upper, -1.0, 1.0)
    index = lax.broadcasted_iota(jnp.int32, (8, 128), 0).astype(jnp.float32)
    for source, flow, half in ((field, velocity, top), (far_field, far_flow, 1 - top)):
        base = half * (8 * tiles)

        def put(tile, value):
            side[pl.ds(pl.multiple_of(base + 8 * tile, 8), 8), :] = value

        bend = (diffuse * direction) / (index + (half.astype(jnp.float32) * 8.0 + 0.5))
        near_two = [column(source, c, 2) for c in range(3)]
        flow_two = [column(flow, c, 2) for c in range(3)]
        distant = [column(source, c, 3) for c in range(3)]
        carry = diffuse + advect * jnp.maximum(-direction * flow_two[1], 0.0)
        stretch = (0.5 * advect * direction) * near_two[1]
        term = [carry * distant[c] + stretch * column(flow, c, 3) for c in range(3)]
        term[0] = term[0] - bend * distant[1]
        term[1] = term[1] + bend * distant[0]
        for c in range(3):
            put(c, column(source, c, 1))
            put(3 + c, column(flow, c, 1))
            put(6 + c, near_two[c])
            put(9 + c, flow_two[c])
            put(12 + c, term[c])
    for depth in (1, 2):
        wall = facing(lambda q: reflect[pl.ds(q, 1), :], depth)
        side[pl.ds(side_wall + depth - 1, 1), :] = wall
        diagonal[pl.ds(diagonal_wall + depth - 1, 1), :] = wall

    for c in range(6):
        own, far = (field, far_field) if c < 3 else (velocity, far_flow)
        parts = []
        for source in (own, far):
            part = jnp.zeros((8, 128), jnp.float32)
            for r in range(8):
                part = jnp.where(
                    slot == r, pltpu.roll(layer(source, c % 3, r), (8 * r + 4) % 128, 1), part
                )
            parts.append(part)
        low = jnp.where(top == 0, parts[0], parts[1])
        high = jnp.where(top == 0, parts[1], parts[0])
        strip[pl.ds(8 * c, 8), :] = jnp.where(slot < 8, low, pltpu.roll(high, 64, 1))
    for depth in (1, 2):
        edge = facing(lambda q: strip[pl.ds(q, 6, stride=8), :], depth)
        side[pl.ds(side_strip + 8 * (depth - 1), 6), :] = edge
        diagonal[pl.ds(8 * (depth - 1), 6), :] = edge
    diagonal[pl.ds(16, 6), :] = jnp.where(
        upper, strip[pl.ds(0, 6, stride=8), :], strip[pl.ds(7, 6, stride=8), :]
    )

    def inner_cell(own, far, start, count, step):
        rows = pl.ds(start, count, stride=step)
        return jnp.where(top == 0, own[rows, :], far[rows, :])

    for place, (r, depth) in enumerate(((0, 1), (0, 2), (1, 1))):
        for part, (own, far) in enumerate(((field, far_field), (velocity, far_flow))):
            side[pl.ds(side_axis + 8 * place + 3 * part, 3), :] = jnp.where(
                upper,
                inner_cell(own, far, r * 8 + depth - 1, 3, 64),
                inner_cell(own, far, r * 8 + 8 - depth, 3, 64),
            )
    carry = (diffuse * 2.0 / 1.5) - advect * jnp.minimum(layer(velocity, 0, 1), 0.0)
    stretch = (0.5 * advect) * layer(field, 0, 1)
    for c in range(3):
        for r in range(2):
            turn[pl.ds(8 * (6 * r + c), 8), :] = layer(field, c, r)
            turn[pl.ds(8 * (6 * r + 3 + c), 8), :] = layer(velocity, c, r)
        turn[pl.ds(8 * (12 + c), 8), :] = carry * layer(field, c, 2) + stretch * layer(
            velocity, c, 2
        )
    strip[pl.ds(48, 8), :] = reflect[...]


def other_corner(side, first, step):
    top = lax.axis_index("row")
    low = side[pl.ds(8 * tiles + first + step, 6, stride=8), :]
    high = side[pl.ds(first + 7 - step, 6, stride=8), :]
    return jnp.where(top == 0, low, high)


def share_kernel(side, turn, opposite, diagonal, out):
    top = lax.axis_index("row")
    half = pl.multiple_of((1 - top) * (8 * tiles), 8)
    out[pl.ds(0, 8 * tiles), :] = side[pl.ds(half, 8 * tiles), :]
    for place, (first, step) in enumerate(((0, 0), (48, 0), (0, 1))):
        low = side[pl.ds(first + 7 - step, 6, stride=8), :]
        high = side[pl.ds(8 * tiles + first + step, 6, stride=8), :]
        out[pl.ds(share_corner + 8 * place, 6), :] = jnp.where(top == 0, low, high)
    out[pl.ds(share_rest, side_length - side_wall), :] = side[
        pl.ds(side_wall, side_length - side_wall), :
    ]
    out[pl.ds(share_turn, 8 * tiles), :] = turn[...]
    out[pl.ds(share_strip, strip_length), :] = opposite[...]
    out[pl.ds(share_diagonal, diagonal_length), :] = diagonal[...]


def compact_kernel(
    field, velocity, far_field, far_flow, reflect, strip, side, diagonal, opposite, shared,
    basis, gram, message, advanced, cells, walls, line, first, second, edge, edge_flow, table,
):
    top = lax.axis_index("row")
    low_half = top == 0
    upper = faces_up()
    mine_low = lax.axis_index("gz") == 0

    def both(own, other):
        return jnp.where(upper, other, own), jnp.where(upper, own, other)

    own_half = pl.multiple_of(top * (8 * tiles), 8)

    def tile_pair(tile):
        return both(
            side[pl.ds(pl.multiple_of(own_half + 8 * tile, 8), 8), :], shared[pl.ds(8 * tile, 8), :]
        )

    def rest_pair(start, count):
        return both(
            side[pl.ds(start, count), :], shared[pl.ds(share_rest + start - side_wall, count), :]
        )

    def diagonal_pair(start, count):
        return both(
            diagonal[pl.ds(start, count), :], shared[pl.ds(share_diagonal + start, count), :]
        )

    behind = [shared[pl.ds(share_turn + 8 * tile, 8), :] for tile in range(tiles)]
    nothing = jnp.zeros((8, 128), jnp.float32)
    for c in range(6):
        source, far = (field, far_field) if c < 3 else (velocity, far_flow)
        sign = signs[c % 3]
        for r in range(8):
            cells[pl.ds(row_of(c, r + 3), 8), :] = layer(source, c % 3, r)
        for w in range(window):
            cells[pl.ds(row_of(c, w) + 8, 8), :] = nothing
        for w in range(3):
            ghost = sign * behind[6 * (2 - w) + c] if w > 0 else 0.0
            cells[pl.ds(row_of(c, w), 8), :] = jnp.where(low_half, ghost, layer(far, c % 3, 5 + w))
            cells[pl.ds(row_of(c, 11 + w), 8), :] = jnp.where(low_half, layer(far, c % 3, w), 0.0)
        for depth in range(2):
            below, above = tile_pair(6 * depth + c)
            cells[pl.ds(row_of(c, 3) + 15 - depth, 8, stride=sub), :] = below
            cells[pl.ds(row_of(c, 3) + 8 + depth, 8, stride=sub), :] = above
    flip = lax.broadcasted_iota(jnp.int32, (6, 128), 0)
    flip = jnp.where((flip == 2) | (flip == 5), 1.0, -1.0)
    for place, (w, first_row, step, depth) in enumerate(((2, 0, 0, 0), (2, 48, 0, 1), (1, 0, 1, 0))):
        axis_high, axis_low = rest_pair(side_axis + 8 * place, 6)
        below, above = both(
            other_corner(side, first_row, step), shared[pl.ds(share_corner + 8 * place, 6), :]
        )
        for axis_part, other, q in ((axis_low, below, 15 - depth), (axis_high, above, 8 + depth)):
            low = pl.ds(row_of(0, w) + q, 6, stride=window * sub)
            high = pl.ds(row_of(0, 13 - w) + q, 6, stride=window * sub)
            cells[low, :] = jnp.where(low_half, flip * axis_part, other)
            cells[high, :] = jnp.where(low_half, other, 0.0)

    slot, inside = lanes(sub) // 8, lanes(sub) % 8
    axial_strip = [
        jnp.where(
            low_half, opposite[pl.ds(8 * tile, 8), :], shared[pl.ds(share_strip + 8 * tile, 8), :]
        )
        for tile in range(7)
    ]
    own_side = (inside < 4) == mine_low

    def merge(own, other):
        return jnp.where(own_side[: own.shape[0]], own, other)

    for part, (tile, pair) in enumerate(
        ((reflect[...], rest_pair(side_wall, 2)), (axial_strip[6], diagonal_pair(diagonal_wall, 2)))
    ):
        below, above = pair
        base = sub * part
        walls[pl.ds(base, 8), :] = tile
        walls[pl.ds(base + 8, 8), :] = nothing
        walls[pl.ds(base + 8, 2), :] = above
        walls[pl.ds(base + 15, 1), :] = below[0:1]
        walls[pl.ds(base + 14, 1), :] = below[1:2]
    factor = merge(
        pltpu.roll(walls[pl.ds(0, sub), :], 84, 1), pltpu.roll(walls[pl.ds(sub, sub), :], 84, 1)
    )

    for c in range(6):
        own = strip[pl.ds(8 * c, 8), :]
        line[pl.ds(sub * c, 8), :] = merge(own, axial_strip[c])
        line[pl.ds(sub * c + 8, 8), :] = nothing
    for depth in (1, 2):
        below, above = rest_pair(side_strip + 8 * (depth - 1), 6)
        beyond_below, beyond_above = diagonal_pair(8 * (depth - 1), 6)
        line[pl.ds(16 - depth, 6, stride=sub), :] = merge(below, beyond_below)
        line[pl.ds(7 + depth, 6, stride=sub), :] = merge(above, beyond_above)
    axis_high, axis_low = diagonal_pair(16, 6)
    combined = []
    for c in range(6):
        value = line[pl.ds(sub * c, sub), :]
        combined.append(jnp.where(low_half, pltpu.roll(value, 16, 1), pltpu.roll(value, 80, 1)))
    for c in range(6):
        sign = signs[c % 3]
        across = shared[pl.ds(share_strip + 8 * c, 8), :]
        own = jnp.where(
            slot[:8] == 1,
            pltpu.roll(behind[c], 12, 1),
            pltpu.roll(behind[6 + c], 4, 1),
        )
        other = jnp.where(slot[:8] == 1, pltpu.roll(across, 8, 1), pltpu.roll(across, 120, 1))
        line[pl.ds(sub * c, 8), :] = sign * merge(own, other)
        line[pl.ds(sub * c + 8, 8), :] = nothing
        line[pl.ds(sub * c + 8, 1), :] = sign * pltpu.roll(axis_high, 8, 1)[c : c + 1]
        line[pl.ds(sub * c + 15, 1), :] = sign * pltpu.roll(axis_low, 8, 1)[c : c + 1]
        ghost = line[pl.ds(sub * c, sub), :]
        combined[c] = jnp.where(jnp.logical_and(slot < 2, low_half), ghost, combined[c])
    combined.append(factor)
    ghosts = [jnp.where(low_half, signs[c] * behind[12 + c], 0.0) for c in range(3)]
    lows, highs = zip(*[tile_pair(12 + c) for c in range(3)])
    march(
        [combined], ghosts, lows, highs, walls.at[pl.ds(0, sub), :], cells, basis, gram, message,
        advanced, first, second, edge, edge_flow, table,
    )


def two_sum(a, b):
    total = a + b
    part = total - a
    return total, (a - (total - part)) + (b - part)


def split(a):
    scaled = 4097.0 * a
    high = scaled - (scaled - a)
    return high, a - high


def two_product(a, b, a_parts, b_parts):
    product = a * b
    (a_high, a_low), (b_high, b_low) = a_parts, b_parts
    rest = ((a_high * b_high - product) + a_high * b_low + a_low * b_high) + a_low * b_low
    return product, rest


def write_sums(line, sums, places):
    spot = lanes(8)
    ones = jnp.ones((128, 128), jnp.bfloat16)
    stacked = jnp.concatenate(sums, axis=0)
    parts = []
    for _ in range(3):
        part = stacked.astype(jnp.bfloat16)
        stacked = stacked - part.astype(jnp.float32)
        parts.append(jnp.dot(part, ones, preferred_element_type=jnp.float32))
    large, small = parts[0], parts[1] + parts[2]
    for index, place in enumerate(places):
        rows = slice(8 * index, 8 * index + 8)
        total, rest = two_sum(large[rows], small[rows])
        for step in (4, 2, 1):
            total, error = two_sum(total, pltpu.roll(total, step, 0))
            rest = rest + pltpu.roll(rest, step, 0) + error
        line = jnp.where(spot == place, total, jnp.where(spot == place + 64, rest, line))
    return line


def gram_place(m, n):
    return 16 + m * (m + 1) // 2 + n


def gram_kernel(basis, out):
    count = basis.shape[0] // 192
    line = jnp.zeros((8, 128), jnp.float32)
    for m in range(count):
        sums = [jnp.zeros((8, 128), jnp.float32) for _ in range(m + 1)]
        for tile in range(24):
            value = basis[pl.ds(192 * m + 8 * tile, 8), :]
            for n in range(m + 1):
                sums[n] += value * basis[pl.ds(192 * n + 8 * tile, 8), :]
        line = write_sums(line, sums, [gram_place(m, n) for n in range(m + 1)])
    out[...] = line[:1]


def finish_kernel(cell_count, messages, advanced, basis, out, hessenberg):
    count = basis.shape[0] // 192
    terms = [messages[device] for device in range(messages.shape[0])]
    errors = []
    while len(terms) > 1:
        pairs = [two_sum(a, b) for a, b in zip(terms[::2], terms[1::2])]
        errors += [error for _, error in pairs]
        terms = [total for total, _ in pairs] + terms[len(terms) // 2 * 2 :]
    while len(errors) > 1:
        errors = [a + b for a, b in zip(errors[::2], errors[1::2])] + errors[len(errors) // 2 * 2 :]
    total = terms[0]
    rest = pltpu.roll(jnp.broadcast_to(total, (8, 128)), 64, 1)
    rest = rest + errors[0] if errors else rest

    def entry(index):
        high = jnp.broadcast_to(total[:, index : index + 1], (8, 128))
        return high, jnp.broadcast_to(rest[:1, index : index + 1], (8, 128))

    pending, pending_rest = [list(part) for part in zip(*[entry(m) for m in range(count)])]
    energy, energy_rest = entry(count)
    weights = []
    diagonals = [entry(gram_place(m, m)) for m in range(count)]
    inverses = [1.0 / diagonal for diagonal, _ in diagonals]
    for m in range(count):
        weight = pending[m] * inverses[m]
        weights.append(weight)
        parts = split(weight)
        diagonal, diagonal_rest = diagonals[m]
        product, error = two_product(weight, diagonal, parts, split(diagonal))
        left = (pending[m] - product) + (pending_rest[m] - error - weight * diagonal_rest)
        product, error = two_product(weight, pending[m], parts, split(pending[m]))
        energy, lost = two_sum(energy, -product)
        energy_rest = energy_rest + (lost - error - weight * (pending_rest[m] + left))
        for n in range(m + 1, count):
            factor, factor_rest = entry(gram_place(n, m))
            product, error = two_product(weight, factor, parts, split(factor))
            pending[n], lost = two_sum(pending[n], -product)
            pending_rest[n] = pending_rest[n] + (lost - error - weight * factor_rest)
    energy = energy + energy_rest
    spread = jnp.sqrt(jnp.maximum(energy, 0.0) / cell_count + epsilon)
    scale = 1.0 / spread
    for tile in range(24):
        rows = pl.ds(8 * tile, 8)
        value = advanced[rows, :]
        for m in range(count):
            value = value - weights[m] * basis[pl.ds(192 * m + 8 * tile, 8), :]
        out[rows, :] = value * scale
    for m in range(count):
        hessenberg[m] = weights[m][0, 0]
    hessenberg[count] = spread[0, 0]


def shift(value, axis, step):
    count = lax.axis_size(axis)
    return lax.ppermute(value, axis, [(i, (i + step) % count) for i in range(count)])


def march_scratch():
    return [
        shape(3 * window * sub, 128),
        shape(3 * window * sub, 128),
        shape(3 * sub, 128),
        shape(3 * sub, 128),
        shape(kinds_of_coefficient * 12 * sub, 128),
    ]


def general_plan(field, velocity, basis, wall_region, wall_conductance):
    loop = lax.axis_size("phi")
    ends = lax.axis_size("gz")
    halves = lax.axis_size("row")
    fold = loop == 4
    many = ends > 2
    vectors = basis.shape[0]
    field_rows = field.reshape(192, 128)
    flow_rows = velocity.reshape(192, 128)
    swap = [(0, 1), (1, 0)]
    far_field = lax.ppermute(field_rows, "row", swap)
    far_flow = lax.ppermute(flow_rows, "row", swap)
    field_rows, flow_rows, basis_rows = near(
        field_rows, flow_rows, basis.reshape(vectors * 192, 128)
    )
    inner = pl.pallas_call(
        inner_kernel, in_specs=vmem(2), out_specs=vmem(1)[0], out_shape=shape(8 * tiles, 128)
    )(field_rows, flow_rows)
    half = loop // 2
    turned = []
    for p in range(loop):
        for r in range(halves):
            turned.append((p * halves + r, ((p + half) % loop if r == 0 else p) * halves + r))
    behind = lax.ppermute(inner, ("phi", "row"), turned)
    far_field, far_flow = near(far_field, far_flow)
    side = side_rows if fold else axis_row
    packed = pl.pallas_call(
        functools.partial(sides_kernel, fold),
        in_specs=[pl.BlockSpec(memory_space=pltpu.SMEM)] + vmem(5),
        out_specs=vmem(3 if fold else 5),
        out_shape=[shape(side, 128), shape(side, 128), shape(8, 128)]
        + ([] if fold else [shape(24, 128)] * 2),
    )(wall_conductance, wall_region, field_rows, flow_rows, far_field, far_flow)
    up, down, reflect = packed[:3]
    below = shift(up, "phi", 1)
    above = shift(down, "phi", -1)
    corners = []
    if not fold:
        corners = [shift(packed[3], "phi", half + 1), shift(packed[4], "phi", half - 1)]
    gram = pl.pallas_call(
        gram_kernel, in_specs=vmem(1), out_specs=vmem(1)[0], out_shape=shape(1, 128)
    )(basis_rows)
    below, above, behind, gram, *corners = lax.optimization_barrier(
        (below, above, behind, gram, *corners)
    )
    below, above, behind, gram, *corners = near(below, above, behind, gram, *corners)
    walls, strip, cells = pl.pallas_call(
        functools.partial(window_kernel, fold),
        in_specs=vmem(8 + len(corners)),
        out_specs=vmem(3),
        out_shape=[shape(sub, 128), shape(6 * sub, 128), shape(6 * window * sub, 128)],
    )(field_rows, flow_rows, far_field, far_flow, below, above, behind, reflect, *corners)
    if many:
        up_pairs = [(i, i + 1) for i in range(ends - 1)]
        others = [
            lax.ppermute(strip, "gz", up_pairs),
            lax.ppermute(strip, "gz", [(b, a) for a, b in up_pairs]),
        ]
    else:
        others = [lax.ppermute(strip, "gz", swap)]
    walls, strip, cells, *others = near(walls, strip, cells, *others)
    devices = lax.axis_size(("phi", "gz", "row"))
    return pl.pallas_call(
        functools.partial(stage_kernel, many),
        in_specs=vmem(8 + len(others)),
        out_specs=vmem(2),
        out_shape=[shape(devices, 1, 128), shape(192, 128)],
        scratch_shapes=march_scratch(),
    )(below, above, behind, walls, strip, *others, cells, basis_rows, gram)


def compact_plan(field, velocity, basis, wall_region, wall_conductance):
    vectors = basis.shape[0]
    field_rows = field.reshape(192, 128)
    flow_rows = velocity.reshape(192, 128)
    axes = ("phi", "gz", "row")
    devices = lax.axis_size(axes)

    def exchange(value, partner):
        pairs = []
        for p in range(4):
            for g in range(2):
                for r in range(2):
                    q, h, t = partner(p, g, r)
                    pairs.append(((p * 2 + g) * 2 + r, (q % 4 * 2 + h) * 2 + t))
        return lax.ppermute(value, axes, pairs)

    def beside(p, r):
        return p + 1 if (p + r) % 2 == 0 else p - 1

    swap = [(0, 1), (1, 0)]
    far_field = lax.ppermute(field_rows, "row", swap)
    far_flow = lax.ppermute(flow_rows, "row", swap)
    reflect, field_rows, flow_rows = pl.pallas_call(
        load_kernel,
        in_specs=[pl.BlockSpec(memory_space=pltpu.SMEM)] + vmem(3),
        out_specs=vmem(3),
        out_shape=[shape(8, 128), shape(192, 128), shape(192, 128)],
    )(wall_conductance, wall_region, field_rows, flow_rows)
    blocks = near(field_rows, flow_rows, far_field, far_flow, reflect)
    side, turn, diagonal, strip = pl.pallas_call(
        send_kernel,
        in_specs=vmem(5),
        out_specs=vmem(4),
        out_shape=[
            shape(side_length, 128),
            shape(8 * tiles, 128),
            shape(diagonal_length, 128),
            shape(strip_length, 128),
        ],
    )(*blocks)
    opposite = exchange(strip, lambda p, g, r: (p + 2, 1 - g, 1) if r == 0 else (p, 1 - g, 0))
    turn = exchange(turn, lambda p, g, r: (p + 2, g, 1) if r == 0 else (p, g, 0))
    diagonal = exchange(diagonal, lambda p, g, r: (beside(p, r), 1 - g, r))
    side = exchange(side, lambda p, g, r: (beside(p, r), g, r))
    (basis_rows,) = near(basis.reshape(vectors * 192, 128))
    gram = pl.pallas_call(
        gram_kernel, in_specs=vmem(1), out_specs=vmem(1)[0], out_shape=shape(1, 128)
    )(basis_rows)
    side, turn, diagonal, opposite, gram = near(
        *lax.optimization_barrier((side, turn, diagonal, opposite, gram))
    )
    share = pl.pallas_call(
        share_kernel, in_specs=vmem(4), out_specs=vmem(1)[0], out_shape=shape(share_length, 128)
    )(side, turn, opposite, diagonal)
    shared = lax.ppermute(share, "row", swap)
    strip, shared = near(strip, shared)
    return pl.pallas_call(
        compact_kernel,
        in_specs=vmem(12),
        out_specs=vmem(2),
        out_shape=[shape(devices, 1, 128), shape(192, 128)],
        scratch_shapes=[
            shape(6 * window * sub, 128),
            shape(2 * sub, 128),
            shape(6 * sub, 128),
        ]
        + march_scratch(),
    )(*blocks, strip, side, diagonal, opposite, shared, basis_rows, gram)


def local(field, velocity, basis, wall_region, wall_conductance):
    axes = ("phi", "gz", "row")
    vectors = basis.shape[0]
    devices = lax.axis_size(axes)
    compact = tuple(lax.axis_size(axis) for axis in axes) == (4, 2, 2)
    plan = compact_plan if compact else general_plan
    message, advanced = plan(field, velocity, basis, wall_region, wall_conductance)
    (basis_rows,) = near(basis.reshape(vectors * 192, 128))
    messages = lax.all_to_all(message, axes, 0, 0, tiled=True)
    messages, advanced = near(messages, advanced)
    out, hessenberg = pl.pallas_call(
        functools.partial(finish_kernel, float(field.size * devices)),
        in_specs=vmem(3),
        out_specs=vmem(1) + [pl.BlockSpec(memory_space=pltpu.SMEM)],
        out_shape=[
            jax.ShapeDtypeStruct((192, 128), jnp.float32),
            jax.ShapeDtypeStruct((vectors + 1,), jnp.float32),
        ],
    )(messages, advanced, basis_rows)
    return out.reshape(field.shape), hessenberg


def solution(mesh):
    return jax.shard_map(
        local,
        mesh=mesh,
        in_specs=(
            P("groups", "row", "phi", "gz"),
            P("groups", "row", "phi", "gz"),
            P("groups", None, "row", "phi", "gz"),
            P(("groups", "phi"), "gz"),
            P("groups"),
        ),
        out_specs=(P("groups", "row", "phi", "gz"), P("groups")),
        check_vma=False,
    )
```

```python
import functools

import jax
import jax.numpy as jnp
import numpy as np
from jax import lax
from jax.experimental import pallas as pl
from jax.experimental.pallas import tpu as pltpu
from jax.sharding import PartitionSpec as P

advect = 0.2
diffuse = 0.1
epsilon = 1e-06
signs = (-1.0, -1.0, 1.0)
wall_signs = (-1.0, 1.0, 1.0)

tiles = 15
wall_row = 8 * tiles
corner_row = wall_row + 8
axis_row = corner_row + 24
side_rows = axis_row + 24
window = 14
sub = 16
kinds_of_coefficient = 15


def row_of(component, w):
    return (component * window + w) * sub


def vmem(count):
    return [pl.BlockSpec(memory_space=pltpu.VMEM)] * count


def shape(*dims):
    return pltpu.VMEM(dims, jnp.float32)


def near(*values):
    return [pltpu.with_memory_space_constraint(value, pltpu.VMEM) for value in values]


def lanes(rows):
    return lax.broadcasted_iota(jnp.int32, (rows, 128), 1)


def layer(source, c, r):
    return source[pl.ds(c * 64 + r * 8, 8), :]


def inner_kernel(field, velocity, inner):
    middle = lax.axis_index("row").astype(jnp.float32) * 8.0 + 1.5
    pull = diffuse * (middle + 0.5) / jnp.full((8, 128), middle)
    carry = pull - advect * jnp.minimum(layer(velocity, 0, 1), 0.0)
    stretch = (0.5 * advect) * layer(field, 0, 1)
    for c in range(3):
        inner[pl.ds(8 * c, 8), :] = layer(field, c, 0)
        inner[pl.ds(8 * (3 + c), 8), :] = layer(velocity, c, 0)
        inner[pl.ds(8 * (6 + c), 8), :] = layer(field, c, 1)
        inner[pl.ds(8 * (9 + c), 8), :] = layer(velocity, c, 1)
        inner[pl.ds(8 * (12 + c), 8), :] = carry * layer(field, c, 2) + stretch * layer(
            velocity, c, 2
        )


def sides_kernel(
    fold, conductance, region, field, velocity, far_field, far_flow, up, down, reflect, *corners
):
    top = lax.axis_index("row")
    kinds = region[...]
    value = jnp.zeros(kinds.shape, jnp.float32)
    for kind in range(conductance.shape[0]):
        value = jnp.where(kinds == kind, conductance[kind], value)
    reflect[...] = 1.0 - 2.0 * value / (1.0 + value)

    def column(source, c, q):
        return source[pl.ds(c * 64 + q, 8, stride=8), :]

    def cell(source, r, q):
        return source[pl.ds(r * 8 + q, 3, stride=64), :]

    radius = lax.broadcasted_iota(jnp.int32, (8, 128), 0).astype(jnp.float32)
    turn = diffuse / (radius + (top.astype(jnp.float32) * 8.0 + 0.5))
    for out, (one, two, three), direction in ((up, (7, 6, 5), -1.0), (down, (0, 1, 2), 1.0)):
        for c in range(3):
            out[pl.ds(8 * c, 8), :] = column(field, c, one)
            out[pl.ds(8 * (3 + c), 8), :] = column(velocity, c, one)
            out[pl.ds(8 * (6 + c), 8), :] = column(field, c, two)
            out[pl.ds(8 * (9 + c), 8), :] = column(velocity, c, two)
        speed = column(velocity, 1, two)
        carry = diffuse + advect * jnp.maximum(-direction * speed, 0.0)
        stretch = (0.5 * advect * direction) * column(field, 1, two)
        far = [column(field, c, three) for c in range(3)]
        term = [carry * far[c] + stretch * column(velocity, c, three) for c in range(3)]
        term[0] = term[0] - (direction * turn) * far[1]
        term[1] = term[1] + (direction * turn) * far[0]
        for c in range(3):
            out[pl.ds(8 * (12 + c), 8), :] = term[c]
        out[pl.ds(wall_row, 1), :] = reflect[pl.ds(one, 1), :]
        out[pl.ds(wall_row + 1, 1), :] = reflect[pl.ds(two, 1), :]
        for place, (r, q) in enumerate(((0, one), (0, two), (1, one))):
            for part, source in enumerate((far_field, far_flow)):
                out[pl.ds(corner_row + 8 * place + 3 * part, 3), :] = jnp.where(
                    top == 0, cell(source, r, q), cell(source, 7 - r, q)
                )
    for side, (one, two) in ((0, (7, 6)), (1, (0, 1))):
        if fold:
            out, base = (down, up)[side], axis_row
        else:
            out, base = corners[side], 0
        for place, (r, q) in enumerate(((0, one), (0, two), (1, one))):
            out[pl.ds(base + 8 * place, 3), :] = cell(field, r, q)
            out[pl.ds(base + 8 * place + 3, 3), :] = cell(velocity, r, q)


def window_kernel(
    fold, field, velocity, far_field, far_flow, below, above, behind, reflect, *rest
):
    if fold:
        axis_low, axis_high, axis_base = above, below, axis_row
    else:
        axis_low, axis_high, axis_base = rest[0], rest[1], 0
    walls, strip, cells = rest[-3:]
    low_half = lax.axis_index("row") == 0
    nothing = jnp.zeros((8, 128), jnp.float32)
    for c in range(6):
        source, far = (field, far_field) if c < 3 else (velocity, far_flow)
        sign = signs[c % 3]
        for r in range(8):
            cells[pl.ds(row_of(c, r + 3), 8), :] = layer(source, c % 3, r)
        for w in range(window):
            cells[pl.ds(row_of(c, w) + 8, 8), :] = nothing
        for w in range(3):
            ghost = sign * behind[pl.ds(48 * (2 - w) + 8 * c, 8), :] if w > 0 else 0.0
            cells[pl.ds(row_of(c, w), 8), :] = jnp.where(low_half, ghost, layer(far, c % 3, 5 + w))
            cells[pl.ds(row_of(c, 11 + w), 8), :] = jnp.where(low_half, layer(far, c % 3, w), 0.0)
        for depth in range(2):
            place = pl.ds(48 * depth + 8 * c, 8)
            cells[pl.ds(row_of(c, 3) + 15 - depth, 8, stride=sub), :] = below[place, :]
            cells[pl.ds(row_of(c, 3) + 8 + depth, 8, stride=sub), :] = above[place, :]
    flip = lax.broadcasted_iota(jnp.int32, (6, 128), 0)
    flip = jnp.where((flip == 2) | (flip == 5), 1.0, -1.0)
    for place, (w, step) in enumerate(((2, 0), (2, 1), (1, 0))):
        for axis_source, source, q in ((axis_low, below, 15 - step), (axis_high, above, 8 + step)):
            ghost = flip * axis_source[pl.ds(axis_base + 8 * place, 6), :]
            other = source[pl.ds(corner_row + 8 * place, 6), :]
            low = jnp.where(low_half, ghost, other)
            high = jnp.where(low_half, other, 0.0)
            for c in range(6):
                cells[pl.ds(row_of(c, w) + q, 1), :] = low[c : c + 1]
                cells[pl.ds(row_of(c, 13 - w) + q, 1), :] = high[c : c + 1]
    walls[pl.ds(0, 8), :] = reflect[...]
    walls[pl.ds(8, 8), :] = nothing
    walls[pl.ds(8, 2), :] = above[pl.ds(wall_row, 2), :]
    walls[pl.ds(15, 1), :] = below[pl.ds(wall_row, 1), :]
    walls[pl.ds(14, 1), :] = below[pl.ds(wall_row + 1, 1), :]
    slot = lanes(sub) // 8
    for c in range(6):
        packed = jnp.where(slot == 12, pltpu.roll(walls[...], 100, 1), 0.0)
        for w in range(1, window - 1):
            row = cells[pl.ds(row_of(c, w), sub), :]
            packed = jnp.where(slot == w - 1, pltpu.roll(row, (8 * (w - 1) + 4) % 128, 1), packed)
        strip[pl.ds(sub * c, sub), :] = packed


def back(value, axis, step=1):
    return pltpu.roll(value, step, axis)


def ahead(value, axis, step=1):
    return pltpu.roll(value, value.shape[axis] - step, axis)


def rate(center, sides, coefficients):
    inward, outward, before, after, under, over = sides
    pull_in, pull_out, pull_before, pull_after, pull_under, pull_over, mix, turn = coefficients
    result = []
    for c in range(3):
        value = (
            (pull_in * inward[c] + pull_out * outward[c])
            + (pull_before * before[c] + pull_after * after[c])
            + (pull_under * under[c] + pull_over * over[c])
        )
        for d in range(3):
            value = value + mix[c][d] * center[d]
        result.append(value)
    result[0] = result[0] - turn * (after[1] - before[1])
    result[1] = result[1] + turn * (after[0] - before[0])
    return result


def coefficients_of(speed, sides, sense, inner_pull, outer_pull, bend, inverse_square, turn):
    inward, outward, before, after, under, over = sides
    radial, around, axial = speed
    around_here = sense * around
    pulls = (
        inner_pull + advect * jnp.maximum(radial, 0.0),
        outer_pull - advect * jnp.minimum(radial, 0.0),
        diffuse + advect * jnp.maximum(around_here, 0.0),
        diffuse - advect * jnp.minimum(around_here, 0.0),
        diffuse + advect * jnp.maximum(axial, 0.0),
        diffuse - advect * jnp.minimum(axial, 0.0),
    )
    keep = -6.0 * diffuse - advect * (jnp.abs(radial) + jnp.abs(around) + jnp.abs(axial))
    half = 0.5 * advect
    mix = []
    for c in range(3):
        mix.append(
            [
                half * (outward[c] - inward[c]),
                (half * sense) * (after[c] - before[c]),
                half * (over[c] - under[c]),
            ]
        )
    mix[0][0] = mix[0][0] + (keep - diffuse * inverse_square)
    mix[1][1] = mix[1][1] + (keep - diffuse * inverse_square) + bend * radial
    mix[1][0] = mix[1][0] - bend * around
    mix[2][2] = mix[2][2] + keep
    return pulls + (mix, turn)


def stage_kernel(many, below, above, behind, walls, strip, *rest):
    others = rest[: 2 if many else 1]
    cells, basis, gram, message, advanced, first, second, edge, edge_flow, table = rest[len(others) :]
    has_high = lax.axis_index("gz") < lax.axis_size("gz") - 1
    inside = lanes(sub) % 8
    mine = [strip[pl.ds(sub * c, sub), :] for c in range(6)]
    if many:
        from_low = [others[0][pl.ds(sub * c, sub), :] for c in range(6)]
        from_high = [others[1][pl.ds(sub * c, sub), :] for c in range(6)]
        strips = [
            [jnp.where(inside < 4, b, a) for a, b in zip(mine, from_low)],
            [jnp.where(inside < 4, a, b) for a, b in zip(mine, from_high)],
        ]
    else:
        other = [others[0][pl.ds(sub * c, sub), :] for c in range(6)]
        strips = [[jnp.where((inside < 4) == has_high, a, b) for a, b in zip(mine, other)]]
    strips = [line + [ahead(line[0], 1, 16)] for line in strips]
    low_half = lax.axis_index("row") == 0
    ghosts = [jnp.where(low_half, signs[c] * layer(behind, 0, 12 + c), 0.0) for c in range(3)]
    lows = [layer(below, 0, 12 + c) for c in range(3)]
    highs = [layer(above, 0, 12 + c) for c in range(3)]
    march(
        strips, ghosts, lows, highs, walls, cells, basis, gram, message, advanced,
        first, second, edge, edge_flow, table,
    )


def march(
    strips, ghosts, lows, highs, walls, cells, basis, gram, message, advanced,
    first, second, edge, edge_flow, table,
):
    top = lax.axis_index("row")
    low_half = top == 0
    place = lax.axis_index("gz")
    has_low = place > 0
    has_high = place < lax.axis_size("gz") - 1
    lane = lanes(sub)
    slot = lane // 8

    number = (slot - 2).astype(jnp.float32) + top.astype(jnp.float32) * 8.0 + 0.5
    inverse = 1.0 / number
    strip_scalars = (
        jnp.where(number < 0.0, -1.0, 1.0),
        diffuse * (number - 0.5) * inverse,
        diffuse * (number + 0.5) * inverse,
        advect * inverse,
        inverse * inverse,
        diffuse * jnp.abs(inverse),
    )
    strip_wall = jnp.logical_and(slot == 10, top == 1)

    def strip_sides(values):
        return (
            [back(v, 1, 8) for v in values],
            [ahead(v, 1, 8) for v in values],
            [back(v, 0) for v in values],
            [ahead(v, 0) for v in values],
            [back(v, 1) for v in values],
            [ahead(v, 1) for v in values],
        )

    def walled(values, factors):
        return [jnp.where(strip_wall, f * back(v, 1, 8), v) for v, f in zip(values, factors)]

    levels = []
    flows = []
    for line in strips:
        factor = line[6]
        flow = walled(line[3:6], wall_signs)
        flows.append(flow)
        weights = coefficients_of(flow, strip_sides(flow), *strip_scalars)
        start = walled(line[:3], [factor] * 3)
        one = rate(start, strip_sides(start), weights)
        one = walled([a + b for a, b in zip(start, one)], [factor] * 3)
        two = rate(one, strip_sides(one), weights)
        two = [0.75 * s + 0.25 * (a + b) for s, a, b in zip(start, one, two)]
        levels.append((start, one, two))

    inner_side = lane % 8 < 4

    def store_edges(target, low_values, high_values):
        for c in range(3):
            low = jnp.where(has_low, back(low_values[c], 1), 0.0)
            high = jnp.where(has_high, ahead(high_values[c], 1), 0.0)
            target[pl.ds(sub * c, sub), :] = jnp.where(inner_side, high, low)

    def axial(value, source, c, w, start, size):
        ghost = source[pl.ds(sub * c + start, size), :]
        ghost = pltpu.roll(ghost, 128 - (8 * (w - 1) + 4), 1)
        at = lane[:size]
        return (
            jnp.where(at == 0, ghost, back(value, 1)),
            jnp.where(at == 127, ghost, ahead(value, 1)),
        )

    def pick(low, high):
        return jnp.where(low_half, np.float32(low), np.float32(high))

    def scalars(w):
        options = []
        for half in range(2):
            r = half * 8 + (w - 3) + 0.5
            options.append(
                (
                    -1.0 if r < 0 else 1.0,
                    diffuse * (r - 0.5) / r,
                    diffuse * (r + 0.5) / r,
                    advect / r,
                    1.0 / (r * r),
                    diffuse / abs(r),
                )
            )
        return [pick(a, b) for a, b in zip(*options)]

    def read(source, c, w, start=0, size=sub):
        return source[pl.ds(row_of(c, w) + start, size), :]

    for c in range(6):
        last = read(cells, c, 10)
        factor = walls[...] if c < 3 else wall_signs[c - 3]
        cells[pl.ds(row_of(c, 11), sub), :] = jnp.where(low_half, read(cells, c, 11), factor * last)

    def surroundings(source, first_component, ends, w, start, size):
        center, sides = [], [[], [], [], [], [], []]
        for c in range(3):
            at = first_component + c
            whole = read(source, at, w)
            value = whole[:size]
            under, over = axial(value, ends, c, w, start, size)
            for side, part in zip(
                sides,
                (
                    read(source, at, w - 1, start, size),
                    read(source, at, w + 1, start, size),
                    back(whole, 0)[:size],
                    ahead(whole, 0)[:size],
                    under,
                    over,
                ),
            ):
                side.append(part)
            center.append(value)
        return center, sides

    def table_rows(kind, w, start, size):
        return pl.ds((kind * 12 + w - 1) * sub + start, size)

    def make_table(w):
        weights = coefficients_of(*surroundings(cells, 3, edge_flow, w, 0, sub), *scalars(w))
        flat = list(weights[:6]) + [value for row in weights[6] for value in row]
        if w not in (1, 12):
            for kind, value in enumerate(flat):
                table[table_rows(kind, w, 0, sub), :] = value
        return weights

    def stored_table(w, start, size):
        flat = [table[table_rows(kind, w, start, size), :] for kind in range(kinds_of_coefficient)]
        mix = [flat[6:9], flat[9:12], flat[12:15]]
        return tuple(flat[:6]) + (mix, scalars(w)[-1])

    def field_rate(source, w, start=0, size=sub, weights=None):
        center, sides = surroundings(source, 0, edge, w, start, size)
        return center, rate(center, sides, weights or stored_table(w, start, size))

    store_edges(edge_flow, flows[0], flows[-1])
    store_edges(edge, levels[0][0], levels[-1][0])
    for w in range(1, 13):
        center, change = field_rate(cells, w, weights=make_table(w))
        for c in range(3):
            first[pl.ds(row_of(c, w), sub), :] = center[c] + change[c]
    for c in range(3):
        low = pl.ds(row_of(c, 1), 8)
        first[low, :] = first[low, :] + ghosts[c]
        before = pl.ds(row_of(c, 3) + 14, 8, stride=sub)
        after = pl.ds(row_of(c, 3) + 9, 8, stride=sub)
        first[before, :] = first[before, :] + lows[c]
        first[after, :] = first[after, :] + highs[c]

    def close_wall(source):
        for c in range(3):
            source[pl.ds(row_of(c, 11), sub), :] = jnp.where(
                low_half, read(source, c, 11), walls[...] * read(source, c, 10)
            )

    close_wall(first)
    store_edges(edge, levels[0][1], levels[-1][1])
    for w in range(2, 12):
        center, change = field_rate(first, w)
        for c in range(3):
            second[pl.ds(row_of(c, w), sub), :] = 0.75 * read(cells, c, w) + 0.25 * (
                center[c] + change[c]
            )
    close_wall(second)
    store_edges(edge, levels[0][2], levels[-1][2])
    count = basis.shape[0] // 192
    sums = [jnp.zeros((8, 128), jnp.float32) for _ in range(count + 1)]
    for w in range(3, 11):
        center, change = field_rate(second, w, 0, 8)
        for c in range(3):
            rows = pl.ds(64 * c + 8 * (w - 3), 8)
            value = read(cells, c, w, 0, 8) / 3.0 + (2.0 / 3.0) * (center[c] + change[c])
            advanced[rows, :] = value
            for m in range(count):
                sums[m] += basis[pl.ds(192 * m + 64 * c + 8 * (w - 3), 8), :] * value
            sums[count] += value * value
    line = write_sums(jnp.broadcast_to(gram[...], (8, 128)), sums, range(count + 1))[:1]
    for device in range(message.shape[0]):
        message[device] = line


side_wall = 16 * tiles
side_strip = side_wall + 8
side_axis = side_strip + 16
side_length = side_axis + 24
diagonal_wall = 24
diagonal_length = 32
strip_length = 56
share_corner = 8 * tiles
share_rest = share_corner + 24
share_turn = share_rest + side_length - side_wall
share_strip = share_turn + 8 * tiles
share_diagonal = share_strip + strip_length
share_length = share_diagonal + diagonal_length


def faces_up():
    return (lax.axis_index("phi") + lax.axis_index("row")) % 2 == 0


def own_strip(source, c):
    slot = lanes(8) // 8
    part = jnp.zeros((8, 128), jnp.float32)
    for r in range(8):
        moved = pltpu.roll(layer(source, c, r), (8 * r + 4) % 128, 1)
        part = jnp.where(slot == r, moved, part)
    return part


def load_kernel(
    conductance, region, field, velocity, reflect, field_copy, flow_copy, turn, own_ends
):
    kinds = region[...]
    value = jnp.zeros(kinds.shape, jnp.float32)
    for kind in range(conductance.shape[0]):
        value = jnp.where(kinds == kind, conductance[kind], value)
    reflect[...] = 1.0 - 2.0 * value / (1.0 + value)
    field_copy[...] = field[...]
    flow_copy[...] = velocity[...]
    carry = (diffuse * 2.0 / 1.5) - advect * jnp.minimum(layer(velocity, 0, 1), 0.0)
    stretch = (0.5 * advect) * layer(field, 0, 1)
    for c in range(3):
        for r in range(2):
            turn[pl.ds(8 * (6 * r + c), 8), :] = layer(field, c, r)
            turn[pl.ds(8 * (6 * r + 3 + c), 8), :] = layer(velocity, c, r)
        turn[pl.ds(8 * (12 + c), 8), :] = carry * layer(field, c, 2) + stretch * layer(
            velocity, c, 2
        )
    for c in range(6):
        own_ends[pl.ds(8 * c, 8), :] = own_strip(field if c < 3 else velocity, c % 3)


def send_kernel(field, velocity, far_field, far_flow, reflect, own_ends, side, diagonal, strip):
    top = lax.axis_index("row")
    upper = faces_up()
    slot = lanes(8) // 8

    def facing(load, depth):
        return jnp.where(upper, load(8 - depth), load(depth - 1))

    def column(source, c, depth):
        return facing(lambda q: source[pl.ds(c * 64 + q, 8, stride=8), :], depth)

    direction = jnp.where(upper, -1.0, 1.0)
    index = lax.broadcasted_iota(jnp.int32, (8, 128), 0).astype(jnp.float32)
    for source, flow, half in ((field, velocity, top), (far_field, far_flow, 1 - top)):
        base = half * (8 * tiles)

        def put(tile, value):
            side[pl.ds(pl.multiple_of(base + 8 * tile, 8), 8), :] = value

        bend = (diffuse * direction) / (index + (half.astype(jnp.float32) * 8.0 + 0.5))
        near_two = [column(source, c, 2) for c in range(3)]
        flow_two = [column(flow, c, 2) for c in range(3)]
        distant = [column(source, c, 3) for c in range(3)]
        carry = diffuse + advect * jnp.maximum(-direction * flow_two[1], 0.0)
        stretch = (0.5 * advect * direction) * near_two[1]
        term = [carry * distant[c] + stretch * column(flow, c, 3) for c in range(3)]
        term[0] = term[0] - bend * distant[1]
        term[1] = term[1] + bend * distant[0]
        for c in range(3):
            put(c, column(source, c, 1))
            put(3 + c, column(flow, c, 1))
            put(6 + c, near_two[c])
            put(9 + c, flow_two[c])
            put(12 + c, term[c])
    for depth in (1, 2):
        wall = facing(lambda q: reflect[pl.ds(q, 1), :], depth)
        side[pl.ds(side_wall + depth - 1, 1), :] = wall
        diagonal[pl.ds(diagonal_wall + depth - 1, 1), :] = wall

    for c in range(6):
        own = own_ends[pl.ds(8 * c, 8), :]
        far = own_strip(far_field if c < 3 else far_flow, c % 3)
        low = jnp.where(top == 0, own, far)
        high = jnp.where(top == 0, far, own)
        strip[pl.ds(8 * c, 8), :] = jnp.where(slot < 8, low, pltpu.roll(high, 64, 1))
    for depth in (1, 2):
        edge = facing(lambda q: strip[pl.ds(q, 6, stride=8), :], depth)
        side[pl.ds(side_strip + 8 * (depth - 1), 6), :] = edge
        diagonal[pl.ds(8 * (depth - 1), 6), :] = edge
    diagonal[pl.ds(16, 6), :] = jnp.where(
        upper, strip[pl.ds(0, 6, stride=8), :], strip[pl.ds(7, 6, stride=8), :]
    )

    def inner_cell(own, far, start, count, step):
        rows = pl.ds(start, count, stride=step)
        return jnp.where(top == 0, own[rows, :], far[rows, :])

    for place, (r, depth) in enumerate(((0, 1), (0, 2), (1, 1))):
        for part, (own, far) in enumerate(((field, far_field), (velocity, far_flow))):
            side[pl.ds(side_axis + 8 * place + 3 * part, 3), :] = jnp.where(
                upper,
                inner_cell(own, far, r * 8 + depth - 1, 3, 64),
                inner_cell(own, far, r * 8 + 8 - depth, 3, 64),
            )
    strip[pl.ds(48, 8), :] = reflect[...]


def other_corner(side, first, step):
    top = lax.axis_index("row")
    low = side[pl.ds(8 * tiles + first + step, 6, stride=8), :]
    high = side[pl.ds(first + 7 - step, 6, stride=8), :]
    return jnp.where(top == 0, low, high)


def share_kernel(side, turn, opposite, diagonal, out):
    top = lax.axis_index("row")
    half = pl.multiple_of((1 - top) * (8 * tiles), 8)
    out[pl.ds(0, 8 * tiles), :] = side[pl.ds(half, 8 * tiles), :]
    for place, (first, step) in enumerate(((0, 0), (48, 0), (0, 1))):
        low = side[pl.ds(first + 7 - step, 6, stride=8), :]
        high = side[pl.ds(8 * tiles + first + step, 6, stride=8), :]
        out[pl.ds(share_corner + 8 * place, 6), :] = jnp.where(top == 0, low, high)
    out[pl.ds(share_rest, side_length - side_wall), :] = side[
        pl.ds(side_wall, side_length - side_wall), :
    ]
    out[pl.ds(share_turn, 8 * tiles), :] = turn[...]
    out[pl.ds(share_strip, strip_length), :] = opposite[...]
    out[pl.ds(share_diagonal, diagonal_length), :] = diagonal[...]


def compact_kernel(
    field, velocity, far_field, far_flow, reflect, strip, side, diagonal, opposite, shared,
    basis, gram, message, advanced, cells, walls, line, first, second, edge, edge_flow, table,
):
    top = lax.axis_index("row")
    low_half = top == 0
    upper = faces_up()
    mine_low = lax.axis_index("gz") == 0

    def both(own, other):
        return jnp.where(upper, other, own), jnp.where(upper, own, other)

    own_half = pl.multiple_of(top * (8 * tiles), 8)

    def tile_pair(tile):
        return both(
            side[pl.ds(pl.multiple_of(own_half + 8 * tile, 8), 8), :], shared[pl.ds(8 * tile, 8), :]
        )

    def rest_pair(start, count):
        return both(
            side[pl.ds(start, count), :], shared[pl.ds(share_rest + start - side_wall, count), :]
        )

    def diagonal_pair(start, count):
        return both(
            diagonal[pl.ds(start, count), :], shared[pl.ds(share_diagonal + start, count), :]
        )

    behind = [shared[pl.ds(share_turn + 8 * tile, 8), :] for tile in range(tiles)]
    nothing = jnp.zeros((8, 128), jnp.float32)
    for c in range(6):
        source, far = (field, far_field) if c < 3 else (velocity, far_flow)
        sign = signs[c % 3]
        for r in range(8):
            cells[pl.ds(row_of(c, r + 3), 8), :] = layer(source, c % 3, r)
        for w in range(window):
            cells[pl.ds(row_of(c, w) + 8, 8), :] = nothing
        for w in range(3):
            ghost = sign * behind[6 * (2 - w) + c] if w > 0 else 0.0
            cells[pl.ds(row_of(c, w), 8), :] = jnp.where(low_half, ghost, layer(far, c % 3, 5 + w))
            cells[pl.ds(row_of(c, 11 + w), 8), :] = jnp.where(low_half, layer(far, c % 3, w), 0.0)
        for depth in range(2):
            below, above = tile_pair(6 * depth + c)
            cells[pl.ds(row_of(c, 3) + 15 - depth, 8, stride=sub), :] = below
            cells[pl.ds(row_of(c, 3) + 8 + depth, 8, stride=sub), :] = above
    flip = lax.broadcasted_iota(jnp.int32, (6, 128), 0)
    flip = jnp.where((flip == 2) | (flip == 5), 1.0, -1.0)
    for place, (w, first_row, step, depth) in enumerate(((2, 0, 0, 0), (2, 48, 0, 1), (1, 0, 1, 0))):
        axis_high, axis_low = rest_pair(side_axis + 8 * place, 6)
        below, above = both(
            other_corner(side, first_row, step), shared[pl.ds(share_corner + 8 * place, 6), :]
        )
        for axis_part, other, q in ((axis_low, below, 15 - depth), (axis_high, above, 8 + depth)):
            low = pl.ds(row_of(0, w) + q, 6, stride=window * sub)
            high = pl.ds(row_of(0, 13 - w) + q, 6, stride=window * sub)
            cells[low, :] = jnp.where(low_half, flip * axis_part, other)
            cells[high, :] = jnp.where(low_half, other, 0.0)

    slot, inside = lanes(sub) // 8, lanes(sub) % 8
    axial_strip = [
        jnp.where(
            low_half, opposite[pl.ds(8 * tile, 8), :], shared[pl.ds(share_strip + 8 * tile, 8), :]
        )
        for tile in range(7)
    ]
    own_side = (inside < 4) == mine_low

    def merge(own, other):
        return jnp.where(own_side[: own.shape[0]], own, other)

    for part, (tile, pair) in enumerate(
        ((reflect[...], rest_pair(side_wall, 2)), (axial_strip[6], diagonal_pair(diagonal_wall, 2)))
    ):
        below, above = pair
        base = sub * part
        walls[pl.ds(base, 8), :] = tile
        walls[pl.ds(base + 8, 8), :] = nothing
        walls[pl.ds(base + 8, 2), :] = above
        walls[pl.ds(base + 15, 1), :] = below[0:1]
        walls[pl.ds(base + 14, 1), :] = below[1:2]
    factor = merge(
        pltpu.roll(walls[pl.ds(0, sub), :], 84, 1), pltpu.roll(walls[pl.ds(sub, sub), :], 84, 1)
    )

    for c in range(6):
        own = strip[pl.ds(8 * c, 8), :]
        line[pl.ds(sub * c, 8), :] = merge(own, axial_strip[c])
        line[pl.ds(sub * c + 8, 8), :] = nothing
    for depth in (1, 2):
        below, above = rest_pair(side_strip + 8 * (depth - 1), 6)
        beyond_below, beyond_above = diagonal_pair(8 * (depth - 1), 6)
        line[pl.ds(16 - depth, 6, stride=sub), :] = merge(below, beyond_below)
        line[pl.ds(7 + depth, 6, stride=sub), :] = merge(above, beyond_above)
    axis_high, axis_low = diagonal_pair(16, 6)
    combined = []
    for c in range(6):
        value = line[pl.ds(sub * c, sub), :]
        combined.append(jnp.where(low_half, pltpu.roll(value, 16, 1), pltpu.roll(value, 80, 1)))
    for c in range(6):
        sign = signs[c % 3]
        across = shared[pl.ds(share_strip + 8 * c, 8), :]
        own = jnp.where(
            slot[:8] == 1,
            pltpu.roll(behind[c], 12, 1),
            pltpu.roll(behind[6 + c], 4, 1),
        )
        other = jnp.where(slot[:8] == 1, pltpu.roll(across, 8, 1), pltpu.roll(across, 120, 1))
        line[pl.ds(sub * c, 8), :] = sign * merge(own, other)
        line[pl.ds(sub * c + 8, 8), :] = nothing
        line[pl.ds(sub * c + 8, 1), :] = sign * pltpu.roll(axis_high, 8, 1)[c : c + 1]
        line[pl.ds(sub * c + 15, 1), :] = sign * pltpu.roll(axis_low, 8, 1)[c : c + 1]
        ghost = line[pl.ds(sub * c, sub), :]
        combined[c] = jnp.where(jnp.logical_and(slot < 2, low_half), ghost, combined[c])
    combined.append(factor)
    ghosts = [jnp.where(low_half, signs[c] * behind[12 + c], 0.0) for c in range(3)]
    lows, highs = zip(*[tile_pair(12 + c) for c in range(3)])
    march(
        [combined], ghosts, lows, highs, walls.at[pl.ds(0, sub), :], cells, basis, gram, message,
        advanced, first, second, edge, edge_flow, table,
    )


def two_sum(a, b):
    total = a + b
    part = total - a
    return total, (a - (total - part)) + (b - part)


def split(a):
    scaled = 4097.0 * a
    high = scaled - (scaled - a)
    return high, a - high


def two_product(a, b, a_parts, b_parts):
    product = a * b
    (a_high, a_low), (b_high, b_low) = a_parts, b_parts
    rest = ((a_high * b_high - product) + a_high * b_low + a_low * b_high) + a_low * b_low
    return product, rest


def write_sums(line, sums, places):
    spot = lanes(8)
    ones = jnp.ones((128, 128), jnp.bfloat16)
    stacked = jnp.concatenate(sums, axis=0)
    parts = []
    for _ in range(3):
        part = stacked.astype(jnp.bfloat16)
        stacked = stacked - part.astype(jnp.float32)
        parts.append(jnp.dot(part, ones, preferred_element_type=jnp.float32))
    large, small = parts[0], parts[1] + parts[2]
    for index, place in enumerate(places):
        rows = slice(8 * index, 8 * index + 8)
        total, rest = two_sum(large[rows], small[rows])
        for step in (4, 2, 1):
            total, error = two_sum(total, pltpu.roll(total, step, 0))
            rest = rest + pltpu.roll(rest, step, 0) + error
        line = jnp.where(spot == place, total, jnp.where(spot == place + 64, rest, line))
    return line


def gram_place(m, n):
    return 16 + m * (m + 1) // 2 + n


def gram_kernel(basis, out):
    count = basis.shape[0] // 192
    line = jnp.zeros((8, 128), jnp.float32)
    for m in range(count):
        sums = [jnp.zeros((8, 128), jnp.float32) for _ in range(m + 1)]
        for tile in range(24):
            value = basis[pl.ds(192 * m + 8 * tile, 8), :]
            for n in range(m + 1):
                sums[n] += value * basis[pl.ds(192 * n + 8 * tile, 8), :]
        line = write_sums(line, sums, [gram_place(m, n) for n in range(m + 1)])
    out[...] = line[:1]


def finish_kernel(cell_count, messages, advanced, basis, out, hessenberg):
    count = basis.shape[0] // 192
    terms = [
        jnp.broadcast_to(messages[device], (8, 128)) for device in range(messages.shape[0])
    ]
    errors = []
    while len(terms) > 1:
        pairs = [two_sum(a, b) for a, b in zip(terms[::2], terms[1::2])]
        errors += [error for _, error in pairs]
        terms = [total for total, _ in pairs] + terms[len(terms) // 2 * 2 :]
    while len(errors) > 1:
        errors = [a + b for a, b in zip(errors[::2], errors[1::2])] + errors[len(errors) // 2 * 2 :]
    total = terms[0]
    rest = pltpu.roll(total, 64, 1)
    rest = rest + errors[0] if errors else rest

    def entry(index):
        high = jnp.broadcast_to(total[:, index : index + 1], (8, 128))
        return high, jnp.broadcast_to(rest[:, index : index + 1], (8, 128))

    pending, pending_rest = [list(part) for part in zip(*[entry(m) for m in range(count)])]
    energy, energy_rest = entry(count)
    weights = []
    diagonals = [entry(gram_place(m, m)) for m in range(count)]
    inverses = [1.0 / diagonal for diagonal, _ in diagonals]
    for m in range(count):
        weight = pending[m] * inverses[m]
        weights.append(weight)
        parts = split(weight)
        diagonal, diagonal_rest = diagonals[m]
        product, error = two_product(weight, diagonal, parts, split(diagonal))
        left = (pending[m] - product) + (pending_rest[m] - error - weight * diagonal_rest)
        product, error = two_product(weight, pending[m], parts, split(pending[m]))
        energy, lost = two_sum(energy, -product)
        energy_rest = energy_rest + (lost - error - weight * (pending_rest[m] + left))
        for n in range(m + 1, count):
            factor, factor_rest = entry(gram_place(n, m))
            product, error = two_product(weight, factor, parts, split(factor))
            pending[n], lost = two_sum(pending[n], -product)
            pending_rest[n] = pending_rest[n] + (lost - error - weight * factor_rest)
    energy = energy + energy_rest
    spread = jnp.sqrt(jnp.maximum(energy, 0.0) / cell_count + epsilon)
    scale = 1.0 / spread
    for tile in range(24):
        rows = pl.ds(8 * tile, 8)
        value = advanced[rows, :]
        for m in range(count):
            value = value - weights[m] * basis[pl.ds(192 * m + 8 * tile, 8), :]
        out[rows, :] = value * scale
    for m in range(count):
        hessenberg[m] = weights[m][0, 0]
    hessenberg[count] = spread[0, 0]


def shift(value, axis, step):
    count = lax.axis_size(axis)
    return lax.ppermute(value, axis, [(i, (i + step) % count) for i in range(count)])


def march_scratch():
    return [
        shape(3 * window * sub, 128),
        shape(3 * window * sub, 128),
        shape(3 * sub, 128),
        shape(3 * sub, 128),
        shape(kinds_of_coefficient * 12 * sub, 128),
    ]


def general_plan(field, velocity, basis, wall_region, wall_conductance):
    loop = lax.axis_size("phi")
    ends = lax.axis_size("gz")
    halves = lax.axis_size("row")
    fold = loop == 4
    many = ends > 2
    vectors = basis.shape[0]
    field_rows = field.reshape(192, 128)
    flow_rows = velocity.reshape(192, 128)
    swap = [(0, 1), (1, 0)]
    far_field = lax.ppermute(field_rows, "row", swap)
    far_flow = lax.ppermute(flow_rows, "row", swap)
    field_rows, flow_rows, basis_rows = near(
        field_rows, flow_rows, basis.reshape(vectors * 192, 128)
    )
    inner = pl.pallas_call(
        inner_kernel, in_specs=vmem(2), out_specs=vmem(1)[0], out_shape=shape(8 * tiles, 128)
    )(field_rows, flow_rows)
    half = loop // 2
    turned = []
    for p in range(loop):
        for r in range(halves):
            turned.append((p * halves + r, ((p + half) % loop if r == 0 else p) * halves + r))
    behind = lax.ppermute(inner, ("phi", "row"), turned)
    far_field, far_flow = near(far_field, far_flow)
    side = side_rows if fold else axis_row
    packed = pl.pallas_call(
        functools.partial(sides_kernel, fold),
        in_specs=[pl.BlockSpec(memory_space=pltpu.SMEM)] + vmem(5),
        out_specs=vmem(3 if fold else 5),
        out_shape=[shape(side, 128), shape(side, 128), shape(8, 128)]
        + ([] if fold else [shape(24, 128)] * 2),
    )(wall_conductance, wall_region, field_rows, flow_rows, far_field, far_flow)
    up, down, reflect = packed[:3]
    below = shift(up, "phi", 1)
    above = shift(down, "phi", -1)
    corners = []
    if not fold:
        corners = [shift(packed[3], "phi", half + 1), shift(packed[4], "phi", half - 1)]
    gram = pl.pallas_call(
        gram_kernel, in_specs=vmem(1), out_specs=vmem(1)[0], out_shape=shape(1, 128)
    )(basis_rows)
    below, above, behind, gram, *corners = lax.optimization_barrier(
        (below, above, behind, gram, *corners)
    )
    below, above, behind, gram, *corners = near(below, above, behind, gram, *corners)
    walls, strip, cells = pl.pallas_call(
        functools.partial(window_kernel, fold),
        in_specs=vmem(8 + len(corners)),
        out_specs=vmem(3),
        out_shape=[shape(sub, 128), shape(6 * sub, 128), shape(6 * window * sub, 128)],
    )(field_rows, flow_rows, far_field, far_flow, below, above, behind, reflect, *corners)
    if many:
        up_pairs = [(i, i + 1) for i in range(ends - 1)]
        others = [
            lax.ppermute(strip, "gz", up_pairs),
            lax.ppermute(strip, "gz", [(b, a) for a, b in up_pairs]),
        ]
    else:
        others = [lax.ppermute(strip, "gz", swap)]
    walls, strip, cells, *others = near(walls, strip, cells, *others)
    devices = lax.axis_size(("phi", "gz", "row"))
    return pl.pallas_call(
        functools.partial(stage_kernel, many),
        in_specs=vmem(8 + len(others)),
        out_specs=vmem(2),
        out_shape=[shape(devices, 1, 128), shape(192, 128)],
        scratch_shapes=march_scratch(),
    )(below, above, behind, walls, strip, *others, cells, basis_rows, gram)


def compact_plan(field, velocity, basis, wall_region, wall_conductance):
    vectors = basis.shape[0]
    field_rows = field.reshape(192, 128)
    flow_rows = velocity.reshape(192, 128)
    axes = ("phi", "gz", "row")
    devices = lax.axis_size(axes)

    def exchange(value, partner):
        pairs = []
        for p in range(4):
            for g in range(2):
                for r in range(2):
                    q, h, t = partner(p, g, r)
                    pairs.append(((p * 2 + g) * 2 + r, (q % 4 * 2 + h) * 2 + t))
        return lax.ppermute(value, axes, pairs)

    def beside(p, r):
        return p + 1 if (p + r) % 2 == 0 else p - 1

    swap = [(0, 1), (1, 0)]
    far_field = lax.ppermute(field_rows, "row", swap)
    far_flow = lax.ppermute(flow_rows, "row", swap)
    reflect, field_rows, flow_rows, turn, own_ends = pl.pallas_call(
        load_kernel,
        in_specs=[pl.BlockSpec(memory_space=pltpu.SMEM)] + vmem(3),
        out_specs=vmem(5),
        out_shape=[
            shape(8, 128),
            shape(192, 128),
            shape(192, 128),
            shape(8 * tiles, 128),
            shape(48, 128),
        ],
    )(wall_conductance, wall_region, field_rows, flow_rows)
    blocks = near(field_rows, flow_rows, far_field, far_flow, reflect)
    side, diagonal, strip = pl.pallas_call(
        send_kernel,
        in_specs=vmem(6),
        out_specs=vmem(3),
        out_shape=[
            shape(side_length, 128),
            shape(diagonal_length, 128),
            shape(strip_length, 128),
        ],
    )(*blocks, *near(own_ends))
    opposite = exchange(strip, lambda p, g, r: (p + 2, 1 - g, 1) if r == 0 else (p, 1 - g, 0))
    turn = exchange(turn, lambda p, g, r: (p + 2, g, 1) if r == 0 else (p, g, 0))
    diagonal = exchange(diagonal, lambda p, g, r: (beside(p, r), 1 - g, r))
    side = exchange(side, lambda p, g, r: (beside(p, r), g, r))
    (basis_rows,) = near(basis.reshape(vectors * 192, 128))
    gram = pl.pallas_call(
        gram_kernel, in_specs=vmem(1), out_specs=vmem(1)[0], out_shape=shape(1, 128)
    )(basis_rows)
    side, turn, diagonal, opposite, gram = near(
        *lax.optimization_barrier((side, turn, diagonal, opposite, gram))
    )
    share = pl.pallas_call(
        share_kernel, in_specs=vmem(4), out_specs=vmem(1)[0], out_shape=shape(share_length, 128)
    )(side, turn, opposite, diagonal)
    shared = lax.ppermute(share, "row", swap)
    strip, shared = near(strip, shared)
    return pl.pallas_call(
        compact_kernel,
        in_specs=vmem(12),
        out_specs=vmem(2),
        out_shape=[shape(devices, 1, 128), shape(192, 128)],
        scratch_shapes=[
            shape(6 * window * sub, 128),
            shape(2 * sub, 128),
            shape(6 * sub, 128),
        ]
        + march_scratch(),
    )(*blocks, strip, side, diagonal, opposite, shared, basis_rows, gram)


def local(field, velocity, basis, wall_region, wall_conductance):
    axes = ("phi", "gz", "row")
    vectors = basis.shape[0]
    devices = lax.axis_size(axes)
    compact = tuple(lax.axis_size(axis) for axis in axes) == (4, 2, 2)
    plan = compact_plan if compact else general_plan
    message, advanced = plan(field, velocity, basis, wall_region, wall_conductance)
    (basis_rows,) = near(basis.reshape(vectors * 192, 128))
    messages = lax.all_to_all(message, axes, 0, 0, tiled=True)
    messages, advanced = near(messages, advanced)
    out, hessenberg = pl.pallas_call(
        functools.partial(finish_kernel, float(field.size * devices)),
        in_specs=vmem(3),
        out_specs=vmem(1) + [pl.BlockSpec(memory_space=pltpu.SMEM)],
        out_shape=[
            jax.ShapeDtypeStruct((192, 128), jnp.float32),
            jax.ShapeDtypeStruct((vectors + 1,), jnp.float32),
        ],
    )(messages, advanced, basis_rows)
    return out.reshape(field.shape), hessenberg


def solution(mesh):
    return jax.shard_map(
        local,
        mesh=mesh,
        in_specs=(
            P("groups", "row", "phi", "gz"),
            P("groups", "row", "phi", "gz"),
            P("groups", None, "row", "phi", "gz"),
            P(("groups", "phi"), "gz"),
            P("groups"),
        ),
        out_specs=(P("groups", "row", "phi", "gz"), P("groups")),
        check_vma=False,
    )
```

```python
import functools

import jax
import jax.numpy as jnp
import numpy as np
from jax import lax
from jax.experimental import pallas as pl
from jax.experimental.pallas import tpu as pltpu
from jax.sharding import PartitionSpec as P

advect = 0.2
diffuse = 0.1
epsilon = 1e-06
signs = (-1.0, -1.0, 1.0)
wall_signs = (-1.0, 1.0, 1.0)

tiles = 15
wall_row = 8 * tiles
corner_row = wall_row + 8
axis_row = corner_row + 24
side_rows = axis_row + 24
window = 14
sub = 16
kinds_of_coefficient = 15


def row_of(component, w):
    return (component * window + w) * sub


def vmem(count):
    return [pl.BlockSpec(memory_space=pltpu.VMEM)] * count


def shape(*dims):
    return pltpu.VMEM(dims, jnp.float32)


def near(*values):
    return [pltpu.with_memory_space_constraint(value, pltpu.VMEM) for value in values]


def lanes(rows):
    return lax.broadcasted_iota(jnp.int32, (rows, 128), 1)


def layer(source, c, r):
    return source[pl.ds(c * 64 + r * 8, 8), :]


def inner_kernel(field, velocity, inner):
    middle = lax.axis_index("row").astype(jnp.float32) * 8.0 + 1.5
    pull = diffuse * (middle + 0.5) / jnp.full((8, 128), middle)
    carry = pull - advect * jnp.minimum(layer(velocity, 0, 1), 0.0)
    stretch = (0.5 * advect) * layer(field, 0, 1)
    for c in range(3):
        inner[pl.ds(8 * c, 8), :] = layer(field, c, 0)
        inner[pl.ds(8 * (3 + c), 8), :] = layer(velocity, c, 0)
        inner[pl.ds(8 * (6 + c), 8), :] = layer(field, c, 1)
        inner[pl.ds(8 * (9 + c), 8), :] = layer(velocity, c, 1)
        inner[pl.ds(8 * (12 + c), 8), :] = carry * layer(field, c, 2) + stretch * layer(
            velocity, c, 2
        )


def sides_kernel(
    fold, conductance, region, field, velocity, far_field, far_flow, up, down, reflect, *corners
):
    top = lax.axis_index("row")
    kinds = region[...]
    value = jnp.zeros(kinds.shape, jnp.float32)
    for kind in range(conductance.shape[0]):
        value = jnp.where(kinds == kind, conductance[kind], value)
    reflect[...] = 1.0 - 2.0 * value / (1.0 + value)

    def column(source, c, q):
        return source[pl.ds(c * 64 + q, 8, stride=8), :]

    def cell(source, r, q):
        return source[pl.ds(r * 8 + q, 3, stride=64), :]

    radius = lax.broadcasted_iota(jnp.int32, (8, 128), 0).astype(jnp.float32)
    turn = diffuse / (radius + (top.astype(jnp.float32) * 8.0 + 0.5))
    for out, (one, two, three), direction in ((up, (7, 6, 5), -1.0), (down, (0, 1, 2), 1.0)):
        for c in range(3):
            out[pl.ds(8 * c, 8), :] = column(field, c, one)
            out[pl.ds(8 * (3 + c), 8), :] = column(velocity, c, one)
            out[pl.ds(8 * (6 + c), 8), :] = column(field, c, two)
            out[pl.ds(8 * (9 + c), 8), :] = column(velocity, c, two)
        speed = column(velocity, 1, two)
        carry = diffuse + advect * jnp.maximum(-direction * speed, 0.0)
        stretch = (0.5 * advect * direction) * column(field, 1, two)
        far = [column(field, c, three) for c in range(3)]
        term = [carry * far[c] + stretch * column(velocity, c, three) for c in range(3)]
        term[0] = term[0] - (direction * turn) * far[1]
        term[1] = term[1] + (direction * turn) * far[0]
        for c in range(3):
            out[pl.ds(8 * (12 + c), 8), :] = term[c]
        out[pl.ds(wall_row, 1), :] = reflect[pl.ds(one, 1), :]
        out[pl.ds(wall_row + 1, 1), :] = reflect[pl.ds(two, 1), :]
        for place, (r, q) in enumerate(((0, one), (0, two), (1, one))):
            for part, source in enumerate((far_field, far_flow)):
                out[pl.ds(corner_row + 8 * place + 3 * part, 3), :] = jnp.where(
                    top == 0, cell(source, r, q), cell(source, 7 - r, q)
                )
    for side, (one, two) in ((0, (7, 6)), (1, (0, 1))):
        if fold:
            out, base = (down, up)[side], axis_row
        else:
            out, base = corners[side], 0
        for place, (r, q) in enumerate(((0, one), (0, two), (1, one))):
            out[pl.ds(base + 8 * place, 3), :] = cell(field, r, q)
            out[pl.ds(base + 8 * place + 3, 3), :] = cell(velocity, r, q)


def window_kernel(
    fold, field, velocity, far_field, far_flow, below, above, behind, reflect, *rest
):
    if fold:
        axis_low, axis_high, axis_base = above, below, axis_row
    else:
        axis_low, axis_high, axis_base = rest[0], rest[1], 0
    walls, strip, cells = rest[-3:]
    low_half = lax.axis_index("row") == 0
    nothing = jnp.zeros((8, 128), jnp.float32)
    for c in range(6):
        source, far = (field, far_field) if c < 3 else (velocity, far_flow)
        sign = signs[c % 3]
        for r in range(8):
            cells[pl.ds(row_of(c, r + 3), 8), :] = layer(source, c % 3, r)
        for w in range(window):
            cells[pl.ds(row_of(c, w) + 8, 8), :] = nothing
        for w in range(3):
            ghost = sign * behind[pl.ds(48 * (2 - w) + 8 * c, 8), :] if w > 0 else 0.0
            cells[pl.ds(row_of(c, w), 8), :] = jnp.where(low_half, ghost, layer(far, c % 3, 5 + w))
            cells[pl.ds(row_of(c, 11 + w), 8), :] = jnp.where(low_half, layer(far, c % 3, w), 0.0)
        for depth in range(2):
            place = pl.ds(48 * depth + 8 * c, 8)
            cells[pl.ds(row_of(c, 3) + 15 - depth, 8, stride=sub), :] = below[place, :]
            cells[pl.ds(row_of(c, 3) + 8 + depth, 8, stride=sub), :] = above[place, :]
    flip = lax.broadcasted_iota(jnp.int32, (6, 128), 0)
    flip = jnp.where((flip == 2) | (flip == 5), 1.0, -1.0)
    for place, (w, step) in enumerate(((2, 0), (2, 1), (1, 0))):
        for axis_source, source, q in ((axis_low, below, 15 - step), (axis_high, above, 8 + step)):
            ghost = flip * axis_source[pl.ds(axis_base + 8 * place, 6), :]
            other = source[pl.ds(corner_row + 8 * place, 6), :]
            low = jnp.where(low_half, ghost, other)
            high = jnp.where(low_half, other, 0.0)
            for c in range(6):
                cells[pl.ds(row_of(c, w) + q, 1), :] = low[c : c + 1]
                cells[pl.ds(row_of(c, 13 - w) + q, 1), :] = high[c : c + 1]
    walls[pl.ds(0, 8), :] = reflect[...]
    walls[pl.ds(8, 8), :] = nothing
    walls[pl.ds(8, 2), :] = above[pl.ds(wall_row, 2), :]
    walls[pl.ds(15, 1), :] = below[pl.ds(wall_row, 1), :]
    walls[pl.ds(14, 1), :] = below[pl.ds(wall_row + 1, 1), :]
    slot = lanes(sub) // 8
    for c in range(6):
        packed = jnp.where(slot == 12, pltpu.roll(walls[...], 100, 1), 0.0)
        for w in range(1, window - 1):
            row = cells[pl.ds(row_of(c, w), sub), :]
            packed = jnp.where(slot == w - 1, pltpu.roll(row, (8 * (w - 1) + 4) % 128, 1), packed)
        strip[pl.ds(sub * c, sub), :] = packed


def back(value, axis, step=1):
    return pltpu.roll(value, step, axis)


def ahead(value, axis, step=1):
    return pltpu.roll(value, value.shape[axis] - step, axis)


def rate(center, sides, coefficients):
    inward, outward, before, after, under, over = sides
    pull_in, pull_out, pull_before, pull_after, pull_under, pull_over, mix, turn = coefficients
    result = []
    for c in range(3):
        value = (
            (pull_in * inward[c] + pull_out * outward[c])
            + (pull_before * before[c] + pull_after * after[c])
            + (pull_under * under[c] + pull_over * over[c])
        )
        for d in range(3):
            value = value + mix[c][d] * center[d]
        result.append(value)
    result[0] = result[0] - turn * (after[1] - before[1])
    result[1] = result[1] + turn * (after[0] - before[0])
    return result


def coefficients_of(speed, sides, sense, inner_pull, outer_pull, bend, inverse_square, turn):
    inward, outward, before, after, under, over = sides
    radial, around, axial = speed
    around_here = sense * around
    pulls = (
        inner_pull + advect * jnp.maximum(radial, 0.0),
        outer_pull - advect * jnp.minimum(radial, 0.0),
        diffuse + advect * jnp.maximum(around_here, 0.0),
        diffuse - advect * jnp.minimum(around_here, 0.0),
        diffuse + advect * jnp.maximum(axial, 0.0),
        diffuse - advect * jnp.minimum(axial, 0.0),
    )
    keep = -6.0 * diffuse - advect * (jnp.abs(radial) + jnp.abs(around) + jnp.abs(axial))
    half = 0.5 * advect
    mix = []
    for c in range(3):
        mix.append(
            [
                half * (outward[c] - inward[c]),
                (half * sense) * (after[c] - before[c]),
                half * (over[c] - under[c]),
            ]
        )
    mix[0][0] = mix[0][0] + (keep - diffuse * inverse_square)
    mix[1][1] = mix[1][1] + (keep - diffuse * inverse_square) + bend * radial
    mix[1][0] = mix[1][0] - bend * around
    mix[2][2] = mix[2][2] + keep
    return pulls + (mix, turn)


def stage_kernel(many, below, above, behind, walls, strip, *rest):
    others = rest[: 2 if many else 1]
    cells, basis, gram, message, advanced, first, second, edge, edge_flow, table = rest[len(others) :]
    has_high = lax.axis_index("gz") < lax.axis_size("gz") - 1
    inside = lanes(sub) % 8
    mine = [strip[pl.ds(sub * c, sub), :] for c in range(6)]
    if many:
        from_low = [others[0][pl.ds(sub * c, sub), :] for c in range(6)]
        from_high = [others[1][pl.ds(sub * c, sub), :] for c in range(6)]
        strips = [
            [jnp.where(inside < 4, b, a) for a, b in zip(mine, from_low)],
            [jnp.where(inside < 4, a, b) for a, b in zip(mine, from_high)],
        ]
    else:
        other = [others[0][pl.ds(sub * c, sub), :] for c in range(6)]
        strips = [[jnp.where((inside < 4) == has_high, a, b) for a, b in zip(mine, other)]]
    strips = [line + [ahead(line[0], 1, 16)] for line in strips]
    low_half = lax.axis_index("row") == 0
    ghosts = [jnp.where(low_half, signs[c] * layer(behind, 0, 12 + c), 0.0) for c in range(3)]
    lows = [layer(below, 0, 12 + c) for c in range(3)]
    highs = [layer(above, 0, 12 + c) for c in range(3)]
    march(
        strips, ghosts, lows, highs, walls, cells, basis, gram, message, advanced,
        first, second, edge, edge_flow, table,
    )


def march(
    strips, ghosts, lows, highs, walls, cells, basis, gram, message, advanced,
    first, second, edge, edge_flow, table,
):
    top = lax.axis_index("row")
    low_half = top == 0
    place = lax.axis_index("gz")
    has_low = place > 0
    has_high = place < lax.axis_size("gz") - 1
    lane = lanes(sub)
    slot = lane // 8

    number = (slot - 2).astype(jnp.float32) + top.astype(jnp.float32) * 8.0 + 0.5
    inverse = 1.0 / number
    strip_scalars = (
        jnp.where(number < 0.0, -1.0, 1.0),
        diffuse * (number - 0.5) * inverse,
        diffuse * (number + 0.5) * inverse,
        advect * inverse,
        inverse * inverse,
        diffuse * jnp.abs(inverse),
    )
    strip_wall = jnp.logical_and(slot == 10, top == 1)

    def strip_sides(values):
        return (
            [back(v, 1, 8) for v in values],
            [ahead(v, 1, 8) for v in values],
            [back(v, 0) for v in values],
            [ahead(v, 0) for v in values],
            [back(v, 1) for v in values],
            [ahead(v, 1) for v in values],
        )

    def walled(values, factors):
        return [jnp.where(strip_wall, f * back(v, 1, 8), v) for v, f in zip(values, factors)]

    levels = []
    flows = []
    for line in strips:
        factor = line[6]
        flow = walled(line[3:6], wall_signs)
        flows.append(flow)
        weights = coefficients_of(flow, strip_sides(flow), *strip_scalars)
        start = walled(line[:3], [factor] * 3)
        one = rate(start, strip_sides(start), weights)
        one = walled([a + b for a, b in zip(start, one)], [factor] * 3)
        two = rate(one, strip_sides(one), weights)
        two = [0.75 * s + 0.25 * (a + b) for s, a, b in zip(start, one, two)]
        levels.append((start, one, two))

    inner_side = lane % 8 < 4

    def store_edges(target, low_values, high_values):
        for c in range(3):
            low = jnp.where(has_low, back(low_values[c], 1), 0.0)
            high = jnp.where(has_high, ahead(high_values[c], 1), 0.0)
            target[pl.ds(sub * c, sub), :] = jnp.where(inner_side, high, low)

    def axial(value, source, c, w, start, size):
        ghost = source[pl.ds(sub * c + start, size), :]
        ghost = pltpu.roll(ghost, 128 - (8 * (w - 1) + 4), 1)
        at = lane[:size]
        return (
            jnp.where(at == 0, ghost, back(value, 1)),
            jnp.where(at == 127, ghost, ahead(value, 1)),
        )

    def pick(low, high):
        return jnp.where(low_half, np.float32(low), np.float32(high))

    def scalars(w):
        options = []
        for half in range(2):
            r = half * 8 + (w - 3) + 0.5
            options.append(
                (
                    -1.0 if r < 0 else 1.0,
                    diffuse * (r - 0.5) / r,
                    diffuse * (r + 0.5) / r,
                    advect / r,
                    1.0 / (r * r),
                    diffuse / abs(r),
                )
            )
        return [pick(a, b) for a, b in zip(*options)]

    def read(source, c, w, start=0, size=sub):
        return source[pl.ds(row_of(c, w) + start, size), :]

    for c in range(6):
        last = read(cells, c, 10)
        factor = walls[...] if c < 3 else wall_signs[c - 3]
        cells[pl.ds(row_of(c, 11), sub), :] = jnp.where(low_half, read(cells, c, 11), factor * last)

    def surroundings(source, first_component, ends, w, start, size):
        center, sides = [], [[], [], [], [], [], []]
        for c in range(3):
            at = first_component + c
            whole = read(source, at, w)
            value = whole[:size]
            under, over = axial(value, ends, c, w, start, size)
            for side, part in zip(
                sides,
                (
                    read(source, at, w - 1, start, size),
                    read(source, at, w + 1, start, size),
                    back(whole, 0)[:size],
                    ahead(whole, 0)[:size],
                    under,
                    over,
                ),
            ):
                side.append(part)
            center.append(value)
        return center, sides

    def table_rows(kind, w, start, size):
        return pl.ds((kind * 12 + w - 1) * sub + start, size)

    def make_table(w):
        weights = coefficients_of(*surroundings(cells, 3, edge_flow, w, 0, sub), *scalars(w))
        flat = list(weights[:6]) + [value for row in weights[6] for value in row]
        if w not in (1, 12):
            for kind, value in enumerate(flat):
                table[table_rows(kind, w, 0, sub), :] = value
        return weights

    def stored_table(w, start, size):
        flat = [table[table_rows(kind, w, start, size), :] for kind in range(kinds_of_coefficient)]
        mix = [flat[6:9], flat[9:12], flat[12:15]]
        return tuple(flat[:6]) + (mix, scalars(w)[-1])

    def field_rate(source, w, start=0, size=sub, weights=None):
        center, sides = surroundings(source, 0, edge, w, start, size)
        return center, rate(center, sides, weights or stored_table(w, start, size))

    store_edges(edge_flow, flows[0], flows[-1])
    store_edges(edge, levels[0][0], levels[-1][0])
    for w in range(1, 13):
        center, change = field_rate(cells, w, weights=make_table(w))
        for c in range(3):
            first[pl.ds(row_of(c, w), sub), :] = center[c] + change[c]
    for c in range(3):
        low = pl.ds(row_of(c, 1), 8)
        first[low, :] = first[low, :] + ghosts[c]
        before = pl.ds(row_of(c, 3) + 14, 8, stride=sub)
        after = pl.ds(row_of(c, 3) + 9, 8, stride=sub)
        first[before, :] = first[before, :] + lows[c]
        first[after, :] = first[after, :] + highs[c]

    def close_wall(source):
        for c in range(3):
            source[pl.ds(row_of(c, 11), sub), :] = jnp.where(
                low_half, read(source, c, 11), walls[...] * read(source, c, 10)
            )

    close_wall(first)
    store_edges(edge, levels[0][1], levels[-1][1])
    for w in range(2, 12):
        center, change = field_rate(first, w)
        for c in range(3):
            second[pl.ds(row_of(c, w), sub), :] = 0.75 * read(cells, c, w) + 0.25 * (
                center[c] + change[c]
            )
    close_wall(second)
    store_edges(edge, levels[0][2], levels[-1][2])
    count = basis.shape[0] // 192
    sums = [jnp.zeros((8, 128), jnp.float32) for _ in range(count + 1)]
    for w in range(3, 11):
        center, change = field_rate(second, w, 0, 8)
        for c in range(3):
            rows = pl.ds(64 * c + 8 * (w - 3), 8)
            value = read(cells, c, w, 0, 8) / 3.0 + (2.0 / 3.0) * (center[c] + change[c])
            advanced[rows, :] = value
            for m in range(count):
                sums[m] += basis[pl.ds(192 * m + 64 * c + 8 * (w - 3), 8), :] * value
            sums[count] += value * value
    line = write_sums(jnp.broadcast_to(gram[...], (8, 128)), sums, range(count + 1))[:1]
    for device in range(message.shape[0]):
        message[device] = line


side_wall = 16 * tiles
side_strip = side_wall + 8
side_axis = side_strip + 16
side_length = side_axis + 24
diagonal_wall = 24
diagonal_length = 32
strip_length = 56
share_corner = 8 * tiles
share_rest = share_corner + 24
share_turn = share_rest + side_length - side_wall
share_strip = share_turn + 8 * tiles
share_diagonal = share_strip + strip_length
share_length = share_diagonal + diagonal_length


def faces_up():
    return (lax.axis_index("phi") + lax.axis_index("row")) % 2 == 0


def load_kernel(conductance, region, field, velocity, reflect, field_copy, flow_copy):
    kinds = region[...]
    value = jnp.zeros(kinds.shape, jnp.float32)
    for kind in range(conductance.shape[0]):
        value = jnp.where(kinds == kind, conductance[kind], value)
    reflect[...] = 1.0 - 2.0 * value / (1.0 + value)
    field_copy[...] = field[...]
    flow_copy[...] = velocity[...]


def send_kernel(field, velocity, far_field, far_flow, reflect, side, turn, diagonal, strip):
    top = lax.axis_index("row")
    upper = faces_up()
    slot = lanes(8) // 8

    def facing(load, depth):
        return jnp.where(upper, load(8 - depth), load(depth - 1))

    def column(source, c, depth):
        return facing(lambda q: source[pl.ds(c * 64 + q, 8, stride=8), :], depth)

    direction = jnp.where(upper, -1.0, 1.0)
    index = lax.broadcasted_iota(jnp.int32, (8, 128), 0).astype(jnp.float32)
    for source, flow, half in ((field, velocity, top), (far_field, far_flow, 1 - top)):
        base = half * (8 * tiles)

        def put(tile, value):
            side[pl.ds(pl.multiple_of(base + 8 * tile, 8), 8), :] = value

        bend = (diffuse * direction) / (index + (half.astype(jnp.float32) * 8.0 + 0.5))
        near_two = [column(source, c, 2) for c in range(3)]
        flow_two = [column(flow, c, 2) for c in range(3)]
        distant = [column(source, c, 3) for c in range(3)]
        carry = diffuse + advect * jnp.maximum(-direction * flow_two[1], 0.0)
        stretch = (0.5 * advect * direction) * near_two[1]
        term = [carry * distant[c] + stretch * column(flow, c, 3) for c in range(3)]
        term[0] = term[0] - bend * distant[1]
        term[1] = term[1] + bend * distant[0]
        for c in range(3):
            put(c, column(source, c, 1))
            put(3 + c, column(flow, c, 1))
            put(6 + c, near_two[c])
            put(9 + c, flow_two[c])
            put(12 + c, term[c])
    for depth in (1, 2):
        wall = facing(lambda q: reflect[pl.ds(q, 1), :], depth)
        side[pl.ds(side_wall + depth - 1, 1), :] = wall
        diagonal[pl.ds(diagonal_wall + depth - 1, 1), :] = wall

    for c in range(6):
        own, far = (field, far_field) if c < 3 else (velocity, far_flow)
        parts = []
        for source in (own, far):
            part = jnp.zeros((8, 128), jnp.float32)
            for r in range(8):
                part = jnp.where(
                    slot == r, pltpu.roll(layer(source, c % 3, r), (8 * r + 4) % 128, 1), part
                )
            parts.append(part)
        low = jnp.where(top == 0, parts[0], parts[1])
        high = jnp.where(top == 0, parts[1], parts[0])
        strip[pl.ds(8 * c, 8), :] = jnp.where(slot < 8, low, pltpu.roll(high, 64, 1))
    for depth in (1, 2):
        edge = facing(lambda q: strip[pl.ds(q, 6, stride=8), :], depth)
        side[pl.ds(side_strip + 8 * (depth - 1), 6), :] = edge
        diagonal[pl.ds(8 * (depth - 1), 6), :] = edge
    diagonal[pl.ds(16, 6), :] = jnp.where(
        upper, strip[pl.ds(0, 6, stride=8), :], strip[pl.ds(7, 6, stride=8), :]
    )

    def inner_cell(own, far, start, count, step):
        rows = pl.ds(start, count, stride=step)
        return jnp.where(top == 0, own[rows, :], far[rows, :])

    for place, (r, depth) in enumerate(((0, 1), (0, 2), (1, 1))):
        for part, (own, far) in enumerate(((field, far_field), (velocity, far_flow))):
            side[pl.ds(side_axis + 8 * place + 3 * part, 3), :] = jnp.where(
                upper,
                inner_cell(own, far, r * 8 + depth - 1, 3, 64),
                inner_cell(own, far, r * 8 + 8 - depth, 3, 64),
            )
    carry = (diffuse * 2.0 / 1.5) - advect * jnp.minimum(layer(velocity, 0, 1), 0.0)
    stretch = (0.5 * advect) * layer(field, 0, 1)
    for c in range(3):
        for r in range(2):
            turn[pl.ds(8 * (6 * r + c), 8), :] = layer(field, c, r)
            turn[pl.ds(8 * (6 * r + 3 + c), 8), :] = layer(velocity, c, r)
        turn[pl.ds(8 * (12 + c), 8), :] = carry * layer(field, c, 2) + stretch * layer(
            velocity, c, 2
        )
    strip[pl.ds(48, 8), :] = reflect[...]


def other_corner(side, first, step):
    top = lax.axis_index("row")
    low = side[pl.ds(8 * tiles + first + step, 6, stride=8), :]
    high = side[pl.ds(first + 7 - step, 6, stride=8), :]
    return jnp.where(top == 0, low, high)


def share_kernel(side, turn, opposite, diagonal, out):
    top = lax.axis_index("row")
    half = pl.multiple_of((1 - top) * (8 * tiles), 8)
    out[pl.ds(0, 8 * tiles), :] = side[pl.ds(half, 8 * tiles), :]
    for place, (first, step) in enumerate(((0, 0), (48, 0), (0, 1))):
        low = side[pl.ds(first + 7 - step, 6, stride=8), :]
        high = side[pl.ds(8 * tiles + first + step, 6, stride=8), :]
        out[pl.ds(share_corner + 8 * place, 6), :] = jnp.where(top == 0, low, high)
    out[pl.ds(share_rest, side_length - side_wall), :] = side[
        pl.ds(side_wall, side_length - side_wall), :
    ]
    out[pl.ds(share_turn, 8 * tiles), :] = turn[...]
    out[pl.ds(share_strip, strip_length), :] = opposite[...]
    out[pl.ds(share_diagonal, diagonal_length), :] = diagonal[...]


def compact_kernel(
    field, velocity, far_field, far_flow, reflect, strip, side, diagonal, opposite, shared,
    basis, gram, message, advanced, cells, walls, line, first, second, edge, edge_flow, table,
):
    top = lax.axis_index("row")
    low_half = top == 0
    upper = faces_up()
    mine_low = lax.axis_index("gz") == 0

    def both(own, other):
        return jnp.where(upper, other, own), jnp.where(upper, own, other)

    own_half = pl.multiple_of(top * (8 * tiles), 8)

    def tile_pair(tile):
        return both(
            side[pl.ds(pl.multiple_of(own_half + 8 * tile, 8), 8), :], shared[pl.ds(8 * tile, 8), :]
        )

    def rest_pair(start, count):
        return both(
            side[pl.ds(start, count), :], shared[pl.ds(share_rest + start - side_wall, count), :]
        )

    def diagonal_pair(start, count):
        return both(
            diagonal[pl.ds(start, count), :], shared[pl.ds(share_diagonal + start, count), :]
        )

    behind = [shared[pl.ds(share_turn + 8 * tile, 8), :] for tile in range(tiles)]
    nothing = jnp.zeros((8, 128), jnp.float32)
    for c in range(6):
        source, far = (field, far_field) if c < 3 else (velocity, far_flow)
        sign = signs[c % 3]
        for r in range(8):
            cells[pl.ds(row_of(c, r + 3), 8), :] = layer(source, c % 3, r)
        for w in range(window):
            cells[pl.ds(row_of(c, w) + 8, 8), :] = nothing
        for w in range(3):
            ghost = sign * behind[6 * (2 - w) + c] if w > 0 else 0.0
            cells[pl.ds(row_of(c, w), 8), :] = jnp.where(low_half, ghost, layer(far, c % 3, 5 + w))
            cells[pl.ds(row_of(c, 11 + w), 8), :] = jnp.where(low_half, layer(far, c % 3, w), 0.0)
        for depth in range(2):
            below, above = tile_pair(6 * depth + c)
            cells[pl.ds(row_of(c, 3) + 15 - depth, 8, stride=sub), :] = below
            cells[pl.ds(row_of(c, 3) + 8 + depth, 8, stride=sub), :] = above
    flip = lax.broadcasted_iota(jnp.int32, (6, 128), 0)
    flip = jnp.where((flip == 2) | (flip == 5), 1.0, -1.0)
    for place, (w, first_row, step, depth) in enumerate(((2, 0, 0, 0), (2, 48, 0, 1), (1, 0, 1, 0))):
        axis_high, axis_low = rest_pair(side_axis + 8 * place, 6)
        below, above = both(
            other_corner(side, first_row, step), shared[pl.ds(share_corner + 8 * place, 6), :]
        )
        for axis_part, other, q in ((axis_low, below, 15 - depth), (axis_high, above, 8 + depth)):
            low = pl.ds(row_of(0, w) + q, 6, stride=window * sub)
            high = pl.ds(row_of(0, 13 - w) + q, 6, stride=window * sub)
            cells[low, :] = jnp.where(low_half, flip * axis_part, other)
            cells[high, :] = jnp.where(low_half, other, 0.0)

    slot, inside = lanes(sub) // 8, lanes(sub) % 8
    axial_strip = [
        jnp.where(
            low_half, opposite[pl.ds(8 * tile, 8), :], shared[pl.ds(share_strip + 8 * tile, 8), :]
        )
        for tile in range(7)
    ]
    own_side = (inside < 4) == mine_low

    def merge(own, other):
        return jnp.where(own_side[: own.shape[0]], own, other)

    for part, (tile, pair) in enumerate(
        ((reflect[...], rest_pair(side_wall, 2)), (axial_strip[6], diagonal_pair(diagonal_wall, 2)))
    ):
        below, above = pair
        base = sub * part
        walls[pl.ds(base, 8), :] = tile
        walls[pl.ds(base + 8, 8), :] = nothing
        walls[pl.ds(base + 8, 2), :] = above
        walls[pl.ds(base + 15, 1), :] = below[0:1]
        walls[pl.ds(base + 14, 1), :] = below[1:2]
    factor = merge(
        pltpu.roll(walls[pl.ds(0, sub), :], 84, 1), pltpu.roll(walls[pl.ds(sub, sub), :], 84, 1)
    )

    for c in range(6):
        own = strip[pl.ds(8 * c, 8), :]
        line[pl.ds(sub * c, 8), :] = merge(own, axial_strip[c])
        line[pl.ds(sub * c + 8, 8), :] = nothing
    for depth in (1, 2):
        below, above = rest_pair(side_strip + 8 * (depth - 1), 6)
        beyond_below, beyond_above = diagonal_pair(8 * (depth - 1), 6)
        line[pl.ds(16 - depth, 6, stride=sub), :] = merge(below, beyond_below)
        line[pl.ds(7 + depth, 6, stride=sub), :] = merge(above, beyond_above)
    axis_high, axis_low = diagonal_pair(16, 6)
    combined = []
    for c in range(6):
        value = line[pl.ds(sub * c, sub), :]
        combined.append(jnp.where(low_half, pltpu.roll(value, 16, 1), pltpu.roll(value, 80, 1)))
    for c in range(6):
        sign = signs[c % 3]
        across = shared[pl.ds(share_strip + 8 * c, 8), :]
        own = jnp.where(
            slot[:8] == 1,
            pltpu.roll(behind[c], 12, 1),
            pltpu.roll(behind[6 + c], 4, 1),
        )
        other = jnp.where(slot[:8] == 1, pltpu.roll(across, 8, 1), pltpu.roll(across, 120, 1))
        line[pl.ds(sub * c, 8), :] = sign * merge(own, other)
        line[pl.ds(sub * c + 8, 8), :] = nothing
        line[pl.ds(sub * c + 8, 1), :] = sign * pltpu.roll(axis_high, 8, 1)[c : c + 1]
        line[pl.ds(sub * c + 15, 1), :] = sign * pltpu.roll(axis_low, 8, 1)[c : c + 1]
        ghost = line[pl.ds(sub * c, sub), :]
        combined[c] = jnp.where(jnp.logical_and(slot < 2, low_half), ghost, combined[c])
    combined.append(factor)
    ghosts = [jnp.where(low_half, signs[c] * behind[12 + c], 0.0) for c in range(3)]
    lows, highs = zip(*[tile_pair(12 + c) for c in range(3)])
    march(
        [combined], ghosts, lows, highs, walls.at[pl.ds(0, sub), :], cells, basis, gram, message,
        advanced, first, second, edge, edge_flow, table,
    )


def two_sum(a, b):
    total = a + b
    part = total - a
    return total, (a - (total - part)) + (b - part)


def split(a):
    scaled = 4097.0 * a
    high = scaled - (scaled - a)
    return high, a - high


def two_product(a, b, a_parts, b_parts):
    product = a * b
    (a_high, a_low), (b_high, b_low) = a_parts, b_parts
    rest = ((a_high * b_high - product) + a_high * b_low + a_low * b_high) + a_low * b_low
    return product, rest


def write_sums(line, sums, places):
    spot = lanes(8)
    ones = jnp.ones((128, 128), jnp.bfloat16)
    stacked = jnp.concatenate(sums, axis=0)
    parts = []
    for _ in range(3):
        part = stacked.astype(jnp.bfloat16)
        stacked = stacked - part.astype(jnp.float32)
        parts.append(jnp.dot(part, ones, preferred_element_type=jnp.float32))
    large, small = parts[0], parts[1] + parts[2]
    for index, place in enumerate(places):
        rows = slice(8 * index, 8 * index + 8)
        total, rest = two_sum(large[rows], small[rows])
        for step in (4, 2, 1):
            total, error = two_sum(total, pltpu.roll(total, step, 0))
            rest = rest + pltpu.roll(rest, step, 0) + error
        line = jnp.where(spot == place, total, jnp.where(spot == place + 64, rest, line))
    return line


def gram_place(m, n):
    return 16 + m * (m + 1) // 2 + n


def gram_kernel(basis, out):
    count = basis.shape[0] // 192
    line = jnp.zeros((8, 128), jnp.float32)
    for m in range(count):
        sums = [jnp.zeros((8, 128), jnp.float32) for _ in range(m + 1)]
        for tile in range(24):
            value = basis[pl.ds(192 * m + 8 * tile, 8), :]
            for n in range(m + 1):
                sums[n] += value * basis[pl.ds(192 * n + 8 * tile, 8), :]
        line = write_sums(line, sums, [gram_place(m, n) for n in range(m + 1)])
    out[...] = line[:1]


def finish_kernel(cell_count, messages, advanced, basis, out, hessenberg):
    count = basis.shape[0] // 192
    terms = [
        jnp.broadcast_to(messages[device], (8, 128)) for device in range(messages.shape[0])
    ]
    errors = []
    while len(terms) > 1:
        pairs = [two_sum(a, b) for a, b in zip(terms[::2], terms[1::2])]
        errors += [error for _, error in pairs]
        terms = [total for total, _ in pairs] + terms[len(terms) // 2 * 2 :]
    while len(errors) > 1:
        errors = [a + b for a, b in zip(errors[::2], errors[1::2])] + errors[len(errors) // 2 * 2 :]
    total = terms[0]
    rest = pltpu.roll(total, 64, 1)
    rest = rest + errors[0] if errors else rest

    def entry(index):
        high = jnp.broadcast_to(total[:, index : index + 1], (8, 128))
        return high, jnp.broadcast_to(rest[:, index : index + 1], (8, 128))

    pending, pending_rest = [list(part) for part in zip(*[entry(m) for m in range(count)])]
    energy, energy_rest = entry(count)
    weights = []
    diagonals = [entry(gram_place(m, m)) for m in range(count)]
    inverses = [1.0 / diagonal for diagonal, _ in diagonals]
    for m in range(count):
        weight = pending[m] * inverses[m]
        weights.append(weight)
        parts = split(weight)
        diagonal, diagonal_rest = diagonals[m]
        product, error = two_product(weight, diagonal, parts, split(diagonal))
        left = (pending[m] - product) + (pending_rest[m] - error - weight * diagonal_rest)
        product, error = two_product(weight, pending[m], parts, split(pending[m]))
        energy, lost = two_sum(energy, -product)
        energy_rest = energy_rest + (lost - error - weight * (pending_rest[m] + left))
        for n in range(m + 1, count):
            factor, factor_rest = entry(gram_place(n, m))
            product, error = two_product(weight, factor, parts, split(factor))
            pending[n], lost = two_sum(pending[n], -product)
            pending_rest[n] = pending_rest[n] + (lost - error - weight * factor_rest)
    energy = energy + energy_rest
    spread = jnp.sqrt(jnp.maximum(energy, 0.0) / cell_count + epsilon)
    scale = 1.0 / spread
    for tile in range(24):
        rows = pl.ds(8 * tile, 8)
        value = advanced[rows, :]
        for m in range(count):
            value = value - weights[m] * basis[pl.ds(192 * m + 8 * tile, 8), :]
        out[rows, :] = value * scale
    for m in range(count):
        hessenberg[m] = weights[m][0, 0]
    hessenberg[count] = spread[0, 0]


def shift(value, axis, step):
    count = lax.axis_size(axis)
    return lax.ppermute(value, axis, [(i, (i + step) % count) for i in range(count)])


def march_scratch():
    return [
        shape(3 * window * sub, 128),
        shape(3 * window * sub, 128),
        shape(3 * sub, 128),
        shape(3 * sub, 128),
        shape(kinds_of_coefficient * 12 * sub, 128),
    ]


def general_plan(field, velocity, basis, wall_region, wall_conductance):
    loop = lax.axis_size("phi")
    ends = lax.axis_size("gz")
    halves = lax.axis_size("row")
    fold = loop == 4
    many = ends > 2
    vectors = basis.shape[0]
    field_rows = field.reshape(192, 128)
    flow_rows = velocity.reshape(192, 128)
    swap = [(0, 1), (1, 0)]
    far_field = lax.ppermute(field_rows, "row", swap)
    far_flow = lax.ppermute(flow_rows, "row", swap)
    field_rows, flow_rows, basis_rows = near(
        field_rows, flow_rows, basis.reshape(vectors * 192, 128)
    )
    inner = pl.pallas_call(
        inner_kernel, in_specs=vmem(2), out_specs=vmem(1)[0], out_shape=shape(8 * tiles, 128)
    )(field_rows, flow_rows)
    half = loop // 2
    turned = []
    for p in range(loop):
        for r in range(halves):
            turned.append((p * halves + r, ((p + half) % loop if r == 0 else p) * halves + r))
    behind = lax.ppermute(inner, ("phi", "row"), turned)
    far_field, far_flow = near(far_field, far_flow)
    side = side_rows if fold else axis_row
    packed = pl.pallas_call(
        functools.partial(sides_kernel, fold),
        in_specs=[pl.BlockSpec(memory_space=pltpu.SMEM)] + vmem(5),
        out_specs=vmem(3 if fold else 5),
        out_shape=[shape(side, 128), shape(side, 128), shape(8, 128)]
        + ([] if fold else [shape(24, 128)] * 2),
    )(wall_conductance, wall_region, field_rows, flow_rows, far_field, far_flow)
    up, down, reflect = packed[:3]
    below = shift(up, "phi", 1)
    above = shift(down, "phi", -1)
    corners = []
    if not fold:
        corners = [shift(packed[3], "phi", half + 1), shift(packed[4], "phi", half - 1)]
    gram = pl.pallas_call(
        gram_kernel, in_specs=vmem(1), out_specs=vmem(1)[0], out_shape=shape(1, 128)
    )(basis_rows)
    below, above, behind, gram, *corners = lax.optimization_barrier(
        (below, above, behind, gram, *corners)
    )
    below, above, behind, gram, *corners = near(below, above, behind, gram, *corners)
    walls, strip, cells = pl.pallas_call(
        functools.partial(window_kernel, fold),
        in_specs=vmem(8 + len(corners)),
        out_specs=vmem(3),
        out_shape=[shape(sub, 128), shape(6 * sub, 128), shape(6 * window * sub, 128)],
    )(field_rows, flow_rows, far_field, far_flow, below, above, behind, reflect, *corners)
    if many:
        up_pairs = [(i, i + 1) for i in range(ends - 1)]
        others = [
            lax.ppermute(strip, "gz", up_pairs),
            lax.ppermute(strip, "gz", [(b, a) for a, b in up_pairs]),
        ]
    else:
        others = [lax.ppermute(strip, "gz", swap)]
    walls, strip, cells, *others = near(walls, strip, cells, *others)
    devices = lax.axis_size(("phi", "gz", "row"))
    return pl.pallas_call(
        functools.partial(stage_kernel, many),
        in_specs=vmem(8 + len(others)),
        out_specs=vmem(2),
        out_shape=[shape(devices, 1, 128), shape(192, 128)],
        scratch_shapes=march_scratch(),
    )(below, above, behind, walls, strip, *others, cells, basis_rows, gram)


def compact_plan(field, velocity, basis, wall_region, wall_conductance):
    vectors = basis.shape[0]
    field_rows = field.reshape(192, 128)
    flow_rows = velocity.reshape(192, 128)
    axes = ("phi", "gz", "row")
    devices = lax.axis_size(axes)

    def exchange(value, partner):
        pairs = []
        for p in range(4):
            for g in range(2):
                for r in range(2):
                    q, h, t = partner(p, g, r)
                    pairs.append(((p * 2 + g) * 2 + r, (q % 4 * 2 + h) * 2 + t))
        return lax.ppermute(value, axes, pairs)

    def beside(p, r):
        return p + 1 if (p + r) % 2 == 0 else p - 1

    swap = [(0, 1), (1, 0)]
    far_field = lax.ppermute(field_rows, "row", swap)
    far_flow = lax.ppermute(flow_rows, "row", swap)
    reflect, field_rows, flow_rows = pl.pallas_call(
        load_kernel,
        in_specs=[pl.BlockSpec(memory_space=pltpu.SMEM)] + vmem(3),
        out_specs=vmem(3),
        out_shape=[shape(8, 128), shape(192, 128), shape(192, 128)],
    )(wall_conductance, wall_region, field_rows, flow_rows)
    blocks = near(field_rows, flow_rows, far_field, far_flow, reflect)
    side, turn, diagonal, strip = pl.pallas_call(
        send_kernel,
        in_specs=vmem(5),
        out_specs=vmem(4),
        out_shape=[
            shape(side_length, 128),
            shape(8 * tiles, 128),
            shape(diagonal_length, 128),
            shape(strip_length, 128),
        ],
    )(*blocks)
    opposite = exchange(strip, lambda p, g, r: (p + 2, 1 - g, 1) if r == 0 else (p, 1 - g, 0))
    turn = exchange(turn, lambda p, g, r: (p + 2, g, 1) if r == 0 else (p, g, 0))
    diagonal = exchange(diagonal, lambda p, g, r: (beside(p, r), 1 - g, r))
    side = exchange(side, lambda p, g, r: (beside(p, r), g, r))
    (basis_rows,) = near(basis.reshape(vectors * 192, 128))
    gram = pl.pallas_call(
        gram_kernel, in_specs=vmem(1), out_specs=vmem(1)[0], out_shape=shape(1, 128)
    )(basis_rows)
    side, turn, diagonal, opposite, gram = near(
        *lax.optimization_barrier((side, turn, diagonal, opposite, gram))
    )
    share = pl.pallas_call(
        share_kernel, in_specs=vmem(4), out_specs=vmem(1)[0], out_shape=shape(share_length, 128)
    )(side, turn, opposite, diagonal)
    shared = lax.ppermute(share, "row", swap)
    strip, shared = near(strip, shared)
    return pl.pallas_call(
        compact_kernel,
        in_specs=vmem(12),
        out_specs=vmem(2),
        out_shape=[shape(devices, 1, 128), shape(192, 128)],
        scratch_shapes=[
            shape(6 * window * sub, 128),
            shape(2 * sub, 128),
            shape(6 * sub, 128),
        ]
        + march_scratch(),
    )(*blocks, strip, side, diagonal, opposite, shared, basis_rows, gram)


def local(field, velocity, basis, wall_region, wall_conductance):
    axes = ("phi", "gz", "row")
    vectors = basis.shape[0]
    devices = lax.axis_size(axes)
    compact = tuple(lax.axis_size(axis) for axis in axes) == (4, 2, 2)
    plan = compact_plan if compact else general_plan
    message, advanced = plan(field, velocity, basis, wall_region, wall_conductance)
    (basis_rows,) = near(basis.reshape(vectors * 192, 128))
    messages = lax.all_to_all(message, axes, 0, 0, tiled=True)
    messages, advanced = near(messages, advanced)
    out, hessenberg = pl.pallas_call(
        functools.partial(finish_kernel, float(field.size * devices)),
        in_specs=vmem(3),
        out_specs=vmem(1) + [pl.BlockSpec(memory_space=pltpu.SMEM)],
        out_shape=[
            jax.ShapeDtypeStruct((192, 128), jnp.float32),
            jax.ShapeDtypeStruct((vectors + 1,), jnp.float32),
        ],
    )(messages, advanced, basis_rows)
    return out.reshape(field.shape), hessenberg


def solution(mesh):
    return jax.shard_map(
        local,
        mesh=mesh,
        in_specs=(
            P("groups", "row", "phi", "gz"),
            P("groups", "row", "phi", "gz"),
            P("groups", None, "row", "phi", "gz"),
            P(("groups", "phi"), "gz"),
            P("groups"),
        ),
        out_specs=(P("groups", "row", "phi", "gz"), P("groups")),
        check_vma=False,
    )
```
